32 devices in a mesh: seq: 4 (over y, x), fsdp: 8 (over z, core).
Axes of the slice: x: 2, y: 2, z: 4, core: 2. Of those that a mesh axis runs over, the one named last changes fastest.
Arguments:
- hidden_in: bfloat16 [8, 512, 2048], P('fsdp', 'seq'), may hold values from -6 to 6
- gain_attn: bfloat16 [2048], P('fsdp'), may hold values from 0.5 to 1.5
- attn_weights: bfloat16 [2048, 4, 2048], P('fsdp'), may hold values from -0.375 to 0.375
- gain_mlp: bfloat16 [2048], P('fsdp'), may hold values from 0.5 to 1.5
- mlp_weights: bfloat16 [8192, 3, 2048], P('fsdp'), may hold values from -0.13258252 to 0.13258252
- out_grad: bfloat16 [8, 512, 2048], P('fsdp', 'seq'), may hold values from -6 to 6
- block_slots: int32 [4, 2], replicated, may hold values from 0 to 7, as said below
- doc_ids: int32 [8, 512], P('fsdp'), may hold values from 0 to 2, as said below
Outputs:
- block_out: bfloat16 [8, 512, 2048], P('fsdp', 'seq')
- grad_in: bfloat16 [8, 512, 2048], P('fsdp', 'seq')
- grad_gain_attn: float32 [2048], P('fsdp')
- grad_attn_weights: float32 [2048, 4, 2048], P('fsdp')
- grad_gain_mlp: float32 [2048], P('fsdp')
- grad_mlp_weights: float32 [8192, 3, 2048], P('fsdp')
The draws below stay inside these ranges and needn't reach their ends.
Inputs may be any that keep to these rules, and one draw needn't show every extreme that they name: `block_slots`: row i holds the two query blocks given to index i of seq; one of them is p and the other 7 - p, and each of the 8 blocks stands in one row. `doc_ids`: along each sequence the document numbers never fall, and all three occur.
All inputs are finite; a program needn't handle non-finite values.
Results may differ from the reference program's by a relative error of at most 0.023.
Values may be sent and summed in bfloat16 or wider, within the bound.
A program may use at most 384 MiB of HBM per device.

```python
import math
import jax
import jax.numpy as jnp
from jax import lax

D = 2048
HEAD = 64
FF = 8192
BLK = 64
LENGTH = 512
SEQS = 8
N_SEQ = 4


def draw_attn_weights(key, part):
    key = jax.random.fold_in(key, 3)
    base = jnp.clip(jax.random.normal(key, (D, 4, D), jnp.float32), -6.0, 6.0)
    boost = max(1.0, math.sqrt(LENGTH) / 8.0)
    factors = jnp.array([1.0, 1.0, 1.0, boost], jnp.float32) / math.sqrt(D)
    return (base * factors[None, :, None]).astype(jnp.bfloat16)


def draw_mlp_weights(key, part):
    key = jax.random.fold_in(key, 4)
    base = jnp.clip(jax.random.normal(key, (FF, 3, D), jnp.float32), -6.0, 6.0)
    factors = jnp.array([1.0 / math.sqrt(D), 1.0 / math.sqrt(D), 1.0 / math.sqrt(FF)], jnp.float32)
    return (base * factors[None, :, None]).astype(jnp.bfloat16)


def draw_block_slots(key, part):
    key = jax.random.fold_in(key, 5)
    perm_key, flip_key = jax.random.split(key)
    ranking = jax.random.permutation(perm_key, N_SEQ).astype(jnp.int32)
    flipped = jax.random.randint(flip_key, (N_SEQ,), 0, 2).astype(jnp.int32)
    early_block = jnp.where(flipped == 1, 2 * N_SEQ - 1 - ranking, ranking)
    return jnp.stack([early_block, 2 * N_SEQ - 1 - early_block], 1).astype(jnp.int32)


def draw_doc_ids(key, part):
    key = jax.random.fold_in(key, 9)
    positions = jnp.arange(LENGTH, dtype=jnp.int32)

    def one_row(row_key):
        parts_keys = jax.random.split(row_key, 3)
        flipped = jax.random.randint(parts_keys[0], (), 0, 2)
        long_end = jax.random.randint(parts_keys[1], (), LENGTH // 2, LENGTH - LENGTH // 8 + 1)
        middle_len = jax.random.randint(parts_keys[2], (), 1, LENGTH - long_end)
        forward_ids = (positions >= long_end).astype(jnp.int32) + (positions >= long_end + middle_len).astype(jnp.int32)
        mirrored = 2 - forward_ids[::-1]
        return jnp.where(flipped == 1, mirrored, forward_ids).astype(jnp.int32)
    return jax.vmap(one_row)(jax.random.split(key, SEQS))


def shard_levels(own_key, shape, shards, low, high):
    def one(axis_at, blocks):
        draws = jax.random.uniform(jax.random.fold_in(jax.random.fold_in(own_key, 6), axis_at), (blocks,), jnp.float32, low / len(shards), high / len(shards))
        return jnp.repeat(jnp.exp(draws), shape[axis_at] // blocks).reshape((-1,) + (1,) * (len(shape) - axis_at - 1))

    loudness = one(*shards[0])
    for cut in shards[1:]:
        loudness = loudness * one(*cut)
    return loudness


def gaussian(rng, extent, width, bound, shards=(), kind=jnp.bfloat16):
    level = shard_levels(rng, extent, shards, -0.22, 0.18) if shards else 1.0
    drawn = jax.random.normal(rng, extent, jnp.float32) * width * level
    return jnp.minimum(jnp.maximum(drawn, -bound), bound).astype(kind)


def setup_inputs(seed: int = 0) -> dict:
    arg_keys = jax.random.split(jax.random.key(seed), 9)
    hidden_in = gaussian(arg_keys[0], (SEQS, LENGTH, D), 1.0, 6.0, ((0, 8), (1, 4)))
    gain_attn = jnp.clip(1.0 + 0.1 * jax.random.normal(arg_keys[1], (D,), jnp.float32), 0.5, 1.5).astype(jnp.bfloat16)
    attn_weights = draw_attn_weights(jax.random.fold_in(arg_keys[8], 71), 0)
    gain_mlp = jnp.clip(1.0 + 0.1 * jax.random.normal(arg_keys[3], (D,), jnp.float32), 0.5, 1.5).astype(jnp.bfloat16)
    mlp_weights = draw_mlp_weights(jax.random.fold_in(arg_keys[8], 71), 0)
    out_grad = gaussian(arg_keys[5], (SEQS, LENGTH, D), 1.0, 6.0, ((0, 8), (1, 4)))
    block_slots = draw_block_slots(jax.random.fold_in(arg_keys[8], 71), 0)
    doc_ids = draw_doc_ids(jax.random.fold_in(arg_keys[8], 71), 0)
    return {"hidden_in": hidden_in, "gain_attn": gain_attn, "attn_weights": attn_weights, "gain_mlp": gain_mlp, "mlp_weights": mlp_weights, "out_grad": out_grad, "block_slots": block_slots, "doc_ids": doc_ids}


@jax.custom_vjp
def low(v):
    return lax.optimization_barrier(v.astype(jnp.bfloat16)).astype(jnp.float32)

@jax.custom_vjp
def low_back(v):
    return v

def low_keep(v):
    return (low(v), None)

def low_pass(kept, grad):
    return (grad,)

def back_keep(v):
    return (v, None)

def back_low(kept, grad):
    return (low(grad),)
low.defvjp(low_keep, low_pass)
low_back.defvjp(back_keep, back_low)
NORM_EPS = 1e-05
ROPE_BASE = 130000.0
MASKED_OUT = -1e+30
EXACT = lax.Precision.HIGHEST

def angles(positions):
    freqs = ROPE_BASE ** (-jnp.arange(0, HEAD, 2).astype(jnp.float32) / HEAD)
    turn = positions.astype(jnp.float32)[:, None] * freqs[None, :]
    return (jnp.cos(turn)[:, None, :], jnp.sin(turn)[:, None, :])

def rotate(field, cosine, sine):
    half = field.shape[-1] // 2
    front = field[..., :half]
    back_half = field[..., half:]
    return jnp.concatenate([front * cosine - back_half * sine, back_half * cosine + front * sine], -1)

def rms_norm(value, gain):
    scale = lax.rsqrt(lax.optimization_barrier(jnp.mean(value * value, axis=-1, keepdims=True)) + NORM_EPS)
    return value * scale * gain

def sequence_block(seq_rows, attn_w, mlp_w, gain_a, gain_m, positions, doc_rows):
    seq_len, model_width = seq_rows.shape
    head_count = model_width // HEAD
    normed = low(rms_norm(seq_rows, gain_a))
    qkv = jnp.dot(normed, attn_w[:, :3, :].reshape(model_width, 3 * model_width), precision=EXACT)
    q_pre = low_back(qkv[:, :model_width])
    k_pre = low_back(qkv[:, model_width:2 * model_width])
    v_val = low(low_back(qkv[:, 2 * model_width:]))
    cosine, sine = angles(positions)
    queries = low(rotate(q_pre.reshape(seq_len, head_count, HEAD), cosine, sine))
    keys = low(rotate(k_pre.reshape(seq_len, head_count, HEAD), cosine, sine))
    values = v_val.reshape(seq_len, head_count, HEAD)
    query_span = min(seq_len, 512)
    starts = (jnp.arange(seq_len // query_span) * query_span).astype(jnp.int32)

    def attend(first_row):
        query_block = lax.dynamic_slice_in_dim(queries, first_row, query_span, 0)
        query_pos = lax.dynamic_slice_in_dim(positions, first_row, query_span, 0)
        query_doc = lax.dynamic_slice_in_dim(doc_rows, first_row, query_span, 0)
        scores = low_back(jnp.einsum('qhd,khd->hqk', query_block, keys, precision=EXACT) * 0.125)
        allowed = ((positions[None, :] <= query_pos[:, None]) & (doc_rows[None, :] == query_doc[:, None]))[None]
        masked = jnp.where(allowed, scores, MASKED_OUT)
        row_top = lax.optimization_barrier(jnp.max(masked, axis=-1, keepdims=True))
        row_total = lax.optimization_barrier(jnp.sum(jnp.where(allowed, jnp.exp(masked - row_top), 0.0), axis=-1, keepdims=True))
        log_total = row_top + jnp.log(row_total)
        attn_prob = low(jnp.where(allowed, jnp.exp(masked - log_total), 0.0))
        attn_out = jnp.einsum('hqk,khd->qhd', attn_prob, values, precision=EXACT)
        return attn_out.reshape(query_span, model_width)
    attn_mix = lax.map(jax.checkpoint(attend), starts).reshape(seq_len, model_width)
    mixed_low = low(low_back(attn_mix))
    branch = low_back(jnp.dot(mixed_low, attn_w[:, 3, :], precision=EXACT))
    middle = seq_rows + branch
    normed_two = low(rms_norm(middle, gain_m))
    gate_val = low_back(jnp.dot(normed_two, mlp_w[:, 0, :].T, precision=EXACT))
    up_val = low_back(jnp.dot(normed_two, mlp_w[:, 1, :].T, precision=EXACT))
    hidden = low(jax.nn.silu(gate_val) * up_val)
    return middle + low_back(jnp.dot(hidden, mlp_w[:, 2, :], precision=EXACT))

def reference(hidden_in, gain_attn, attn_weights, gain_mlp, mlp_weights, out_grad, block_slots, doc_ids):
    slot_table = block_slots.reshape(-1).astype(jnp.int32)
    positions = (slot_table[:, None] * BLK + jnp.arange(BLK, dtype=jnp.int32)[None, :]).reshape(-1).astype(jnp.int32)

    def forward(source, gain_a, attn_w, gain_m, mlp_w):

        def one_seq(seq_pair):
            seq_rows, doc_line = seq_pair
            doc_rows = doc_line[positions]
            return sequence_block(seq_rows, attn_w, mlp_w, gain_a, gain_m, positions, doc_rows)
        return lax.map(one_seq, (source, doc_ids))
    primals = (hidden_in.astype(jnp.float32), gain_attn.astype(jnp.float32), attn_weights.astype(jnp.float32), gain_mlp.astype(jnp.float32), mlp_weights.astype(jnp.float32))
    result, pullback = jax.vjp(forward, *primals)
    gradients = pullback(out_grad.astype(jnp.float32))
    return (result.astype(jnp.bfloat16), gradients[0].astype(jnp.bfloat16), gradients[1], gradients[2], gradients[3], gradients[4])
```

```python
import functools

import jax
import jax.numpy as jnp
from jax import lax
from jax.experimental import pallas as pl
from jax.experimental.pallas import tpu as pltpu
from jax.sharding import PartitionSpec as P

HEAD = 64


NORM_EPS = 1e-05
ROPE_BASE = 130000.0
MASKED_OUT = -1e30
F32 = jnp.float32
BF16 = jnp.bfloat16
MESH = pl.DeviceIdType.MESH
DMA = pltpu.SemaphoreType.DMA
ANY = pl.BlockSpec(memory_space=pl.ANY)
VMEM = pl.BlockSpec(memory_space=pltpu.VMEM)


def send(src, dst, send_sem, recv_sem, device):
    return pltpu.make_async_remote_copy(
        src_ref=src,
        dst_ref=dst,
        send_sem=send_sem,
        recv_sem=recv_sem,
        device_id=device,
        device_id_type=MESH,
    )


class Place:
    def __init__(self, n_seq, n_fsdp):
        self.n_seq, self.line = n_seq, n_fsdp // 2
        self.s = lax.axis_index("seq")
        self.f = lax.axis_index("fsdp")
        self.r = lax.div(self.f, 2)
        self.c = lax.rem(self.f, 2)
        self.up = (self.s, self.f + 2)
        self.down = (self.s, self.f - 2)
        self.sister = (self.s, 2 * self.r + 1 - self.c)

    def peer(self, d):
        return (jnp.bitwise_xor(self.s, d), self.f)

    def greet(self):
        barrier = pltpu.get_barrier_semaphore()
        wrap = 2 * self.line
        partners = [
            (self.s, lax.rem(self.f + 2, wrap)),
            (self.s, lax.rem(self.f + wrap - 2, wrap)),
            self.sister,
        ]
        partners += [self.peer(d) for d in range(1, self.n_seq)]
        for partner in partners:
            pl.semaphore_signal(barrier, inc=1, device_id=partner, device_id_type=MESH)
        pl.semaphore_wait(barrier, len(partners))


class GatherLine:
    def __init__(self, x, n_seq, n_fsdp, parts=1):
        line = n_fsdp // 2
        self.args, self.in_specs = [x], [ANY]
        self.outs = [jax.ShapeDtypeStruct((n_fsdp,) + x.shape, x.dtype)]
        self.out_specs = [ANY]
        self.scratch = [DMA((line, parts)) for _ in range(5)] + [DMA((1,))]
        self.parts = parts

    def steps(self, at, refs):
        x, o, line_r, sis_r, up_s, down_s, sis_s, own_s = refs
        parts, line, r, c = self.parts, at.line, at.r, at.c
        rows = x.shape[0] // parts

        def cut(ref, k):
            return ref.at[pl.ds(k * rows, rows)]

        def go_up(src, b, k):
            return send(src, cut(o.at[2 * b + c], k), up_s.at[b, k], line_r.at[b, k], at.up)

        def go_down(src, b, k):
            return send(src, cut(o.at[2 * b + c], k), down_s.at[b, k], line_r.at[b, k], at.down)

        def go_sister(src, b, k):
            return send(src, cut(o.at[2 * b + c], k), sis_s.at[b, k], sis_r.at[b, k], at.sister)

        own = pltpu.make_async_copy(x, o.at[at.f], own_s.at[0])
        own.start()
        for k in range(parts):
            src = cut(x, k)
            pl.when(r < line - 1)(lambda: go_up(src, r, k).start())
            pl.when(r > 0)(lambda: go_down(src, r, k).start())
            go_sister(src, r, k).start()
        yield
        for t in range(1, line):
            for k in range(parts):
                low, high = r - t, r + t

                @pl.when(low >= 0)
                def _():
                    src = cut(o.at[2 * low + c], k)
                    go_up(src, low, k).wait_recv()
                    pl.when(r < line - 1)(lambda: go_up(src, low, k).start())
                    go_sister(src, low, k).start()

                @pl.when(high < line)
                def _():
                    src = cut(o.at[2 * high + c], k)
                    go_down(src, high, k).wait_recv()
                    pl.when(r > 0)(lambda: go_down(src, high, k).start())
                    go_sister(src, high, k).start()

            yield
        for b in range(line):
            for k in range(parts):
                src = cut(o.at[2 * b + 1 - c], k)
                send(src, src, sis_s.at[b, k], sis_r.at[b, k], at.sister).wait_recv()
                src = cut(x, k)
                go_sister(src, b, k).wait_send()
                pl.when((b <= r) & (r < line - 1))(lambda: go_up(src, b, k).wait_send())
                pl.when((b >= r) & (r > 0))(lambda: go_down(src, b, k).wait_send())
        own.wait()


class ScatterLine:
    def __init__(self, part, n_seq, n_fsdp, parts=1, out_dtype=F32):
        line = n_fsdp // 2
        block = part.shape[1:]
        self.args, self.in_specs = [part], [VMEM]
        self.outs = [jax.ShapeDtypeStruct(block, out_dtype)]
        self.out_specs = [VMEM]
        self.scratch = [
            pltpu.VMEM((line,) + block, part.dtype),
            pltpu.VMEM((line + 1,) + block, part.dtype),
        ]
        self.scratch += [DMA((line, parts)), DMA((line, parts)), DMA((line, parts))]
        self.scratch += [DMA((line + 1, parts))]
        self.parts = parts

    def steps(self, at, refs):
        part, o, sis, come, sis_s, sis_r, line_s, line_r = refs
        parts, line, r, c = self.parts, at.line, at.r, at.c
        rows = part.shape[1] // parts
        tile = 16 if rows % 16 == 0 else rows

        def cut(ref, k):
            return ref.at[pl.ds(k * rows, rows)]

        def to_sister(b, k):
            return send(
                cut(part.at[2 * b + 1 - c], k),
                cut(sis.at[b], k),
                sis_s.at[b, k],
                sis_r.at[b, k],
                at.sister,
            )

        def slot(b, own):
            return jnp.where(b == own, line, b)

        def go_up(b, k):
            return send(cut(sis.at[b], k), cut(come.at[b], k), line_s.at[b, k], line_r.at[b, k], at.up)

        def go_down(b, k, own):
            i = slot(b, own)
            return send(
                cut(sis.at[b], k), cut(come.at[i], k), line_s.at[b, k], line_r.at[i, k], at.down
            )

        def add(b, k, came, out=None):
            def body(i, carry):
                at_rows = pl.ds(k * rows + i * tile, tile)
                total = part[2 * b + c, at_rows].astype(F32) + sis[b, at_rows].astype(F32)
                for j in came:
                    total = total + come[j, at_rows].astype(F32)
                if out is None:
                    sis[b, at_rows] = total.astype(sis.dtype)
                else:
                    out[at_rows] = total.astype(out.dtype)
                return carry

            lax.fori_loop(0, rows // tile, body, 0)

        order = []
        for j in range(line):
            order += [b for b in (line - 1 - j, j) if b not in order]
        for b in order:
            for k in range(parts):
                to_sister(b, k).start()
        yield
        for j in range(line - 1):
            for k in range(parts):
                b = line - 1 - j

                @pl.when(b > r)
                def _():
                    to_sister(b, k).wait_recv()

                    @pl.when(r > 0)
                    def _():
                        go_up(b, k).wait_recv()
                        add(b, k, [b])

                    pl.when(r == 0)(lambda: add(b, k, []))
                    go_up(b, k).start()

                @pl.when(j < r)
                def _():
                    to_sister(j, k).wait_recv()

                    @pl.when(r < line - 1)
                    def _():
                        go_down(j, k, -1).wait_recv()
                        add(j, k, [j])

                    pl.when(r == line - 1)(lambda: add(j, k, []))
                    go_down(j, k, r - 1).start()

            yield
        for k in range(parts):
            to_sister(r, k).wait_recv()
            pl.when(r > 0)(lambda: go_up(r, k).wait_recv())
            pl.when(r < line - 1)(lambda: go_down(r, k, r).wait_recv())
            pl.when(r == 0)(lambda: add(r, k, [line], o))
            pl.when(r == line - 1)(lambda: add(r, k, [r], o))
            pl.when((r > 0) & (r < line - 1))(lambda: add(r, k, [r, line], o))
        yield
        for b in range(line):
            for k in range(parts):
                to_sister(b, k).wait_send()
                pl.when(b != r)(lambda: go_up(b, k).wait_send())


class GatherSeq:
    def __init__(self, x, n_seq, n_fsdp):
        self.args, self.in_specs = [x], [ANY]
        self.outs = [jax.ShapeDtypeStruct((n_seq,) + x.shape, x.dtype)]
        self.out_specs = [ANY]
        self.scratch = [DMA((n_seq,)), DMA((n_seq,))]

    def steps(self, at, refs):
        x, o, s_sem, r_sem = refs

        def go(d):
            return send(x, o.at[at.s], s_sem.at[d], r_sem.at[d], at.peer(d))

        for d in reversed(range(1, at.n_seq)):
            go(d).start()
        own = pltpu.make_async_copy(x, o.at[at.s], s_sem.at[0])
        own.start()
        yield
        own.wait()
        for d in range(1, at.n_seq):
            go(d).wait()


class SwapSeq:
    def __init__(self, x, n_seq, n_fsdp):
        self.args, self.in_specs = [x], [ANY]
        self.outs = [jax.ShapeDtypeStruct(x.shape, x.dtype)]
        self.out_specs = [ANY]
        self.scratch = [DMA((n_seq,)), DMA((n_seq,))]

    def steps(self, at, refs):
        x, o, s_sem, r_sem = refs

        def go(d):
            peer = at.peer(d)
            return send(x.at[peer[0]], o.at[at.s], s_sem.at[d], r_sem.at[d], peer)

        for d in reversed(range(1, at.n_seq)):
            go(d).start()
        own = pltpu.make_async_copy(x.at[at.s], o.at[at.s], s_sem.at[0])
        own.start()
        yield
        own.wait()
        for d in range(1, at.n_seq):
            go(d).wait()


class ScatterSeq:
    def __init__(self, part, n_seq, n_fsdp, out_dtype=F32):
        block = part.shape[1:]
        self.args, self.in_specs = [part], [VMEM]
        self.outs = [jax.ShapeDtypeStruct(block, out_dtype)]
        self.out_specs = [VMEM]
        self.scratch = [pltpu.VMEM((n_seq,) + block, part.dtype), DMA((n_seq,)), DMA((n_seq,))]

    def steps(self, at, refs):
        part, o, land, s_sem, r_sem = refs
        rows = part.shape[1]
        tile = 16 if rows % 16 == 0 else rows

        def go(d):
            peer = at.peer(d)
            return send(part.at[peer[0]], land.at[d], s_sem.at[d], r_sem.at[d], peer)

        for d in reversed(range(1, at.n_seq)):
            go(d).start()
        yield
        for d in range(1, at.n_seq):
            go(d).wait()

        def body(i, carry):
            at_rows = pl.ds(i * tile, tile)
            total = part[at.s, at_rows].astype(F32)
            for d in range(1, at.n_seq):
                total = total + land[d, at_rows].astype(F32)
            o[at_rows] = total.astype(o.dtype)
            return carry

        lax.fori_loop(0, rows // tile, body, 0)


def transfer(name, collective_id, n_seq, n_fsdp, *ops):
    n_in = [len(op.args) for op in ops]
    n_out = [len(op.outs) for op in ops]
    n_scratch = [len(op.scratch) for op in ops]

    def kernel(*refs):
        at = Place(n_seq, n_fsdp)
        at.greet()
        first_out = sum(n_in)
        first_scratch = first_out + sum(n_out)
        running = []
        for i, op in enumerate(ops):
            mine = []
            for base, count in ((0, n_in), (first_out, n_out), (first_scratch, n_scratch)):
                start = base + sum(count[:i])
                mine += refs[start : start + count[i]]
            running.append(op.steps(at, mine))
        while running:
            for one in list(running):
                if next(one, "end") == "end":
                    running.remove(one)

    return pl.pallas_call(
        kernel,
        out_shape=[o for op in ops for o in op.outs],
        in_specs=[s for op in ops for s in op.in_specs],
        out_specs=[s for op in ops for s in op.out_specs],
        scratch_shapes=[s for op in ops for s in op.scratch],
        compiler_params=pltpu.CompilerParams(
            collective_id=collective_id, has_side_effects=True, vmem_limit_bytes=48 * 2**20
        ),
        name=name,
    )(*[a for op in ops for a in op.args])


def angles(positions):
    freqs = ROPE_BASE ** (-jnp.arange(0, HEAD, 2).astype(jnp.float32) / HEAD)
    turn = positions.astype(jnp.float32)[:, None] * freqs[None, :]
    return (jnp.cos(turn)[:, None, :], jnp.sin(turn)[:, None, :])


def rotate(field, cosine, sine):
    half = field.shape[-1] // 2
    front = field[..., :half]
    back_half = field[..., half:]
    return jnp.concatenate(
        [front * cosine - back_half * sine, back_half * cosine + front * sine], -1
    )


def norm_back(grad_normed, value, scale, gain):
    weighted = grad_normed * gain
    inner_mean = jnp.mean(weighted * value, axis=-1, keepdims=True)
    return scale * (weighted - value * scale * scale * inner_mean)


def scale_of(value):
    return lax.rsqrt(jnp.mean(value * value, axis=-1, keepdims=True) + NORM_EPS)


def dot(a, b, dims):
    return lax.dot_general(a, b, (dims, ((), ())), preferred_element_type=F32)


def on_device(
    n_seq, n_fsdp,
    hidden_in, gain_attn, attn_weights, gain_mlp, mlp_weights, out_grad, block_slots, doc_ids,
):
    tok_rows = hidden_in.shape[1]
    model = hidden_in.shape[2]
    length = doc_ids.shape[1]
    share = model // n_seq
    heads = share // HEAD
    block_rows = tok_rows // 2
    seq_index = lax.axis_index("seq")
    within = jnp.arange(block_rows, dtype=jnp.int32)
    pos = (block_slots.reshape(-1)[:, None] * block_rows + within[None, :]).reshape(-1)
    doc = doc_ids[0][pos]
    cosine, sine = angles(pos)
    move = functools.partial

    def run(name, cid, *ops):
        return transfer(name, cid, n_seq, n_fsdp, *[op(n_seq=n_seq, n_fsdp=n_fsdp) for op in ops])

    w_share = lax.dynamic_slice_in_dim(attn_weights, seq_index * share, share, 2)
    own_gains = jnp.concatenate(
        [
            jnp.broadcast_to(gain_attn[None], (16,) + gain_attn.shape),
            jnp.broadcast_to(gain_mlp[None], (16,) + gain_mlp.shape),
        ],
        0,
    )
    w, x_all, gains = run(
        "gather_in",
        1,
        move(GatherLine, w_share.reshape(-1, 4 * share), parts=2),
        move(GatherSeq, hidden_in[0]),
        move(GatherLine, own_gains),
    )
    w = w.reshape(model, 4 * share)
    w_qkv, w_out = w[:, : 3 * share], w[:, 3 * share :]
    x_all = x_all.reshape(length, model)
    gains = gains.astype(F32)
    gain_a, gain_m = gains[:, 0].reshape(model), gains[:, 16].reshape(model)
    late_grad, x_all = lax.optimization_barrier((out_grad[0], x_all))
    grad_all = lax.all_gather(late_grad, "fsdp", axis=0, tiled=True)

    x_wide = x_all.astype(F32)
    n1 = (x_wide * scale_of(x_wide) * gain_a).astype(BF16)
    qkv = dot(n1, w_qkv, ((1,), (0,)))

    def turn(field, s):
        return rotate(field.reshape(length, heads, HEAD), cosine, s).astype(BF16)

    q = turn(qkv[:, :share], sine)
    k = turn(qkv[:, share : 2 * share], sine)
    v = qkv[:, 2 * share :].astype(BF16).reshape(length, heads, HEAD)
    allowed = ((pos[None, :] <= pos[:, None]) & (doc[None, :] == doc[:, None]))[None]
    z = jnp.einsum("qhd,khd->hqk", q, k, preferred_element_type=F32) * 0.125
    z = jnp.where(allowed, z, MASKED_OUT)
    top = jnp.max(z, axis=-1, keepdims=True)
    e = jnp.where(allowed, jnp.exp(z - top), 0.0)
    p = e / jnp.sum(e, axis=-1, keepdims=True)
    p_low = p.astype(BF16)
    o = jnp.einsum("hqk,khd->qhd", p_low, v, preferred_element_type=F32)
    o = o.reshape(length, share).astype(BF16)
    (o_all,) = run("gather_o", 2, move(GatherSeq, o))
    o_all = o_all.transpose(1, 0, 2).reshape(length, model)
    y = dot(o_all, w_out, ((1,), (0,))).astype(BF16)
    (y,) = run("swap_y", 3, move(SwapSeq, y.reshape(n_seq, tok_rows, share)))
    y = y.transpose(1, 0, 2).reshape(tok_rows, model)

    source = hidden_in[0].astype(F32)
    middle = source + y.astype(F32)
    scale_m = scale_of(middle)
    n2 = (middle * scale_m * gain_m).astype(BF16)
    (n2_all,) = run("gather_n2", 4, move(GatherLine, n2, parts=2))
    n2_all = n2_all.reshape(-1, model)
    w_gate, w_up, w_down = mlp_weights[:, 0], mlp_weights[:, 1], mlp_weights[:, 2]
    gate = dot(n2_all, w_gate, ((1,), (1,)))
    up = dot(n2_all, w_up, ((1,), (1,)))
    grad_act = dot(grad_all, w_down, ((1,), (1,)))
    sigma = jax.nn.sigmoid(gate)
    hid = (gate * sigma * up).astype(BF16)
    dg = (grad_act * up * sigma * (1.0 + gate * (1.0 - sigma))).astype(BF16)
    du = (grad_act * gate * sigma).astype(BF16)
    mlp_grad = jnp.stack(
        [
            dot(dg, n2_all, ((0,), (0,))).astype(BF16),
            dot(du, n2_all, ((0,), (0,))).astype(BF16),
            dot(hid, grad_all, ((0,), (0,))).astype(BF16),
        ],
        1,
    )
    mlp_grad = lax.psum(mlp_grad, "seq").astype(F32)

    dn2_part = (dot(dg, w_gate, ((1,), (0,))) + dot(du, w_up, ((1,), (0,)))).astype(BF16)
    (dn2,) = run(
        "scatter_dn2", 5, move(ScatterLine, dn2_part.reshape(n_fsdp, tok_rows, model), parts=2)
    )
    out_part = dot(hid, w_down, ((1,), (0,))).astype(BF16)

    dh1 = out_grad[0].astype(F32) + norm_back(dn2, middle, scale_m, gain_m)
    gain_m_term = jnp.sum(dn2 * middle * scale_m, axis=0)
    da = dh1.astype(BF16)
    (da_cols,) = run(
        "swap_da", 6, move(SwapSeq, da.reshape(tok_rows, n_seq, share).transpose(1, 0, 2))
    )
    da_cols = da_cols.reshape(length, share)
    do_part = dot(da_cols, w_out, ((1,), (1,))).astype(BF16)
    do, mlp_out = run(
        "scatter_do",
        7,
        move(ScatterSeq, do_part.reshape(length, n_seq, share).transpose(1, 0, 2), out_dtype=BF16),
        move(ScatterLine, out_part.reshape(n_fsdp, tok_rows, model), parts=2),
    )
    block_out = (middle + mlp_out).astype(BF16)
    do = do.reshape(length, heads, HEAD)
    dp = jnp.einsum("qhd,khd->hqk", do, v, preferred_element_type=F32)
    delta = jnp.sum(p * dp, axis=-1, keepdims=True)
    dz = (p * (dp - delta)).astype(BF16)
    dq = jnp.einsum("hqk,khd->qhd", dz, k, preferred_element_type=F32) * 0.125
    dk = jnp.einsum("hqk,qhd->khd", dz, q, preferred_element_type=F32) * 0.125
    dv = jnp.einsum("hqk,qhd->khd", p_low, do, preferred_element_type=F32)
    dqkv = jnp.concatenate(
        [
            turn(dq, -sine).reshape(length, share),
            turn(dk, -sine).reshape(length, share),
            dv.reshape(length, share).astype(BF16),
        ],
        1,
    )
    dn1_part = dot(dqkv, w_qkv, ((1,), (1,))).astype(BF16)
    dw_qkv = dot(n1, dqkv, ((0,), (0,))).astype(BF16)
    dw_o = dot(o_all, da_cols, ((0,), (0,))).astype(BF16)
    dw = jnp.concatenate([dw_qkv, dw_o], 1)
    dn1, dw = run(
        "scatter_dw",
        8,
        move(ScatterSeq, dn1_part.reshape(n_seq, tok_rows, model)),
        move(ScatterLine, dw.reshape(n_fsdp, -1, 4 * share), parts=2, out_dtype=BF16),
    )
    scale_a = scale_of(source)
    grad_in = (dh1 + norm_back(dn1, source, scale_a, gain_a)).astype(BF16)
    gain_a_term = jnp.sum(dn1 * source * scale_a, axis=0)
    gain_terms = jnp.stack([gain_a_term, gain_m_term], 0).reshape(2, n_fsdp, -1)
    gain_terms = jnp.pad(gain_terms.transpose(1, 0, 2), ((0, 0), (0, 6), (0, 0)))
    dw, gain_terms = run(
        "gather_dw", 9, move(GatherSeq, dw), move(ScatterLine, gain_terms)
    )
    attn_grad = dw.reshape(n_seq, -1, 4, share).transpose(1, 2, 0, 3).reshape(-1, 4, model)
    attn_grad = attn_grad.astype(F32)
    (gain_terms,) = run("gather_gain", 10, move(GatherSeq, gain_terms))
    gain_terms = jnp.sum(gain_terms, axis=0)
    return (block_out[None], grad_in[None], gain_terms[0], attn_grad, gain_terms[1], mlp_grad)


def solution(mesh):
    return jax.shard_map(
        functools.partial(on_device, mesh.shape["seq"], mesh.shape["fsdp"]),
        mesh=mesh,
        in_specs=(
            P("fsdp", "seq", None),
            P("fsdp"),
            P("fsdp", None, None),
            P("fsdp"),
            P("fsdp", None, None),
            P("fsdp", "seq", None),
            P(),
            P("fsdp", None),
        ),
        out_specs=(
            P("fsdp", "seq", None),
            P("fsdp", "seq", None),
            P("fsdp"),
            P("fsdp", None, None),
            P("fsdp"),
            P("fsdp", None, None),
        ),
        check_vma=False,
    )
```

```python
import functools
import types

import jax
import jax.numpy as jnp
from jax import lax
from jax.experimental import pallas as pl
from jax.experimental.pallas import tpu as pltpu
from jax.sharding import PartitionSpec as P

HEAD = 64


NORM_EPS = 1e-05
ROPE_BASE = 130000.0
MASKED_OUT = -1e30
F32 = jnp.float32
BF16 = jnp.bfloat16
MESH = pl.DeviceIdType.MESH
DMA = pltpu.SemaphoreType.DMA
ANY = pl.BlockSpec(memory_space=pl.ANY)
VMEM = pl.BlockSpec(memory_space=pltpu.VMEM)


def send(src, dst, send_sem, recv_sem, device):
    return pltpu.make_async_remote_copy(
        src_ref=src,
        dst_ref=dst,
        send_sem=send_sem,
        recv_sem=recv_sem,
        device_id=device,
        device_id_type=MESH,
    )


class Place:
    def __init__(self, n_seq, n_fsdp):
        self.n_seq, self.line = n_seq, n_fsdp // 2
        self.s = lax.axis_index("seq")
        self.f = lax.axis_index("fsdp")
        self.r = lax.div(self.f, 2)
        self.c = lax.rem(self.f, 2)
        self.up = (self.s, self.f + 2)
        self.down = (self.s, self.f - 2)
        self.sister = (self.s, 2 * self.r + 1 - self.c)

    def peer(self, d):
        return (jnp.bitwise_xor(self.s, d), self.f)

    def greet(self):
        barrier = pltpu.get_barrier_semaphore()
        wrap = 2 * self.line
        partners = [
            (self.s, lax.rem(self.f + 2, wrap)),
            (self.s, lax.rem(self.f + wrap - 2, wrap)),
            self.sister,
        ]
        partners += [self.peer(d) for d in range(1, self.n_seq)]
        for partner in partners:
            pl.semaphore_signal(barrier, inc=1, device_id=partner, device_id_type=MESH)
        pl.semaphore_wait(barrier, len(partners))


class GatherLine:
    def __init__(self, n_fsdp, parts=1):
        line = n_fsdp // 2
        self.scratch = [DMA((line, parts)) for _ in range(5)] + [DMA((1,))]
        self.parts = parts

    def steps(self, at, x, o, refs, use=None):
        line_r, sis_r, up_s, down_s, sis_s, own_s = refs
        parts, line, r, c = self.parts, at.line, at.r, at.c
        rows = o.shape[1] // parts

        def cut(ref, k):
            return ref.at[pl.ds(k * rows, rows)]

        def go_up(src, b, k):
            return send(src, cut(o.at[2 * b + c], k), up_s.at[b, k], line_r.at[b, k], at.up)

        def go_down(src, b, k):
            return send(src, cut(o.at[2 * b + c], k), down_s.at[b, k], line_r.at[b, k], at.down)

        def go_sister(src, b, k):
            return send(src, cut(o.at[2 * b + c], k), sis_s.at[b, k], sis_r.at[b, k], at.sister)

        def complete(b):
            for k in range(parts):
                src = cut(o.at[2 * b + 1 - c], k)
                send(src, src, sis_s.at[b, k], sis_r.at[b, k], at.sister).wait_recv()
            if use is not None:
                use(b)

        own = pltpu.make_async_copy(x, o.at[at.f], own_s.at[0])
        own.start()
        for k in range(parts):
            src = cut(x, k)
            pl.when(r < line - 1)(lambda: go_up(src, r, k).start())
            pl.when(r > 0)(lambda: go_down(src, r, k).start())
            go_sister(src, r, k).start()
        yield
        for t in range(1, line):
            for k in range(parts):
                low, high = r - t, r + t

                @pl.when(low >= 0)
                def _():
                    src = cut(o.at[2 * low + c], k)
                    go_up(src, low, k).wait_recv()
                    pl.when(r < line - 1)(lambda: go_up(src, low, k).start())
                    go_sister(src, low, k).start()

                @pl.when(high < line)
                def _():
                    src = cut(o.at[2 * high + c], k)
                    go_down(src, high, k).wait_recv()
                    pl.when(r > 0)(lambda: go_down(src, high, k).start())
                    go_sister(src, high, k).start()

            yield
            if t == 1:
                own.wait()
                complete(r)
            else:
                pl.when(r - t + 1 >= 0)(lambda: complete(r - t + 1))
                pl.when(r + t - 1 < line)(lambda: complete(r + t - 1))
        pl.when(r - line + 1 >= 0)(lambda: complete(r - line + 1))
        pl.when(r + line - 1 < line)(lambda: complete(r + line - 1))
        yield
        for b in range(line):
            for k in range(parts):
                src = cut(x, k)
                go_sister(src, b, k).wait_send()
                pl.when((b <= r) & (r < line - 1))(lambda: go_up(src, b, k).wait_send())
                pl.when((b >= r) & (r > 0))(lambda: go_down(src, b, k).wait_send())


class ScatterLine:
    def __init__(self, part, n_fsdp, parts=1, far=False):
        line = n_fsdp // 2
        block = part.shape[1:]
        self.scratch = [
            pltpu.VMEM((line,) + block, part.dtype),
            pltpu.VMEM((line + 1,) + block, part.dtype),
        ]
        self.scratch += [DMA((line, parts)), DMA((line, parts)), DMA((line, parts))]
        self.scratch += [DMA((line + 1, parts))]
        if far:
            self.scratch += [pltpu.VMEM((line,) + block, part.dtype), DMA((line,))]
        self.parts, self.far = parts, far

    def steps(self, at, refs):
        part, o, sis, come, sis_s, sis_r, line_s, line_r = refs[:8]
        near, near_s = refs[8:] if self.far else (None, None)
        parts, line, r, c = self.parts, at.line, at.r, at.c
        rows = part.shape[1] // parts
        tile = 16 if rows % 16 == 0 else rows

        def cut(ref, k):
            return ref.at[pl.ds(k * rows, rows)]

        def to_sister(b, k):
            return send(
                cut(part.at[2 * b + 1 - c], k),
                cut(sis.at[b], k),
                sis_s.at[b, k],
                sis_r.at[b, k],
                at.sister,
            )

        def slot(b, own):
            return jnp.where(b == own, line, b)

        def go_up(b, k):
            return send(cut(sis.at[b], k), cut(come.at[b], k), line_s.at[b, k], line_r.at[b, k], at.up)

        def go_down(b, k, own):
            i = slot(b, own)
            return send(
                cut(sis.at[b], k), cut(come.at[i], k), line_s.at[b, k], line_r.at[i, k], at.down
            )

        def add(b, k, came, out=None):
            def body(i, carry):
                at_rows = pl.ds(k * rows + i * tile, tile)
                own = near[b, at_rows] if self.far else part[2 * b + c, at_rows]
                total = own.astype(F32) + sis[b, at_rows].astype(F32)
                for j in came:
                    total = total + come[j, at_rows].astype(F32)
                if out is None:
                    sis[b, at_rows] = total.astype(sis.dtype)
                else:
                    out[at_rows] = total.astype(out.dtype)
                return carry

            lax.fori_loop(0, rows // tile, body, 0)

        order = []
        for j in range(line):
            order += [b for b in (line - 1 - j, j) if b not in order]
        for b in order:
            for k in range(parts):
                to_sister(b, k).start()
        if self.far:
            loads = [
                pltpu.make_async_copy(part.at[2 * b + c], near.at[b], near_s.at[b])
                for b in range(line)
            ]
            for one in loads:
                one.start()
            for one in loads:
                one.wait()
        yield
        for j in range(line - 1):
            for k in range(parts):
                b = line - 1 - j

                @pl.when(b > r)
                def _():
                    to_sister(b, k).wait_recv()

                    @pl.when(r > 0)
                    def _():
                        go_up(b, k).wait_recv()
                        add(b, k, [b])

                    pl.when(r == 0)(lambda: add(b, k, []))
                    go_up(b, k).start()

                @pl.when(j < r)
                def _():
                    to_sister(j, k).wait_recv()

                    @pl.when(r < line - 1)
                    def _():
                        go_down(j, k, -1).wait_recv()
                        add(j, k, [j])

                    pl.when(r == line - 1)(lambda: add(j, k, []))
                    go_down(j, k, r - 1).start()

            yield
        for k in range(parts):
            to_sister(r, k).wait_recv()
            pl.when(r > 0)(lambda: go_up(r, k).wait_recv())
            pl.when(r < line - 1)(lambda: go_down(r, k, r).wait_recv())
            pl.when(r == 0)(lambda: add(r, k, [line], o))
            pl.when(r == line - 1)(lambda: add(r, k, [r], o))
            pl.when((r > 0) & (r < line - 1))(lambda: add(r, k, [r, line], o))
        yield
        for b in range(line):
            for k in range(parts):
                to_sister(b, k).wait_send()
                pl.when(b != r)(lambda: go_up(b, k).wait_send())


class GatherSeq:
    def __init__(self, n_seq):
        self.scratch = [DMA((n_seq,)), DMA((n_seq,))]

    def steps(self, at, refs):
        x, o, s_sem, r_sem = refs

        def go(d):
            return send(x, o.at[at.s], s_sem.at[d], r_sem.at[d], at.peer(d))

        for d in reversed(range(1, at.n_seq)):
            go(d).start()
        own = pltpu.make_async_copy(x, o.at[at.s], s_sem.at[0])
        own.start()
        yield
        own.wait()
        for d in range(1, at.n_seq):
            go(d).wait()


class ScatterSeq:
    def __init__(self, part):
        self.scratch = [pltpu.VMEM(part.shape, part.dtype), DMA(part.shape[:1]), DMA(part.shape[:1])]

    def steps(self, at, refs):
        part, o, land, s_sem, r_sem = refs
        rows = part.shape[1]
        tile = 16 if rows % 16 == 0 else rows

        def go(d):
            peer = at.peer(d)
            return send(part.at[peer[0]], land.at[d], s_sem.at[d], r_sem.at[d], peer)

        for d in reversed(range(1, at.n_seq)):
            go(d).start()
        yield
        for d in range(1, at.n_seq):
            go(d).wait()

        def body(i, carry):
            at_rows = pl.ds(i * tile, tile)
            total = part[at.s, at_rows].astype(F32)
            for d in range(1, at.n_seq):
                total = total + land[d, at_rows].astype(F32)
            o[at_rows] = total.astype(o.dtype)
            return carry

        lax.fori_loop(0, rows // tile, body, 0)


class ReduceSeq:
    def __init__(self, shape, dtype, n_seq):
        rows, cols = shape
        self.bits = n_seq.bit_length() - 1
        self.rows = rows // 2
        self.room = self.rows - (self.rows >> self.bits)
        self.scratch = [
            pltpu.VMEM(shape, dtype),
            pltpu.VMEM((2 * self.room, cols), dtype),
            DMA((2,)),
            DMA((2, self.bits)),
            DMA((2, self.bits)),
            DMA((2, n_seq)),
            DMA((2, n_seq)),
            DMA((2,)),
        ]

    def steps(self, at, refs):
        g_in, o, g, land, load_s, rs_s, rs_r, ag_s, ag_r, own_s = refs
        bits = self.bits
        orders = [[(i + p) % bits for i in range(bits)] for p in range(2)]
        mult = self.rows >> bits

        def bit(t, b):
            return jnp.bitwise_and(lax.shift_right_logical(t, b), 1)

        def base(p, t, n):
            low = p * self.rows
            for i in range(n):
                low = low + bit(t, orders[p][i]) * (self.rows >> (i + 1))
            return pl.multiple_of(low, mult)

        def load(p):
            part = pl.ds(p * self.rows, self.rows)
            return pltpu.make_async_copy(g_in.at[part], g.at[part], load_s.at[p])

        def slot(p, i):
            return p * self.room + sum(self.rows >> (j + 1) for j in range(i))

        def halve(p, i):
            size = self.rows >> (i + 1)
            other = jnp.bitwise_xor(at.s, 1 << orders[p][i])
            return send(
                g.at[pl.ds(base(p, other, i + 1), size)],
                land.at[pl.ds(slot(p, i), size)],
                rs_s.at[p, i],
                rs_r.at[p, i],
                (other, at.f),
            )

        def add(p, i):
            size = self.rows >> (i + 1)
            low, first = base(p, at.s, i + 1), slot(p, i)

            def body(j, carry):
                mine = pl.ds(pl.multiple_of(low + j * 16, 16), 16)
                came = pl.ds(pl.multiple_of(first + j * 16, 16), 16)
                total = g[mine].astype(F32) + land[came].astype(F32)
                g[mine] = total.astype(g.dtype)
                return carry

            lax.fori_loop(0, size // 16, body, 0)

        def masks(p, j):
            out = [0]
            for i in range(j):
                out += [m | (1 << orders[p][bits - 1 - i]) for m in out]
            return out

        def double(p, j, mask):
            b = orders[p][bits - 1 - j]
            piece = pl.ds(base(p, jnp.bitwise_xor(at.s, mask), bits), mult)
            src = g.at[piece] if mask == 0 else o.at[piece]
            i = (1 << b) | mask
            return send(
                src, o.at[piece], ag_s.at[p, i], ag_r.at[p, i], (jnp.bitwise_xor(at.s, 1 << b), at.f)
            )

        def arrive(p, j, mask):
            b = orders[p][bits - 1 - j]
            piece = pl.ds(base(p, jnp.bitwise_xor(at.s, (1 << b) | mask), bits), mult)
            i = (1 << b) | mask
            return send(
                o.at[piece], o.at[piece], ag_s.at[p, i], ag_r.at[p, i],
                (jnp.bitwise_xor(at.s, 1 << b), at.f),
            )

        def own(p):
            piece = pl.ds(base(p, at.s, bits), mult)
            return pltpu.make_async_copy(g.at[piece], o.at[piece], own_s.at[p])

        for p in range(2):
            load(p).start()
        for p in range(2):
            load(p).wait()
            halve(p, 0).start()
        yield
        for i in range(bits):
            for p in range(2):
                halve(p, i).wait_recv()
                add(p, i)
                if i + 1 < bits:
                    halve(p, i + 1).start()
                else:
                    for j in range(bits):
                        double(p, j, 0).start()
                    own(p).start()
                yield
        for j in range(bits):
            for p in range(2):
                for mask in masks(p, j):
                    arrive(p, j, mask).wait_recv()
                    came = (1 << orders[p][bits - 1 - j]) | mask
                    for later in range(j + 1, bits):
                        double(p, later, came).start()
                yield
        for p in range(2):
            own(p).wait()
            for i in range(bits):
                halve(p, i).wait_send()
            for j in range(bits):
                for mask in masks(p, j):
                    double(p, j, mask).wait_send()


class SpreadSeq:
    def __init__(self, n_seq):
        self.bits = n_seq.bit_length() - 1
        self.scratch = [DMA((2, n_seq)), DMA((2, n_seq)), DMA((1,))]

    def steps(self, at, refs):
        x, o, s_sem, r_sem, own_s = refs
        bits, half = self.bits, x.shape[0] // 2
        orders = [[(i + p) % bits for i in range(bits)] for p in range(2)]

        def known(p, j):
            out = [0]
            for i in range(j):
                out += [m | (1 << orders[p][i]) for m in out]
            return out

        def piece(p, mask):
            return o.at[jnp.bitwise_xor(at.s, mask), pl.ds(p * half, half)]

        def go(p, j, mask):
            b = 1 << orders[p][j]
            src = x.at[pl.ds(p * half, half)] if mask == 0 else piece(p, mask)
            i = b | mask
            return send(src, piece(p, mask), s_sem.at[p, i], r_sem.at[p, i], at.peer(b))

        def arrive(p, j, mask):
            b = 1 << orders[p][j]
            i = b | mask
            here = piece(p, i)
            return send(here, here, s_sem.at[p, i], r_sem.at[p, i], at.peer(b))

        for p in range(2):
            for j in range(bits):
                go(p, j, 0).start()
        own = pltpu.make_async_copy(x, o.at[at.s], own_s.at[0])
        own.start()
        yield
        for j in range(bits):
            for p in range(2):
                for mask in known(p, j):
                    arrive(p, j, mask).wait_recv()
                    for later in range(j + 1, bits):
                        go(p, later, (1 << orders[p][j]) | mask).start()
            yield
        own.wait()
        for j in range(bits):
            for p in range(2):
                for mask in known(p, j):
                    go(p, j, mask).wait_send()


def interleave(order, running):
    for name in order:
        if name in running and next(running[name], END) is END:
            del running[name]
    while running:
        for name in list(running):
            if next(running[name], END) is END:
                del running[name]


END = object()


class Rooms:
    def __init__(self):
        self.args, self.in_specs, self.outs, self.out_specs, self.scratch = [], [], [], [], []
        self.names = ([], [], [])

    def note(self, group, name, x):
        many = isinstance(x, (list, tuple))
        self.names[group].append((name, len(x) if many else None))
        return list(x) if many else [x]

    def take(self, spec, **arrays):
        for name, x in arrays.items():
            new = self.note(0, name, x)
            self.args += new
            self.in_specs += [spec] * len(new)

    def give(self, spec, **shapes):
        for name, x in shapes.items():
            new = self.note(1, name, x)
            self.outs += new
            self.out_specs += [spec] * len(new)

    def keep(self, **kinds):
        for name, x in kinds.items():
            self.scratch += self.note(2, name, x)

    def bind(self, refs, groups):
        table, refs = types.SimpleNamespace(), list(refs)
        for group in groups:
            for name, many in self.names[group]:
                count = 1 if many is None else many
                mine, refs = refs[:count], refs[count:]
                setattr(table, name, mine[0] if many is None else mine)
        return table

    def run(self, body, name, collective_id, n_seq, n_fsdp):
        def kernel(*refs):
            at = Place(n_seq, n_fsdp)
            at.greet()
            body(at, self.bind(refs, (0, 1, 2)))

        out = pl.pallas_call(
            kernel,
            out_shape=self.outs,
            in_specs=self.in_specs,
            out_specs=self.out_specs,
            scratch_shapes=self.scratch,
            compiler_params=pltpu.CompilerParams(
                collective_id=collective_id, has_side_effects=True, vmem_limit_bytes=62 * 2**20
            ),
            name=name,
        )(*self.args)
        return self.bind(out, (1,))


def like(shape, dtype=BF16):
    return jax.ShapeDtypeStruct(tuple(shape), dtype)


def room(*shape, dtype=BF16):
    return pltpu.VMEM(shape, dtype)


def dot(a, b, dims):
    return lax.dot_general(a, b, (dims, ((), ())), preferred_element_type=F32)


NN = ((1,), (0,))
NT = ((1,), (1,))
TN = ((0,), (0,))


def turned(x, cos, sin):
    lane = lax.broadcasted_iota(jnp.int32, x.shape, 1)
    other = jnp.where(lane % HEAD < HEAD // 2, pltpu.roll(x, 96, 1), pltpu.roll(x, 32, 1))
    return x * cos + other * sin


def head_masks():
    lane = lax.broadcasted_iota(jnp.int32, (1, 128), 1)
    first = (lane < HEAD).astype(F32)
    return first, 1.0 - first


def back_pair(pair, do, q, k, v, lse, cos, sin, dqkv, masking, dk, dv):
    pos_col, pos_row, doc_col, doc_row = masking
    length, share = q.shape
    span = 256
    masks = head_masks()
    lane = lax.broadcasted_iota(jnp.int32, (span, 128), 1)
    lanes = slice(pair * 128, pair * 128 + 128)
    dk[...] = jnp.zeros_like(dk)
    dv[...] = jnp.zeros_like(dv)

    def one_span(i, carry):
        rows = pl.ds(pl.multiple_of(i * span, span), span)
        allowed = (pos_row[...] <= pos_col[rows]) & (doc_row[...] == doc_col[rows])
        bias = jnp.where(allowed, 0.0, MASKED_OUT)
        dq = jnp.zeros((span, 128), F32)
        for h in range(2):
            mask = masks[h].astype(BF16)
            field, grad = q[rows, lanes] * mask, do[rows, lanes] * mask
            log_total = jnp.sum(
                jnp.where(lane == 2 * pair + h, lse[rows], 0.0), axis=-1, keepdims=True
            )
            z = dot(field, k[:, lanes], NT) * 0.125 + bias
            prob = jnp.exp(z - log_total)
            dp = dot(grad, v[:, lanes], NT)
            delta = jnp.sum(prob * dp, axis=-1, keepdims=True)
            dz = (prob * (dp - delta)).astype(BF16)
            dq = dq + dot(dz, k[:, lanes], NN) * masks[h]
            dk[...] += dot(dz, field, TN)
            dv[...] += dot(prob.astype(BF16), grad, TN)
        dqkv[rows, lanes] = turned(dq * 0.125, cos[rows], -sin[rows]).astype(BF16)
        return carry

    lax.fori_loop(0, length // span, one_span, 0)
    at = share + pair * 128
    dqkv[:, at : at + 128] = turned(dk[...] * 0.125, cos[...], -sin[...]).astype(BF16)
    at = 2 * share + pair * 128
    dqkv[:, at : at + 128] = dv[...].astype(BF16)


def norm_back(grad_normed, value, scale, gain):
    weighted = grad_normed * gain
    inner_mean = jnp.mean(weighted * value, axis=-1, keepdims=True)
    return scale * (weighted - value * scale * scale * inner_mean)


def scale_of(value):
    return lax.rsqrt(jnp.mean(value * value, axis=-1, keepdims=True) + NORM_EPS)


def front(n_seq, n_fsdp, w_own, hidden, gains, out_grad, mlp_w, tables):
    cos, sin, pos_col, pos_row, doc_col, doc_row = tables
    tok, model = hidden.shape
    length, share = n_seq * tok, w_own.shape[1] // 4
    line, rows_f, units = n_fsdp // 2, w_own.shape[0], mlp_w.shape[1]
    qkv_shape, o_shape = (n_fsdp, rows_f, 3 * share), (n_fsdp, rows_f, share)
    per = n_fsdp // n_seq
    n_pairs = share // 128
    span = 256
    get_w, get_o = GatherLine(n_fsdp, 2), GatherLine(n_fsdp)
    get_gain, get_grad, get_n2 = GatherLine(n_fsdp), GatherLine(n_fsdp, 2), GatherLine(n_fsdp, 2)
    get_x = GatherSeq(n_seq)
    rooms = Rooms()
    rooms.take(
        VMEM, hidden=hidden, gains=gains, cos=cos, sin=sin,
        pos_col=pos_col, pos_row=pos_row, doc_col=doc_col, doc_row=doc_row,
    )
    rooms.take(ANY, w_own=w_own, out_grad=out_grad, mlp_w=mlp_w)
    rooms.give(
        ANY,
        w_qkv_out=like(qkv_shape),
        w_o_out=like(o_shape),
        n1_out=like((n_seq, length, share)),
        o_out=like((n_seq, length, share)),
        n2_out=like((n_fsdp, tok, model)),
        grad_out=like((n_fsdp, tok, model)),
        hid=like((n_fsdp * tok, units)),
        dg=like((n_fsdp * tok, units)),
        du=like((n_fsdp * tok, units)),
    )
    rooms.give(
        VMEM,
        q=like((length, share)),
        k=like((length, share)),
        v=like((length, share)),
        lse=like((length, 128), F32),
        middle=like((tok, model), F32),
        gain_a=like((1, model), F32),
        gain_m=like((1, model), F32),
    )
    rooms.keep(
        get_w=get_w.scratch, get_o=get_o.scratch, get_gain=get_gain.scratch,
        get_grad=get_grad.scratch, get_n2=get_n2.scratch, get_x=get_x.scratch,
        w_qkv_all=room(*qkv_shape),
        w_o_all=room(*o_shape),
        gains_all=room(n_fsdp, *gains.shape),
        x_all=room(n_seq, tok, model),
        n1=room(n_fsdp, length, rows_f),
        o_all=room(n_seq, length, share),
        y_total=room(length, share, dtype=F32),
        y=room(n_seq, tok, share),
        y_land=room(n_seq, tok, share),
        n2=room(tok, model),
        n2_all=room(n_fsdp, tok, model),
        grad_all=room(n_fsdp, tok, model),
        w_gate=room(units, model),
        w_up=room(units, model),
        w_down=room(units, model),
        act=room(n_fsdp * tok, units, dtype=F32),
        stage=room(line, 3, 2 * tok, units),
        load=DMA((3,)),
        save=DMA((6 + n_fsdp,)),
        stage_s=DMA((line, 3)),
        o_s=DMA((n_pairs, n_seq)),
        o_r=DMA((n_pairs, n_seq)),
        y_s=DMA((n_seq,)),
        y_r=DMA((n_seq,)),
    )

    def body(at, r):
        loads = [
            pltpu.make_async_copy(r.mlp_w.at[i], w, r.load.at[i])
            for i, w in enumerate((r.w_gate, r.w_up, r.w_down))
        ]
        saves = []
        w_qkv, w_o = r.w_own.at[:, pl.ds(0, 3 * share)], r.w_own.at[:, pl.ds(3 * share, share)]

        def save(src, dst):
            saves.append(pltpu.make_async_copy(src, dst, r.save.at[len(saves)]))
            saves[-1].start()

        def total(c, rows, cols):
            low, left = (c // 2) * length, (c % 2) * share
            return (
                slice(low + rows.start, low + rows.stop), slice(left + cols.start, left + cols.stop)
            )

        def project(b):
            for f in (2 * b, 2 * b + 1):
                for c in range(3):
                    weights = r.w_qkv_all[f, :, c * share : (c + 1) * share]
                    for i in range(0, length, span):
                        part = dot(r.n1[f, i : i + span], weights, NN)
                        r.act[total(c, slice(i, i + span), slice(0, share))] += part

        def grad_of(b):
            rows = pl.ds(pl.multiple_of(2 * tok * b, 2 * tok), 2 * tok)
            grad = r.grad_all[pl.ds(2 * b, 2)].reshape(2 * tok, model)
            r.act[rows] = dot(grad, r.w_down[...], NT)

        def stored(b, k):
            rows = pl.ds(pl.multiple_of(2 * tok * b, 2 * tok), 2 * tok)
            return pltpu.make_async_copy(
                r.stage.at[b, k], (r.hid, r.dg, r.du)[k].at[rows], r.stage_s.at[b, k]
            )

        def activate(b):
            rows = pl.ds(pl.multiple_of(2 * tok * b, 2 * tok), 2 * tok)
            n2 = r.n2_all[pl.ds(2 * b, 2)].reshape(2 * tok, model)
            gate = dot(n2, r.w_gate[...], NT)
            up = dot(n2, r.w_up[...], NT)
            grad = r.act[rows]
            sigma = jax.nn.sigmoid(gate)
            silu = gate * sigma
            r.stage[b, 0] = (silu * up).astype(BF16)
            r.stage[b, 1] = (grad * up * sigma * (1.0 + gate * (1.0 - sigma))).astype(BF16)
            r.stage[b, 2] = (grad * silu).astype(BF16)
            for k in range(3):
                stored(b, k).start()

        def attend(pair):
            lanes = slice(pair * 128, pair * 128 + 128)
            masks = head_masks()
            lane = lax.broadcasted_iota(jnp.int32, (span, 128), 1)

            def one_span(i, carry):
                rows = pl.ds(pl.multiple_of(i * span, span), span)
                allowed = (r.pos_row[...] <= r.pos_col[rows]) & (r.doc_row[...] == r.doc_col[rows])
                bias = jnp.where(allowed, 0.0, MASKED_OUT)
                parts = []
                for h in range(2):
                    field = r.q[rows, lanes] * masks[h].astype(BF16)
                    z = dot(field, r.k[:, lanes], NT) * 0.125 + bias
                    top = jnp.max(z, axis=-1, keepdims=True)
                    e = jnp.exp(z - top)
                    sum_e = jnp.sum(e, axis=-1, keepdims=True)
                    prob = (e * (1.0 / sum_e)).astype(BF16)
                    parts.append(dot(prob, r.v[:, lanes], NN) * masks[h])
                    here = lane == 2 * pair + h
                    r.lse[rows] = jnp.where(here, top + jnp.log(sum_e), r.lse[rows])
                r.o_all[at.s, rows, lanes] = (parts[0] + parts[1]).astype(BF16)
                return carry

            lax.fori_loop(0, length // span, one_span, 0)

        def go_o(pair, d, owner):
            here = r.o_all.at[owner, :, pl.ds(pair * 128, 128)]
            return send(here, here, r.o_s.at[pair, d], r.o_r.at[pair, d], at.peer(d))

        def go_y(d):
            peer = at.peer(d)
            return send(r.y.at[peer[0]], r.y_land.at[d], r.y_s.at[d], r.y_r.at[d], peer)

        def chain():
            weights = get_w.steps(at, w_qkv, r.w_qkv_all, r.get_w, project)
            next(weights)
            rows_in = get_x.steps(at, [r.hidden, r.x_all] + r.get_x)
            next(rows_in)
            for one in loads:
                one.start()
            r.act[...] = jnp.zeros_like(r.act)
            for _ in get_gain.steps(at, r.gains, r.gains_all, r.get_gain):
                pass
            for f in range(n_fsdp):
                cols = slice(f * rows_f, (f + 1) * rows_f)
                r.gain_a[:, cols] = r.gains_all[f, 0:1].astype(F32)
                r.gain_m[:, cols] = r.gains_all[f, 16:17].astype(F32)
            next(weights)
            for _ in rows_in:
                pass
            r.lse[...] = jnp.zeros_like(r.lse)

            def norm(i, carry):
                j, k = i // (tok // 16), i % (tok // 16)
                x = r.x_all[j, pl.ds(pl.multiple_of(k * 16, 16), 16)].astype(F32)
                normed = (x * scale_of(x) * r.gain_a[...]).astype(BF16)
                rows = pl.ds(pl.multiple_of(i * 16, 16), 16)
                for f in range(n_fsdp):
                    r.n1[f, rows] = normed[:, f * rows_f : (f + 1) * rows_f]
                return carry

            lax.fori_loop(0, length // 16, norm, 0)
            for f in range(n_fsdp):
                save(r.n1.at[f], r.n1_out.at[f // per, :, pl.ds((f % per) * rows_f, rows_f)])
            yield
            for _ in weights:
                yield
            save(r.w_qkv_all, r.w_qkv_out)
            for c, out in enumerate((r.q, r.k)):
                for j in range(0, share, 128):
                    field = r.act[total(c, slice(0, length), slice(j, j + 128))]
                    out[:, j : j + 128] = turned(field, r.cos[...], r.sin[...]).astype(BF16)
            r.v[...] = r.act[total(2, slice(0, length), slice(0, share))].astype(BF16)
            projected.append(True)
            yield
            for pair in range(n_pairs):
                attend(pair)
                for d in reversed(range(1, n_seq)):
                    go_o(pair, d, at.s).start()
                yield
            for _ in out_weights:
                pass
            for d in range(n_seq):
                owner = at.peer(d)[0]
                if d:
                    for pair in range(n_pairs):
                        go_o(pair, d, owner).wait_recv()
                for h in range(per):
                    part = dot(
                        r.o_all[owner, :, h * rows_f : (h + 1) * rows_f],
                        r.w_o_all[owner * per + h],
                        NN,
                    )
                    if d == 0 and h == 0:
                        r.y_total[...] = part
                    else:
                        r.y_total[...] += part
                yield
            for j in range(n_seq):
                r.y[j] = r.y_total[j * tok : (j + 1) * tok].astype(BF16)
            for d in reversed(range(1, n_seq)):
                go_y(d).start()
            save(r.o_all, r.o_out)
            save(r.w_o_all, r.w_o_out)
            r.y_land[0] = r.y[at.s]
            yield
            for d in range(1, n_seq):
                go_y(d).wait()

            def middle(i, carry):
                rows = pl.ds(pl.multiple_of(i * 16, 16), 16)
                for j in range(n_seq):
                    cols = slice(j * share, (j + 1) * share)
                    branch = r.y_land[jnp.bitwise_xor(at.s, j), rows].astype(F32)
                    r.middle[rows, cols] = r.hidden[rows, cols].astype(F32) + branch
                h = r.middle[rows]
                r.n2[rows] = (h * scale_of(h) * r.gain_m[...]).astype(BF16)
                return carry

            lax.fori_loop(0, tok // 16, middle, 0)
            yield
            tokens = get_n2.steps(at, r.n2, r.n2_all, r.get_n2, activate)
            next(tokens)
            yield
            next(tokens)
            for _ in grads:
                pass
            for one in loads[:2]:
                one.wait()
            for _ in tokens:
                yield

        def cotangents():
            while not projected:
                yield
            loads[2].wait()
            yield from get_grad.steps(at, r.out_grad, r.grad_all, r.get_grad, grad_of)
            save(r.grad_all, r.grad_out)

        projected = []
        out_weights = get_o.steps(at, w_o, r.w_o_all, r.get_o)
        grads = cotangents()
        order = [0, 0, 0, 1, 0, 0, 1, 0, 1, 0, 1, 0, 1, 1, 2, 0, 0, 2, 0, 0, 0, 0, 2, 0, 2, 0]
        interleave(order, {0: chain(), 1: out_weights, 2: grads})
        for pair in range(n_pairs):
            for d in range(1, n_seq):
                go_o(pair, d, at.s).wait_send()
        save(r.n2_all, r.n2_out)
        for b in range(line):
            for k in range(3):
                stored(b, k).wait()
        for one in saves:
            one.wait()

    return rooms.run(body, "front", 1, n_seq, n_fsdp)


BACK_ONE_ORDER = [2, 0, 0, 0, 3]


def back_one(n_seq, n_fsdp, dn2_part, middle, out_grad, gain_m, w_qkv, w_o, o_all, n1, saved, grads):
    q, k, v, lse, cos, sin, pos_col, pos_row, doc_col, doc_row = saved
    tok, model = middle.shape
    length, share = q.shape
    rooms = Rooms()
    rooms.take(
        VMEM, middle=middle, out_grad=out_grad, gain_m=gain_m, q=q, k=k, v=v, lse=lse,
        cos=cos, sin=sin, pos_col=pos_col, pos_row=pos_row, doc_col=doc_col, doc_row=doc_row,
    )
    rooms.take(ANY, dn2_part=dn2_part, w_qkv=w_qkv, w_o=w_o, o_all=o_all, n1=n1, g_in=grads)
    rooms.give(ANY, g_out=[like(g.shape) for g in grads], dw_qkv=like((model, 3 * share)))
    rooms.give(
        VMEM,
        dh1=like((tok, model), F32),
        gain=like((8, model), F32),
        dn1_part=like((n_seq, tok, model)),
        dw_o=like((model // n_fsdp, share)),
    )
    line = ScatterLine(dn2_part, n_fsdp, 2, far=True)
    o_block = like((n_fsdp, model // n_fsdp, share))
    line_o = ScatterLine(o_block, n_fsdp)
    reduces = [ReduceSeq(g.shape, g.dtype, n_seq) for g in grads]
    rooms.keep(
        line=line.scratch,
        line_o=line_o.scratch,
        reduce_0=reduces[0].scratch,
        reduce_1=reduces[1].scratch,
        dw_o_part=room(*o_block.shape),
        dn2=room(tok, model, dtype=F32),
        da=room(tok, model),
        da_cols=room(length, share),
        w_qkv_here=room(*w_qkv.shape),
        w_o_here=room(*w_o.shape),
        o_here=room(*o_all.shape),
        do_part=room(n_seq, length, share),
        do_land=room(n_seq, length, share),
        do=room(length, share),
        dqkv=room(length, 3 * share),
        dk=room(length, 128, dtype=F32),
        dv=room(length, 128, dtype=F32),
        dw_stage=room(2, share, 3 * share),
        load=DMA((4,)),
        stage=DMA((2,)),
        swap=[DMA((n_seq,)), DMA((n_seq,))],
        do_sem=[DMA((n_seq,)), DMA((n_seq,))],
    )

    def body(at, r):
        def chain():
            loads = [
                pltpu.make_async_copy(a, b, r.load.at[i])
                for i, (a, b) in enumerate(
                    ((r.w_qkv, r.w_qkv_here), (r.w_o, r.w_o_here), (r.o_all, r.o_here), (r.n1, r.o_here))
                )
            ]
            for one in loads[:3]:
                one.start()
            yield from line.steps(at, [r.dn2_part, r.dn2] + r.line)
            middle, out_grad, gain_m = r.middle, r.out_grad, r.gain_m
            dn2, dh1, da, gain = r.dn2, r.dh1, r.da, r.gain
            gain[...] = jnp.zeros_like(gain)

            def norm(i, carry):
                rows = pl.ds(i * 16, 16)
                h, grad = middle[rows], dn2[rows]
                scale = lax.rsqrt(jnp.mean(h * h, axis=-1, keepdims=True) + NORM_EPS)
                wide = out_grad[rows].astype(F32) + norm_back(grad, h, scale, gain_m[...])
                dh1[rows] = wide
                da[rows] = wide.astype(BF16)
                term = grad * h * scale
                gain[...] += term[:8] + term[8:]
                return carry

            lax.fori_loop(0, tok // 16, norm, 0)
            da_cols = r.da_cols
            swap_s, swap_r = r.swap

            def swap(d):
                peer = at.peer(d)
                cols = pl.ds(pl.multiple_of(peer[0] * share, 128), share)
                rows = pl.ds(pl.multiple_of(at.s * tok, tok), tok)
                return send(da.at[:, cols], da_cols.at[rows], swap_s.at[d], swap_r.at[d], peer)

            for d in reversed(range(1, n_seq)):
                swap(d).start()
            cols = pl.ds(pl.multiple_of(at.s * share, 128), share)
            rows = pl.ds(pl.multiple_of(at.s * tok, tok), tok)
            da_cols[rows] = da[:, cols]
            for one in loads[:3]:
                one.wait()
            yield
            for d in range(1, n_seq):
                swap(d).wait()
            w_qkv_here, w_o_here, o_here = r.w_qkv_here, r.w_o_here, r.o_here
            do_part, do_land = r.do_part, r.do_land
            do_s, do_r = r.do_sem

            def go(d):
                return send(
                    do_part.at[d], do_land.at[d], do_s.at[d], do_r.at[d], at.peer(d)
                )

            for d in reversed(range(n_seq)):
                rows = pl.ds(pl.multiple_of(at.peer(d)[0] * share, share), share)
                do_part[d] = dot(da_cols[...], w_o_here[rows], NT).astype(BF16)
                if d:
                    go(d).start()
            yield
            dw_o = r.dw_o_part
            per = n_fsdp // n_seq
            for j in range(n_seq):
                field = dot(o_here[j], da_cols[...], TN).astype(BF16)
                dw_o[j * per : (j + 1) * per] = field.reshape((per,) + dw_o.shape[1:])
            loads[3].start()
            running[1] = line_o.steps(at, [dw_o, r.dw_o] + r.line_o)
            yield
            for d in range(1, n_seq):
                go(d).wait()
            do = r.do

            def sum_do(i, carry):
                rows = pl.ds(i * 16, 16)
                total = do_part[0, rows].astype(F32)
                for d in range(1, n_seq):
                    total = total + do_land[d, rows].astype(F32)
                do[rows] = total.astype(BF16)
                return carry

            lax.fori_loop(0, length // 16, sum_do, 0)
            yield
            dqkv = r.dqkv
            masking = [r.pos_col, r.pos_row, r.doc_col, r.doc_row]
            for pair in range(share // 128):
                back_pair(
                    pair, do, r.q, r.k, r.v, r.lse, r.cos, r.sin,
                    dqkv, masking, r.dk, r.dv,
                )
                yield
            loads[3].wait()
            dw_qkv, stage, stage_s = r.dw_qkv, r.dw_stage, r.stage

            def put(j):
                return pltpu.make_async_copy(
                    stage.at[j % 2], dw_qkv.at[pl.ds(j * share, share)], stage_s.at[j % 2]
                )

            for j in range(n_seq):
                if j >= 2:
                    put(j - 2).wait()
                stage[j % 2] = dot(o_here[j], dqkv[...], TN).astype(BF16)
                put(j).start()
                yield
            dn1_part = r.dn1_part
            for j in range(n_seq):
                rows = slice(j * share, (j + 1) * share)
                field = dot(dqkv[...], w_qkv_here[rows], NT).astype(BF16)
                dn1_part[:, :, rows] = field.reshape(n_seq, tok, share)
                yield
            put(n_seq - 2).wait()
            put(n_seq - 1).wait()

        running = {
            0: chain(),
            2: reduces[0].steps(at, [r.g_in[0], r.g_out[0]] + r.reduce_0),
            3: reduces[1].steps(at, [r.g_in[1], r.g_out[1]] + r.reduce_1),
        }
        interleave(BACK_ONE_ORDER, running)

    return rooms.run(body, "back_one", 2, n_seq, n_fsdp)


BACK_TWO_ORDER = [0, 2, 1, 3, 0, 2, 0, 1, 0]


def back_two(
    n_seq, n_fsdp, dn1_part, dw_qkv, dw_o, out_part, middle, source, dh1, gain_a, gain_m_term, grad
):
    tok, model = middle.shape
    rooms = Rooms()
    line = ScatterLine(dw_qkv, n_fsdp, 2, far=True)
    line_out = ScatterLine(out_part, n_fsdp, 2, far=True)
    gain_block = like((n_fsdp, 8, model // n_fsdp), F32)
    line_gain = ScatterLine(gain_block, n_fsdp)
    scatter = ScatterSeq(dn1_part)
    reduce = ReduceSeq(grad.shape, grad.dtype, n_seq)
    spread, spread_o = SpreadSeq(n_seq), SpreadSeq(n_seq)
    gather = GatherSeq(n_seq)
    rooms.take(
        VMEM, dn1_part=dn1_part, middle=middle, source=source, dh1=dh1,
        gain_a=gain_a, gain_m_term=gain_m_term,
    )
    rooms.take(ANY, dw_qkv=dw_qkv, out_part=out_part, dw_o=dw_o, g_in=grad)
    rooms.give(
        ANY,
        g_out=like(grad.shape),
        dw_qkv_all=like((n_seq,) + dw_qkv.shape[1:]),
        dw_o_all=like((n_seq,) + dw_o.shape),
    )
    rooms.give(
        VMEM,
        block_out=like((tok, model)),
        grad_in=like((tok, model)),
        gains=like(gain_block.shape[1:], F32),
    )
    rooms.keep(
        line=line.scratch,
        line_out=line_out.scratch,
        line_gain=line_gain.scratch,
        scatter=scatter.scratch,
        reduce=reduce.scratch,
        spread=spread.scratch,
        spread_o=spread_o.scratch,
        gather=gather.scratch,
        dw_own=room(*dw_qkv.shape[1:]),
        mlp_out=room(tok, model, dtype=F32),
        dn1=room(tok, model, dtype=F32),
        gain_part=room(*gain_block.shape, dtype=F32),
        gain_own=room(*gain_block.shape[1:], dtype=F32),
        gain_all=room(n_seq, *gain_block.shape[1:], dtype=F32),
        gain_sum=room(8, model, dtype=F32),
    )

    def body(at, r):
        def weights():
            yield from line.steps(at, [r.dw_qkv, r.dw_own] + r.line)
            yield from spread.steps(at, [r.dw_own, r.dw_qkv_all] + r.spread)

        def rows_out():
            yield from line_out.steps(at, [r.out_part, r.mlp_out] + r.line_out)
            middle, mlp_out, block_out = r.middle, r.mlp_out, r.block_out

            def add(i, carry):
                rows = pl.ds(i * 16, 16)
                block_out[rows] = (middle[rows] + mlp_out[rows]).astype(BF16)
                return carry

            lax.fori_loop(0, tok // 16, add, 0)

        def rows_in():
            yield from scatter.steps(at, [r.dn1_part, r.dn1] + r.scatter)
            source, dh1, dn1 = r.source, r.dh1, r.dn1
            gain_a, grad_in, gain_sum = r.gain_a, r.grad_in, r.gain_sum
            gain_sum[...] = jnp.zeros_like(gain_sum)

            def norm(i, carry):
                rows = pl.ds(i * 16, 16)
                x, grad = source[rows].astype(F32), dn1[rows]
                scale = lax.rsqrt(jnp.mean(x * x, axis=-1, keepdims=True) + NORM_EPS)
                wide = dh1[rows] + norm_back(grad, x, scale, gain_a[...])
                grad_in[rows] = wide.astype(BF16)
                term = grad * x * scale
                gain_sum[...] += term[:8] + term[8:]
                return carry

            lax.fori_loop(0, tok // 16, norm, 0)
            first = jnp.sum(gain_sum[...], axis=0, keepdims=True)
            second = jnp.sum(r.gain_m_term[...], axis=0, keepdims=True)
            row = lax.broadcasted_iota(jnp.int32, gain_sum.shape, 0)
            both = jnp.where(row == 0, first, jnp.where(row == 1, second, 0.0))
            part, width = r.gain_part, model // n_fsdp
            for f in range(n_fsdp):
                part[f] = both[:, f * width : (f + 1) * width]
            yield
            yield from line_gain.steps(at, [part, r.gain_own] + r.line_gain)
            yield from gather.steps(at, [r.gain_own, r.gain_all] + r.gather)
            total = r.gain_all[0]
            for j in range(1, n_seq):
                total = total + r.gain_all[j]
            r.gains[...] = total

        running = {
            0: weights(),
            1: reduce.steps(at, [r.g_in, r.g_out] + r.reduce),
            2: rows_in(),
            3: spread_o.steps(at, [r.dw_o, r.dw_o_all] + r.spread_o),
            4: rows_out(),
        }
        interleave(BACK_TWO_ORDER, running)

    return rooms.run(body, "back_two", 3, n_seq, n_fsdp)


def widen_mlp_kernel(gate, up, down, out):
    for c, ref in enumerate((gate, up, down)):
        out[c] = ref[...].astype(F32)


def widen_attn_kernel(qkv, o, out):
    n_seq, rows, share = o.shape
    for s in range(n_seq):
        at = pl.ds(s * share, share)
        for c in range(3):
            out[:, c, at] = qkv[s, :, c * share : (c + 1) * share].astype(F32)
        out[:, 3, at] = o[s].astype(F32)


def grid_call(kernel, name, grid, args, in_specs, outs, out_specs, scratch=(), aliases=None):
    return pl.pallas_call(
        kernel,
        grid=grid,
        out_shape=outs,
        in_specs=in_specs,
        out_specs=out_specs,
        scratch_shapes=list(scratch),
        input_output_aliases=aliases or {},
        compiler_params=pltpu.CompilerParams(vmem_limit_bytes=48 * 2**20),
        name=name,
    )(*args)


def angles(positions):
    freqs = ROPE_BASE ** (-jnp.arange(0, HEAD, 2).astype(jnp.float32) / HEAD)
    turn = positions.astype(jnp.float32)[:, None] * freqs[None, :]
    cosine, sine = jnp.cos(turn), jnp.sin(turn)
    return jnp.concatenate([cosine] * 4, 1), jnp.concatenate([-sine, sine] * 2, 1)


def on_device(
    n_seq, n_fsdp,
    hidden_in, gain_attn, attn_weights, gain_mlp, mlp_weights, out_grad, block_slots, doc_ids,
):
    tok, model = hidden_in.shape[1:]
    share = model // n_seq
    block_rows = tok // 2
    within = jnp.arange(block_rows, dtype=jnp.int32)
    slot = block_slots.reshape(-1)
    pos = (slot[:, None] * block_rows + within[None, :]).reshape(-1)
    pick = slot[:, None] == jnp.arange(slot.shape[0], dtype=jnp.int32)[None, :]
    doc = doc_ids[0].reshape(1, -1, block_rows)
    doc = jnp.sum(jnp.where(pick[:, :, None], doc, 0), axis=1).reshape(-1)
    tables = (*angles(pos), pos[:, None], pos[None, :], doc[:, None], doc[None, :])
    start = lax.axis_index("seq") * share
    w_own = lax.dynamic_slice_in_dim(attn_weights, start, share, 2).reshape(-1, 4 * share)
    gains = jnp.concatenate(
        [
            jnp.broadcast_to(gain_attn[None], (16,) + gain_attn.shape),
            jnp.broadcast_to(gain_mlp[None], (16,) + gain_mlp.shape),
        ],
        0,
    )
    mlp_w = mlp_weights.transpose(1, 0, 2)
    a = front(n_seq, n_fsdp, w_own, hidden_in[0], gains, out_grad[0], mlp_w, tables)
    n2_all, grad_all = a.n2_out.reshape(-1, model), a.grad_out.reshape(-1, model)
    w_qkv, w_o = a.w_qkv_out.reshape(model, -1), a.w_o_out.reshape(model, -1)
    grad_down = dot(a.hid, grad_all, TN).astype(BF16)
    grad_gate = dot(a.dg, n2_all, TN).astype(BF16)
    grad_up = dot(a.du, n2_all, TN).astype(BF16)
    dn2_part = (dot(a.dg, mlp_w[0], NN) + dot(a.du, mlp_w[1], NN)).astype(BF16)
    out_part = dot(a.hid, mlp_w[2], NN).astype(BF16)
    b = back_one(
        n_seq, n_fsdp, dn2_part.reshape(n_fsdp, tok, model), a.middle, out_grad[0], a.gain_m,
        w_qkv, w_o, a.o_out, a.n1_out, (a.q, a.k, a.v, a.lse, *tables), (grad_down, grad_gate),
    )
    grad_down, grad_gate = b.g_out
    c = back_two(
        n_seq, n_fsdp, b.dn1_part, b.dw_qkv.reshape(n_fsdp, -1, 3 * share), b.dw_o,
        out_part.reshape(n_fsdp, tok, model), a.middle, hidden_in[0], b.dh1, a.gain_a, b.gain,
        grad_up,
    )
    own_rows, units = b.dw_o.shape[0], grad_up.shape[0]
    step = min(own_rows, 64)
    attn_grad = grid_call(
        widen_attn_kernel,
        "widen_attn",
        (own_rows // step,),
        (c.dw_qkv_all, c.dw_o_all),
        [
            pl.BlockSpec((n_seq, step, 3 * share), lambda i: (0, i, 0)),
            pl.BlockSpec((n_seq, step, share), lambda i: (0, i, 0)),
        ],
        like((own_rows, 4, model), F32),
        pl.BlockSpec((step, 4, model), lambda i: (i, 0, 0)),
    )
    step = min(units, 128)
    mlp_grad = grid_call(
        widen_mlp_kernel,
        "widen_mlp",
        (units // step,),
        (grad_gate, c.g_out, grad_down),
        [pl.BlockSpec((step, model), lambda i: (i, 0))] * 3,
        like((3, units, model), F32),
        pl.BlockSpec((3, step, model), lambda i: (0, i, 0)),
    )
    mlp_grad = mlp_grad.transpose(1, 0, 2)
    return (c.block_out[None], c.grad_in[None], c.gains[0], attn_grad, c.gains[1], mlp_grad)


def solution(mesh):
    return jax.shard_map(
        functools.partial(on_device, mesh.shape["seq"], mesh.shape["fsdp"]),
        mesh=mesh,
        in_specs=(
            P("fsdp", "seq", None),
            P("fsdp"),
            P("fsdp", None, None),
            P("fsdp"),
            P("fsdp", None, None),
            P("fsdp", "seq", None),
            P(),
            P("fsdp", None),
        ),
        out_specs=(
            P("fsdp", "seq", None),
            P("fsdp", "seq", None),
            P("fsdp"),
            P("fsdp", None, None),
            P("fsdp"),
            P("fsdp", None, None),
        ),
        check_vma=False,
    )
```

```python
import functools
import math
import types

import jax
import jax.numpy as jnp
from jax import lax
from jax.experimental import pallas as pl
from jax.experimental.pallas import tpu as pltpu
from jax.sharding import PartitionSpec as P

HEAD = 64


NORM_EPS = 1e-05
ROPE_BASE = 130000.0
MASKED_OUT = -1e30
F32 = jnp.float32
BF16 = jnp.bfloat16
MESH = pl.DeviceIdType.MESH
DMA = pltpu.SemaphoreType.DMA
ANY = pl.BlockSpec(memory_space=pl.ANY)
VMEM = pl.BlockSpec(memory_space=pltpu.VMEM)


def send(src, dst, send_sem, recv_sem, device):
    return pltpu.make_async_remote_copy(
        src_ref=src,
        dst_ref=dst,
        send_sem=send_sem,
        recv_sem=recv_sem,
        device_id=device,
        device_id_type=MESH,
    )


class Place:
    def __init__(self, n_seq, n_fsdp):
        self.n_seq, self.line = n_seq, n_fsdp // 2
        self.s = lax.axis_index("seq")
        self.f = lax.axis_index("fsdp")
        self.r = lax.div(self.f, 2)
        self.c = lax.rem(self.f, 2)
        self.up = (self.s, self.f + 2)
        self.down = (self.s, self.f - 2)
        self.sister = (self.s, 2 * self.r + 1 - self.c)

    def peer(self, d):
        return (jnp.bitwise_xor(self.s, d), self.f)

    def greet(self):
        barrier = pltpu.get_barrier_semaphore()
        wrap = 2 * self.line
        partners = [
            (self.s, lax.rem(self.f + 2, wrap)),
            (self.s, lax.rem(self.f + wrap - 2, wrap)),
            self.sister,
        ]
        partners += [self.peer(d) for d in range(1, self.n_seq)]
        for partner in partners:
            pl.semaphore_signal(barrier, inc=1, device_id=partner, device_id_type=MESH)
        pl.semaphore_wait(barrier, len(partners))


class GatherLine:
    def __init__(self, n_fsdp, parts=1):
        line = n_fsdp // 2
        self.scratch = [DMA((line, parts)) for _ in range(5)] + [DMA((1,))]
        self.parts = parts

    def steps(self, at, x, o, refs, use=None):
        line_r, sis_r, up_s, down_s, sis_s, own_s = refs
        parts, line, r, c = self.parts, at.line, at.r, at.c
        rows = o.shape[1] // parts

        def cut(ref, k):
            return ref.at[pl.ds(k * rows, rows)]

        def go_up(src, b, k):
            return send(src, cut(o.at[2 * b + c], k), up_s.at[b, k], line_r.at[b, k], at.up)

        def go_down(src, b, k):
            return send(src, cut(o.at[2 * b + c], k), down_s.at[b, k], line_r.at[b, k], at.down)

        def go_sister(src, b, k):
            return send(src, cut(o.at[2 * b + c], k), sis_s.at[b, k], sis_r.at[b, k], at.sister)

        def complete(b):
            for k in range(parts):
                src = cut(o.at[2 * b + 1 - c], k)
                send(src, src, sis_s.at[b, k], sis_r.at[b, k], at.sister).wait_recv()
            if use is not None:
                use(b)

        own = pltpu.make_async_copy(x, o.at[at.f], own_s.at[0])
        own.start()
        for k in range(parts):
            src = cut(x, k)
            pl.when(r < line - 1)(lambda: go_up(src, r, k).start())
            pl.when(r > 0)(lambda: go_down(src, r, k).start())
            go_sister(src, r, k).start()
        yield
        for t in range(1, line):
            for k in range(parts):
                low, high = r - t, r + t

                @pl.when(low >= 0)
                def _():
                    src = cut(o.at[2 * low + c], k)
                    go_up(src, low, k).wait_recv()
                    pl.when(r < line - 1)(lambda: go_up(src, low, k).start())
                    go_sister(src, low, k).start()

                @pl.when(high < line)
                def _():
                    src = cut(o.at[2 * high + c], k)
                    go_down(src, high, k).wait_recv()
                    pl.when(r > 0)(lambda: go_down(src, high, k).start())
                    go_sister(src, high, k).start()

            yield
            if t == 1:
                own.wait()
                complete(r)
            else:
                pl.when(r - t + 1 >= 0)(lambda: complete(r - t + 1))
                pl.when(r + t - 1 < line)(lambda: complete(r + t - 1))
        pl.when(r - line + 1 >= 0)(lambda: complete(r - line + 1))
        pl.when(r + line - 1 < line)(lambda: complete(r + line - 1))
        yield
        for b in range(line):
            for k in range(parts):
                src = cut(x, k)
                go_sister(src, b, k).wait_send()
                pl.when((b <= r) & (r < line - 1))(lambda: go_up(src, b, k).wait_send())
                pl.when((b >= r) & (r > 0))(lambda: go_down(src, b, k).wait_send())


class ScatterLine:
    def __init__(self, part, n_fsdp, parts=1, far=False):
        line = n_fsdp // 2
        block = part.shape[1:]
        self.scratch = [
            pltpu.VMEM((line,) + block, part.dtype),
            pltpu.VMEM((line + 1,) + block, part.dtype),
        ]
        self.scratch += [DMA((line, parts)), DMA((line, parts)), DMA((line, parts))]
        self.scratch += [DMA((line + 1, parts))]
        if far:
            self.scratch += [pltpu.VMEM((line,) + block, part.dtype), DMA((line,))]
        self.parts, self.far = parts, far

    def steps(self, at, refs):
        part, o, sis, come, sis_s, sis_r, line_s, line_r = refs[:8]
        near, near_s = refs[8:] if self.far else (None, None)
        parts, line, r, c = self.parts, at.line, at.r, at.c
        rows = part.shape[1] // parts
        tile = 16 if rows % 16 == 0 else rows

        def cut(ref, k):
            return ref.at[pl.ds(k * rows, rows)]

        def to_sister(b, k):
            return send(
                cut(part.at[2 * b + 1 - c], k),
                cut(sis.at[b], k),
                sis_s.at[b, k],
                sis_r.at[b, k],
                at.sister,
            )

        def slot(b, own):
            return jnp.where(b == own, line, b)

        def go_up(b, k):
            return send(cut(sis.at[b], k), cut(come.at[b], k), line_s.at[b, k], line_r.at[b, k], at.up)

        def go_down(b, k, own):
            i = slot(b, own)
            return send(
                cut(sis.at[b], k), cut(come.at[i], k), line_s.at[b, k], line_r.at[i, k], at.down
            )

        def add(b, k, came, out=None):
            def body(i, carry):
                at_rows = pl.ds(k * rows + i * tile, tile)
                own = near[b, at_rows] if self.far else part[2 * b + c, at_rows]
                total = own.astype(F32) + sis[b, at_rows].astype(F32)
                for j in came:
                    total = total + come[j, at_rows].astype(F32)
                if out is None:
                    sis[b, at_rows] = total.astype(sis.dtype)
                else:
                    out[at_rows] = total.astype(out.dtype)
                return carry

            lax.fori_loop(0, rows // tile, body, 0)

        order = []
        for j in range(line):
            order += [b for b in (line - 1 - j, j) if b not in order]
        for b in order:
            for k in range(parts):
                to_sister(b, k).start()
        if self.far:
            loads = [
                pltpu.make_async_copy(part.at[2 * b + c], near.at[b], near_s.at[b])
                for b in range(line)
            ]
            for one in loads:
                one.start()
            for one in loads:
                one.wait()
        yield
        for j in range(line - 1):
            for k in range(parts):
                b = line - 1 - j

                @pl.when(b > r)
                def _():
                    to_sister(b, k).wait_recv()

                    @pl.when(r > 0)
                    def _():
                        go_up(b, k).wait_recv()
                        add(b, k, [b])

                    pl.when(r == 0)(lambda: add(b, k, []))
                    go_up(b, k).start()

                @pl.when(j < r)
                def _():
                    to_sister(j, k).wait_recv()

                    @pl.when(r < line - 1)
                    def _():
                        go_down(j, k, -1).wait_recv()
                        add(j, k, [j])

                    pl.when(r == line - 1)(lambda: add(j, k, []))
                    go_down(j, k, r - 1).start()

            yield
        for k in range(parts):
            to_sister(r, k).wait_recv()
            pl.when(r > 0)(lambda: go_up(r, k).wait_recv())
            pl.when(r < line - 1)(lambda: go_down(r, k, r).wait_recv())
            pl.when(r == 0)(lambda: add(r, k, [line], o))
            pl.when(r == line - 1)(lambda: add(r, k, [r], o))
            pl.when((r > 0) & (r < line - 1))(lambda: add(r, k, [r, line], o))
        yield
        for b in range(line):
            for k in range(parts):
                to_sister(b, k).wait_send()
                pl.when(b != r)(lambda: go_up(b, k).wait_send())


class GatherSeq:
    def __init__(self, n_seq):
        self.scratch = [DMA((n_seq,)), DMA((n_seq,))]

    def steps(self, at, refs):
        x, o, s_sem, r_sem = refs

        def go(d):
            return send(x, o.at[at.s], s_sem.at[d], r_sem.at[d], at.peer(d))

        for d in reversed(range(1, at.n_seq)):
            go(d).start()
        own = pltpu.make_async_copy(x, o.at[at.s], s_sem.at[0])
        own.start()
        yield
        own.wait()
        for d in range(1, at.n_seq):
            go(d).wait()


class HalveSeq:
    def __init__(self, shape, dtype, n_seq):
        n, rows, cols = shape
        bits = n_seq.bit_length() - 1
        self.half = rows // 2
        self.orders = [[(i + p) % bits for i in range(bits)] for p in range(2)]
        self.scratch = [
            pltpu.VMEM((2, n - 1, self.half, cols), dtype), DMA((2, n - 1)), DMA((2, n - 1))
        ]

    def masks(self, p, i):
        out = [0]
        for b in self.orders[p][i + 1 :]:
            out += [m | (1 << b) for m in out]
        return out

    def slot(self, p, i, u):
        return sum(len(self.masks(p, j)) for j in range(i)) + self.masks(p, i).index(u)

    def steps(self, at, part, o, refs):
        land, s_sem, r_sem = refs
        half, bits = self.half, len(self.orders[0])
        tile = 16 if half % 16 == 0 else half

        def go(p, i, u):
            b = 1 << self.orders[p][i]
            if i == 0:
                src = part.at[b | u, pl.ds(p * half, half)]
            else:
                src = land.at[p, self.slot(p, 0, b | u)]
            n = self.slot(p, i, u)
            return send(src, land.at[p, n], s_sem.at[p, n], r_sem.at[p, n], at.peer(b))

        def add(p, u, upto, out, first):
            def body(k, carry):
                rows = pl.ds(pl.multiple_of(k * tile, tile), tile)
                total = part[u, pl.ds(pl.multiple_of(p * half + k * tile, tile), tile)].astype(F32)
                for i in range(upto):
                    total = total + land[p, self.slot(p, i, u), rows].astype(F32)
                out[pl.ds(pl.multiple_of(first + k * tile, tile), tile)] = total.astype(out.dtype)
                return carry

            lax.fori_loop(0, half // tile, body, 0)

        for p in range(2):
            for u in self.masks(p, 0):
                go(p, 0, u).start()
        yield
        for i in range(bits):
            for p in range(2):
                for u in self.masks(p, i):
                    go(p, i, u).wait_recv()
                if i + 1 < bits:
                    b = 1 << self.orders[p][i + 1]
                    for u in self.masks(p, i + 1):
                        add(p, b | u, i + 1, land.at[p, self.slot(p, 0, b | u)], 0)
                        go(p, i + 1, u).start()
                else:
                    add(p, 0, bits, o, p * half)
            yield
        for p in range(2):
            for i in range(bits):
                for u in self.masks(p, i):
                    go(p, i, u).wait_send()


class ReduceSeq:
    def __init__(self, shape, dtype, n_seq, parts=4):
        rows, cols = shape
        self.bits, self.parts = n_seq.bit_length() - 1, parts
        self.rows = rows // parts
        self.room = self.rows - (self.rows >> self.bits)
        self.scratch = [
            pltpu.VMEM(shape, dtype),
            pltpu.VMEM((parts * self.room, cols), dtype),
            DMA((parts,)),
            DMA((parts, self.bits)),
            DMA((parts, self.bits)),
            DMA((parts, n_seq)),
            DMA((parts, n_seq)),
            DMA((parts,)),
        ]

    def steps(self, at, refs, fill=None):
        g_in, o, g, land, load_s, rs_s, rs_r, ag_s, ag_r, own_s = refs
        bits, parts = self.bits, range(self.parts)
        orders = [[(i + p) % bits for i in range(bits)] for p in parts]
        mult = self.rows >> bits

        def bit(t, b):
            return jnp.bitwise_and(lax.shift_right_logical(t, b), 1)

        def base(p, t, n):
            low = p * self.rows
            for i in range(n):
                low = low + bit(t, orders[p][i]) * (self.rows >> (i + 1))
            return pl.multiple_of(low, mult)

        def load(p):
            part = pl.ds(p * self.rows, self.rows)
            return pltpu.make_async_copy(g_in.at[part], g.at[part], load_s.at[p])

        def slot(p, i):
            return p * self.room + sum(self.rows >> (j + 1) for j in range(i))

        def halve(p, i):
            size = self.rows >> (i + 1)
            other = jnp.bitwise_xor(at.s, 1 << orders[p][i])
            return send(
                g.at[pl.ds(base(p, other, i + 1), size)],
                land.at[pl.ds(slot(p, i), size)],
                rs_s.at[p, i],
                rs_r.at[p, i],
                (other, at.f),
            )

        def add(p, i):
            size = self.rows >> (i + 1)
            low, first = base(p, at.s, i + 1), slot(p, i)

            def body(j, carry):
                mine = pl.ds(pl.multiple_of(low + j * 16, 16), 16)
                came = pl.ds(pl.multiple_of(first + j * 16, 16), 16)
                total = g[mine].astype(F32) + land[came].astype(F32)
                g[mine] = total.astype(g.dtype)
                return carry

            lax.fori_loop(0, size // 16, body, 0)

        def masks(p, j):
            out = [0]
            for i in range(j):
                out += [m | (1 << orders[p][bits - 1 - i]) for m in out]
            return out

        def double(p, j, mask):
            b = orders[p][bits - 1 - j]
            piece = pl.ds(base(p, jnp.bitwise_xor(at.s, mask), bits), mult)
            src = g.at[piece] if mask == 0 else o.at[piece]
            i = (1 << b) | mask
            return send(
                src, o.at[piece], ag_s.at[p, i], ag_r.at[p, i], (jnp.bitwise_xor(at.s, 1 << b), at.f)
            )

        def arrive(p, j, mask):
            b = orders[p][bits - 1 - j]
            piece = pl.ds(base(p, jnp.bitwise_xor(at.s, (1 << b) | mask), bits), mult)
            i = (1 << b) | mask
            return send(
                o.at[piece], o.at[piece], ag_s.at[p, i], ag_r.at[p, i],
                (jnp.bitwise_xor(at.s, 1 << b), at.f),
            )

        def own(p):
            piece = pl.ds(base(p, at.s, bits), mult)
            return pltpu.make_async_copy(g.at[piece], o.at[piece], own_s.at[p])

        if g_in is not None:
            for p in parts:
                load(p).start()
        for p in parts:
            if g_in is not None:
                load(p).wait()
            if fill is not None:
                fill(p * self.rows, self.rows)
            halve(p, 0).start()
        yield
        for i in range(bits):
            for p in parts:
                halve(p, i).wait_recv()
                add(p, i)
                if i + 1 < bits:
                    halve(p, i + 1).start()
                else:
                    for j in range(bits):
                        double(p, j, 0).start()
                    own(p).start()
                yield
        for j in range(bits):
            for p in parts:
                for mask in masks(p, j):
                    arrive(p, j, mask).wait_recv()
                    came = (1 << orders[p][bits - 1 - j]) | mask
                    for later in range(j + 1, bits):
                        double(p, later, came).start()
                yield
        for p in parts:
            own(p).wait()
            for i in range(bits):
                halve(p, i).wait_send()
            for j in range(bits):
                for mask in masks(p, j):
                    double(p, j, mask).wait_send()


class SpreadSeq:
    def __init__(self, n_seq):
        self.bits = n_seq.bit_length() - 1
        self.scratch = [DMA((2, n_seq)), DMA((2, n_seq)), DMA((1,))]

    def steps(self, at, refs):
        x, o, s_sem, r_sem, own_s = refs
        bits, half = self.bits, x.shape[0] // 2
        orders = [[(i + p) % bits for i in range(bits)] for p in range(2)]

        def known(p, j):
            out = [0]
            for i in range(j):
                out += [m | (1 << orders[p][i]) for m in out]
            return out

        def piece(p, mask):
            return o.at[jnp.bitwise_xor(at.s, mask), pl.ds(p * half, half)]

        def go(p, j, mask):
            b = 1 << orders[p][j]
            src = x.at[pl.ds(p * half, half)] if mask == 0 else piece(p, mask)
            i = b | mask
            return send(src, piece(p, mask), s_sem.at[p, i], r_sem.at[p, i], at.peer(b))

        def arrive(p, j, mask):
            b = 1 << orders[p][j]
            i = b | mask
            here = piece(p, i)
            return send(here, here, s_sem.at[p, i], r_sem.at[p, i], at.peer(b))

        for p in range(2):
            for j in range(bits):
                go(p, j, 0).start()
        own = pltpu.make_async_copy(x, o.at[at.s], own_s.at[0])
        own.start()
        yield
        for j in range(bits):
            for p in range(2):
                for mask in known(p, j):
                    arrive(p, j, mask).wait_recv()
                    for later in range(j + 1, bits):
                        go(p, later, (1 << orders[p][j]) | mask).start()
            yield
        own.wait()
        for j in range(bits):
            for p in range(2):
                for mask in known(p, j):
                    go(p, j, mask).wait_send()


def interleave(order, running):
    for name in order:
        if name in running and next(running[name], END) is END:
            del running[name]
    while running:
        for name in list(running):
            if next(running[name], END) is END:
                del running[name]


END = object()


class Rooms:
    def __init__(self):
        self.args, self.in_specs, self.outs, self.out_specs, self.scratch = [], [], [], [], []
        self.names = ([], [], [])

    def note(self, group, name, x):
        many = isinstance(x, (list, tuple))
        self.names[group].append((name, len(x) if many else None))
        return list(x) if many else [x]

    def take(self, spec, **arrays):
        for name, x in arrays.items():
            new = self.note(0, name, x)
            self.args += new
            self.in_specs += [spec] * len(new)

    def give(self, spec, **shapes):
        for name, x in shapes.items():
            new = self.note(1, name, x)
            self.outs += new
            self.out_specs += [spec] * len(new)

    def keep(self, **kinds):
        for name, x in kinds.items():
            self.scratch += self.note(2, name, x)

    def bind(self, refs, groups):
        table, refs = types.SimpleNamespace(), list(refs)
        for group in groups:
            for name, many in self.names[group]:
                count = 1 if many is None else many
                mine, refs = refs[:count], refs[count:]
                setattr(table, name, mine[0] if many is None else mine)
        return table

    def run(self, body, name, collective_id, n_seq, n_fsdp):
        def kernel(*refs):
            at = Place(n_seq, n_fsdp)
            at.greet()
            body(at, self.bind(refs, (0, 1, 2)))

        out = pl.pallas_call(
            kernel,
            out_shape=self.outs,
            in_specs=self.in_specs,
            out_specs=self.out_specs,
            scratch_shapes=self.scratch,
            compiler_params=pltpu.CompilerParams(
                collective_id=collective_id, has_side_effects=True, vmem_limit_bytes=62 * 2**20
            ),
            name=name,
        )(*self.args)
        return self.bind(out, (1,))


def like(shape, dtype=BF16):
    return jax.ShapeDtypeStruct(tuple(shape), dtype)


def room(*shape, dtype=BF16):
    return pltpu.VMEM(shape, dtype)


def dot(a, b, dims):
    return lax.dot_general(a, b, (dims, ((), ())), preferred_element_type=F32)


NN = ((1,), (0,))
NT = ((1,), (1,))
TN = ((0,), (0,))


def turned(x, cos, sin):
    lane = lax.broadcasted_iota(jnp.int32, x.shape, 1)
    other = jnp.where(lane % HEAD < HEAD // 2, pltpu.roll(x, 96, 1), pltpu.roll(x, 32, 1))
    return x * cos + other * sin


def head_masks():
    lane = lax.broadcasted_iota(jnp.int32, (1, 128), 1)
    first = (lane < HEAD).astype(F32)
    return first, 1.0 - first


def back_pair(pair, do, q, k, v, lse, cos, sin, dqkv, masking, dk, dv):
    pos_col, pos_row, doc_col, doc_row = masking
    length, share = q.shape
    span = 256
    masks = head_masks()
    lane = lax.broadcasted_iota(jnp.int32, (span, 128), 1)
    lanes = slice(pair * 128, pair * 128 + 128)
    dk[...] = jnp.zeros_like(dk)
    dv[...] = jnp.zeros_like(dv)

    def one_span(i, carry):
        rows = pl.ds(pl.multiple_of(i * span, span), span)
        allowed = (pos_row[...] <= pos_col[rows]) & (doc_row[...] == doc_col[rows])
        bias = jnp.where(allowed, 0.0, MASKED_OUT)
        dq = jnp.zeros((span, 128), F32)
        for h in range(2):
            mask = masks[h].astype(BF16)
            field, grad = q[rows, lanes] * mask, do[rows, lanes] * mask
            log_total = jnp.sum(
                jnp.where(lane == 2 * pair + h, lse[rows], 0.0), axis=-1, keepdims=True
            )
            z = dot(field, k[:, lanes], NT) * 0.125 + bias
            prob = jnp.exp(z - log_total)
            dp = dot(grad, v[:, lanes], NT)
            delta = jnp.sum(prob * dp, axis=-1, keepdims=True)
            dz = (prob * (dp - delta)).astype(BF16)
            dq = dq + dot(dz, k[:, lanes], NN) * masks[h]
            dk[...] += dot(dz, field, TN)
            dv[...] += dot(prob.astype(BF16), grad, TN)
        dqkv[rows, lanes] = turned(dq * 0.125, cos[rows], -sin[rows]).astype(BF16)
        return carry

    lax.fori_loop(0, length // span, one_span, 0)
    at = share + pair * 128
    dqkv[:, at : at + 128] = turned(dk[...] * 0.125, cos[...], -sin[...]).astype(BF16)
    at = 2 * share + pair * 128
    dqkv[:, at : at + 128] = dv[...].astype(BF16)


def norm_back(grad_normed, value, scale, gain):
    weighted = grad_normed * gain
    inner_mean = jnp.mean(weighted * value, axis=-1, keepdims=True)
    return scale * (weighted - value * scale * scale * inner_mean)


def scale_of(value):
    return lax.rsqrt(jnp.mean(value * value, axis=-1, keepdims=True) + NORM_EPS)


def fill_tables(slots, docs, r):
    length = docs.shape[1]
    block = length // (2 * slots.shape[0])

    def place(shape, axis):
        i = lax.broadcasted_iota(jnp.int32, shape, axis)
        slot = jnp.zeros(shape, jnp.int32)
        for j in range(2 * slots.shape[0]):
            slot = jnp.where(i // block == j, slots[j // 2, j % 2], slot)
        return slot * block + i % block

    r.pos_col[...] = place((length, 1), 0)
    r.pos_row[...] = place((1, length), 1)
    lane = lax.broadcasted_iota(jnp.int32, (1, 128), 1)
    half = HEAD // 2
    steps = (lane % half).astype(F32) / half
    freqs = jnp.exp(steps * -math.log(ROPE_BASE))
    sign = jnp.where(lane % HEAD < half, -1.0, 1.0)
    r.doc_row[...] = jnp.zeros((1, length), jnp.int32)

    def body(i, carry):
        rows = pl.ds(pl.multiple_of(i * 128, 128), 128)
        pos = r.pos_col[rows]
        turn = pos.astype(F32) * freqs
        r.cos[rows] = jnp.cos(turn)
        r.sin[rows] = jnp.sin(turn) * sign
        at = lax.broadcasted_iota(jnp.int32, (128, length), 1)
        own = jnp.sum(jnp.where(at == pos, docs[...], 0), axis=1, keepdims=True)
        r.doc_col[rows] = own
        here = lax.broadcasted_iota(jnp.int32, (128, length), 0) + i * 128
        r.doc_row[...] += jnp.sum(jnp.where(at == here, own, 0), axis=0, keepdims=True)
        return carry

    lax.fori_loop(0, length // 128, body, 0)


FRONT_ORDER = [0, 0, 0, 1, 0, 0, 1, 0, 1, 0, 1, 0, 1, 1, 2, 0, 0, 2, 0, 0, 0, 0, 2, 0, 2, 0]


def front(n_seq, n_fsdp, w_own, hidden, own_gains, out_grad, mlp_w, slots, docs):
    tok, model = hidden.shape
    length, share = n_seq * tok, w_own.shape[1] // 4
    line, rows_f, units = n_fsdp // 2, w_own.shape[0], mlp_w.shape[1]
    qkv_shape, o_shape = (n_fsdp, rows_f, 3 * share), (n_fsdp, rows_f, share)
    per = n_fsdp // n_seq
    n_pairs = share // 128
    span = 256
    get_w, get_o = GatherLine(n_fsdp, 2), GatherLine(n_fsdp)
    get_gain, get_grad, get_n2 = GatherLine(n_fsdp), GatherLine(n_fsdp, 2), GatherLine(n_fsdp, 2)
    get_x = GatherSeq(n_seq)
    rooms = Rooms()
    rooms.take(VMEM, hidden=hidden, own_gains=own_gains, docs=docs)
    rooms.take(pl.BlockSpec(memory_space=pltpu.SMEM), slots=slots)
    rooms.take(ANY, w_own=w_own, out_grad=out_grad, mlp_w=mlp_w)
    rooms.give(
        ANY,
        w_qkv_out=like(qkv_shape),
        w_o_out=like(o_shape),
        n1_out=like((n_seq, length, share)),
        o_out=like((n_seq, length, share)),
        n2_out=like((n_fsdp, tok, model)),
        grad_out=like((n_fsdp, tok, model)),
        hid=like((n_fsdp * tok, units)),
        dg=like((n_fsdp * tok, units)),
        du=like((n_fsdp * tok, units)),
    )
    rooms.give(
        VMEM,
        q=like((length, share)),
        k=like((length, share)),
        v=like((length, share)),
        lse=like((length, 128), F32),
        middle=like((tok, model), F32),
        gain_a=like((1, model), F32),
        gain_m=like((1, model), F32),
        cos=like((length, 128), F32),
        sin=like((length, 128), F32),
        pos_col=like((length, 1), jnp.int32),
        pos_row=like((1, length), jnp.int32),
        doc_col=like((length, 1), jnp.int32),
        doc_row=like((1, length), jnp.int32),
    )
    rooms.keep(
        gains=room(32, rows_f),
        get_w=get_w.scratch, get_o=get_o.scratch, get_gain=get_gain.scratch,
        get_grad=get_grad.scratch, get_n2=get_n2.scratch, get_x=get_x.scratch,
        w_qkv_all=room(*qkv_shape),
        w_o_all=room(*o_shape),
        gains_all=room(n_fsdp, 32, rows_f),
        x_all=room(n_seq, tok, model),
        n1=room(n_fsdp, length, rows_f),
        o_all=room(n_seq, length, share),
        y_total=room(length, share, dtype=F32),
        y=room(n_seq, tok, share),
        y_land=room(n_seq, tok, share),
        n2=room(tok, model),
        n2_all=room(n_fsdp, tok, model),
        grad_all=room(n_fsdp, tok, model),
        w_gate=room(units, model),
        w_up=room(units, model),
        w_down=room(units, model),
        act=room(n_fsdp * tok, units, dtype=F32),
        stage=room(line, 3, 2 * tok, units),
        load=DMA((3,)),
        save=DMA((6 + n_fsdp,)),
        stage_s=DMA((line, 3)),
        o_s=DMA((n_pairs, n_seq)),
        o_r=DMA((n_pairs, n_seq)),
        y_s=DMA((n_seq,)),
        y_r=DMA((n_seq,)),
    )

    def body(at, r):
        loads = [
            pltpu.make_async_copy(r.mlp_w.at[i], w, r.load.at[i])
            for i, w in enumerate((r.w_gate, r.w_up, r.w_down))
        ]
        saves = []
        w_qkv, w_o = r.w_own.at[:, pl.ds(0, 3 * share)], r.w_own.at[:, pl.ds(3 * share, share)]

        def save(src, dst):
            saves.append(pltpu.make_async_copy(src, dst, r.save.at[len(saves)]))
            saves[-1].start()

        def total(c, rows, cols):
            low, left = (c // 2) * length, (c % 2) * share
            return (
                slice(low + rows.start, low + rows.stop), slice(left + cols.start, left + cols.stop)
            )

        def project(b):
            for f in (2 * b, 2 * b + 1):
                for c in range(3):
                    weights = r.w_qkv_all[f, :, c * share : (c + 1) * share]
                    for i in range(0, length, span):
                        part = dot(r.n1[f, i : i + span], weights, NN)
                        r.act[total(c, slice(i, i + span), slice(0, share))] += part

        def grad_of(b):
            rows = pl.ds(pl.multiple_of(2 * tok * b, 2 * tok), 2 * tok)
            grad = r.grad_all[pl.ds(2 * b, 2)].reshape(2 * tok, model)
            r.act[rows] = dot(grad, r.w_down[...], NT)

        def stored(b, k):
            rows = pl.ds(pl.multiple_of(2 * tok * b, 2 * tok), 2 * tok)
            return pltpu.make_async_copy(
                r.stage.at[b, k], (r.hid, r.dg, r.du)[k].at[rows], r.stage_s.at[b, k]
            )

        def activate(b):
            rows = pl.ds(pl.multiple_of(2 * tok * b, 2 * tok), 2 * tok)
            n2 = r.n2_all[pl.ds(2 * b, 2)].reshape(2 * tok, model)
            gate = dot(n2, r.w_gate[...], NT)
            up = dot(n2, r.w_up[...], NT)
            grad = r.act[rows]
            sigma = jax.nn.sigmoid(gate)
            silu = gate * sigma
            r.stage[b, 0] = (silu * up).astype(BF16)
            r.stage[b, 1] = (grad * up * sigma * (1.0 + gate * (1.0 - sigma))).astype(BF16)
            r.stage[b, 2] = (grad * silu).astype(BF16)
            for k in range(3):
                stored(b, k).start()

        def attend(pair):
            lanes = slice(pair * 128, pair * 128 + 128)
            masks = head_masks()
            lane = lax.broadcasted_iota(jnp.int32, (span, 128), 1)

            def one_span(i, carry):
                rows = pl.ds(pl.multiple_of(i * span, span), span)
                allowed = (r.pos_row[...] <= r.pos_col[rows]) & (r.doc_row[...] == r.doc_col[rows])
                bias = jnp.where(allowed, 0.0, MASKED_OUT)
                parts = []
                for h in range(2):
                    field = r.q[rows, lanes] * masks[h].astype(BF16)
                    z = dot(field, r.k[:, lanes], NT) * 0.125 + bias
                    top = jnp.max(z, axis=-1, keepdims=True)
                    e = jnp.exp(z - top)
                    sum_e = jnp.sum(e, axis=-1, keepdims=True)
                    prob = (e * (1.0 / sum_e)).astype(BF16)
                    parts.append(dot(prob, r.v[:, lanes], NN) * masks[h])
                    here = lane == 2 * pair + h
                    r.lse[rows] = jnp.where(here, top + jnp.log(sum_e), r.lse[rows])
                r.o_all[at.s, rows, lanes] = (parts[0] + parts[1]).astype(BF16)
                return carry

            lax.fori_loop(0, length // span, one_span, 0)

        def go_o(pair, d, owner):
            here = r.o_all.at[owner, :, pl.ds(pair * 128, 128)]
            return send(here, here, r.o_s.at[pair, d], r.o_r.at[pair, d], at.peer(d))

        def go_y(d):
            peer = at.peer(d)
            return send(r.y.at[peer[0]], r.y_land.at[d], r.y_s.at[d], r.y_r.at[d], peer)

        def chain():
            weights = get_w.steps(at, w_qkv, r.w_qkv_all, r.get_w, project)
            next(weights)
            rows_in = get_x.steps(at, [r.hidden, r.x_all] + r.get_x)
            next(rows_in)
            for one in loads:
                one.start()
            r.act[...] = jnp.zeros_like(r.act)
            for i, gain in enumerate(r.own_gains):
                r.gains[16 * i : 16 * i + 16] = jnp.broadcast_to(gain[...], (16, rows_f))
            gain_steps = get_gain.steps(at, r.gains, r.gains_all, r.get_gain)
            next(gain_steps)
            fill_tables(r.slots, r.docs, r)
            for _ in gain_steps:
                pass
            for f in range(n_fsdp):
                cols = slice(f * rows_f, (f + 1) * rows_f)
                r.gain_a[:, cols] = r.gains_all[f, 0:1].astype(F32)
                r.gain_m[:, cols] = r.gains_all[f, 16:17].astype(F32)
            next(weights)
            for _ in rows_in:
                pass
            r.lse[...] = jnp.zeros_like(r.lse)

            def norm(i, carry):
                j, k = i // (tok // 16), i % (tok // 16)
                x = r.x_all[j, pl.ds(pl.multiple_of(k * 16, 16), 16)].astype(F32)
                normed = (x * scale_of(x) * r.gain_a[...]).astype(BF16)
                rows = pl.ds(pl.multiple_of(i * 16, 16), 16)
                for f in range(n_fsdp):
                    r.n1[f, rows] = normed[:, f * rows_f : (f + 1) * rows_f]
                return carry

            lax.fori_loop(0, length // 16, norm, 0)
            for f in range(n_fsdp):
                save(r.n1.at[f], r.n1_out.at[f // per, :, pl.ds((f % per) * rows_f, rows_f)])
            yield
            for _ in weights:
                yield
            save(r.w_qkv_all, r.w_qkv_out)
            for c, out in enumerate((r.q, r.k)):
                for j in range(0, share, 128):
                    field = r.act[total(c, slice(0, length), slice(j, j + 128))]
                    out[:, j : j + 128] = turned(field, r.cos[...], r.sin[...]).astype(BF16)
            r.v[...] = r.act[total(2, slice(0, length), slice(0, share))].astype(BF16)
            projected.append(True)
            yield
            for pair in range(n_pairs):
                attend(pair)
                for d in reversed(range(1, n_seq)):
                    go_o(pair, d, at.s).start()
                yield
            for _ in out_weights:
                pass
            for d in range(n_seq):
                owner = at.peer(d)[0]
                if d:
                    for pair in range(n_pairs):
                        go_o(pair, d, owner).wait_recv()
                for h in range(per):
                    part = dot(
                        r.o_all[owner, :, h * rows_f : (h + 1) * rows_f],
                        r.w_o_all[owner * per + h],
                        NN,
                    )
                    if d == 0 and h == 0:
                        r.y_total[...] = part
                    else:
                        r.y_total[...] += part
                yield
            for j in range(n_seq):
                r.y[j] = r.y_total[j * tok : (j + 1) * tok].astype(BF16)
            for d in reversed(range(1, n_seq)):
                go_y(d).start()
            save(r.o_all, r.o_out)
            save(r.w_o_all, r.w_o_out)
            r.y_land[0] = r.y[at.s]
            yield
            for d in range(1, n_seq):
                go_y(d).wait()

            def middle(i, carry):
                rows = pl.ds(pl.multiple_of(i * 16, 16), 16)
                for j in range(n_seq):
                    cols = slice(j * share, (j + 1) * share)
                    branch = r.y_land[jnp.bitwise_xor(at.s, j), rows].astype(F32)
                    r.middle[rows, cols] = r.hidden[rows, cols].astype(F32) + branch
                h = r.middle[rows]
                r.n2[rows] = (h * scale_of(h) * r.gain_m[...]).astype(BF16)
                return carry

            lax.fori_loop(0, tok // 16, middle, 0)
            yield
            tokens = get_n2.steps(at, r.n2, r.n2_all, r.get_n2, activate)
            next(tokens)
            yield
            next(tokens)
            for _ in grads:
                pass
            for one in loads[:2]:
                one.wait()
            for _ in tokens:
                yield

        def cotangents():
            blocks = get_grad.steps(at, r.out_grad, r.grad_all, r.get_grad, grad_of)
            next(blocks)
            yield
            next(blocks)
            yield
            while not projected:
                yield
            loads[2].wait()
            for _ in blocks:
                yield
            save(r.grad_all, r.grad_out)

        projected = []
        out_weights = get_o.steps(at, w_o, r.w_o_all, r.get_o)
        grads = cotangents()
        interleave(FRONT_ORDER, {0: chain(), 1: out_weights, 2: grads})
        for pair in range(n_pairs):
            for d in range(1, n_seq):
                go_o(pair, d, at.s).wait_send()
        save(r.n2_all, r.n2_out)
        for b in range(line):
            for k in range(3):
                stored(b, k).wait()
        for one in saves:
            one.wait()

    return rooms.run(body, "front", 1, n_seq, n_fsdp)


MIDDLE_ORDER = [0, 0, 1, 1, 2, 2, 2, 2, 0, 1, 1, 2, 2, 0, 1, 1, 2, 2, 0, 1, 1, 0, 1, 1]


def middle(n_seq, n_fsdp, hid, dg, du, n2_all, grad_all, mlp_w, h1, out_grad, gain_m):
    tok, model = h1.shape
    tokens, units = hid.shape
    share, length, line = model // n_seq, n_seq * tok, n_fsdp // 2
    step = min(256, units)
    rooms = Rooms()
    rooms.take(VMEM, h1=h1, out_grad=out_grad, gain_m=gain_m)
    rooms.take(ANY, far=[hid, grad_all, dg, du, n2_all], mlp_w=mlp_w)
    rooms.give(
        ANY,
        grad_down=like((units, model)),
        grads=[like((units, model))] * 2,
        out_part=like((n_fsdp, tok, model)),
    )
    rooms.give(
        VMEM, dh1=like((tok, model), F32), gain=like((8, model), F32), da_cols=like((length, share))
    )
    scatter = ScatterLine(like((n_fsdp, tok, model)), n_fsdp, 2)
    reduce = ReduceSeq((units, model), BF16, n_seq)
    rooms.keep(
        scatter=scatter.scratch,
        reduce=reduce.scratch,
        near=[room(*x.shape) for x in (hid, grad_all, dg, du, n2_all)],
        weights=[room(units, model)] * 3,
        dn2_part=room(n_fsdp, tok, model),
        dn2=room(tok, model, dtype=F32),
        da=room(tok, model),
        stage=room(2, 2 * tok, model),
        load=DMA((8,)),
        stage_s=DMA((2,)),
        swap=[DMA((n_seq,)), DMA((n_seq,))],
    )

    def body(at, r):
        hid, grad_all, dg, du, n2_all = r.near
        gate_w, up_w, down_w = r.weights
        loads = [
            pltpu.make_async_copy(a, b, r.load.at[i])
            for i, (a, b) in enumerate(
                list(zip(r.far, r.near)) + [(r.mlp_w.at[i], w) for i, w in enumerate(r.weights)]
            )
        ]

        def ready(*which):
            for i in which:
                loads[i].wait()

        def to_grad(act, rows_in, i):
            return dot(act[:, i : i + step], rows_in[...].reshape(tokens, model), TN).astype(BF16)

        def chain():
            for i in (0, 1, 2, 3, 5, 6, 4, 7):
                loads[i].start()
            ready(0, 1)
            next(down)
            yield
            ready(2, 3, 5, 6)
            for b in range(line):
                rows = slice(2 * tok * b, 2 * tok * (b + 1))
                part = dot(dg[rows], gate_w[...], NN) + dot(du[rows], up_w[...], NN)
                r.dn2_part[2 * b : 2 * b + 2] = part.astype(BF16).reshape(2, tok, model)
            yield from scatter.steps(at, [r.dn2_part, r.dn2] + r.scatter)
            h1, out_grad, gain_m = r.h1, r.out_grad, r.gain_m
            dn2, dh1, da, gain = r.dn2, r.dh1, r.da, r.gain
            gain[...] = jnp.zeros_like(gain)

            def norm(i, carry):
                rows = pl.ds(i * 16, 16)
                h, grad = h1[rows], dn2[rows]
                scale = lax.rsqrt(jnp.mean(h * h, axis=-1, keepdims=True) + NORM_EPS)
                wide = out_grad[rows].astype(F32) + norm_back(grad, h, scale, gain_m[...])
                dh1[rows] = wide
                da[rows] = wide.astype(BF16)
                term = grad * h * scale
                gain[...] += term[:8] + term[8:]
                return carry

            lax.fori_loop(0, tok // 16, norm, 0)
            da_cols = r.da_cols
            swap_s, swap_r = r.swap

            def swap(d):
                peer = at.peer(d)
                cols = pl.ds(pl.multiple_of(peer[0] * share, 128), share)
                rows = pl.ds(pl.multiple_of(at.s * tok, tok), tok)
                return send(da.at[:, cols], da_cols.at[rows], swap_s.at[d], swap_r.at[d], peer)

            for d in reversed(range(1, n_seq)):
                swap(d).start()
            cols = pl.ds(pl.multiple_of(at.s * share, 128), share)
            rows = pl.ds(pl.multiple_of(at.s * tok, tok), tok)
            da_cols[rows] = da[:, cols]
            yield
            for d in range(1, n_seq):
                swap(d).wait()

        def products():
            ready(4, 7)
            jobs = [(r.grads[0], dg, n2_all, i) for i in range(0, units, step)]
            jobs += [(r.grads[1], du, n2_all, i) for i in range(0, units, step)]
            jobs += [(None, None, None, b) for b in range(line)]
            waiting = [None, None]
            for n, (out, act, rows_in, i) in enumerate(jobs):
                if waiting[n % 2] is not None:
                    waiting[n % 2].wait()
                if out is None:
                    rows = slice(2 * tok * i, 2 * tok * (i + 1))
                    r.stage[n % 2] = dot(hid[rows], down_w[...], NN).astype(BF16)
                    src = r.stage.at[n % 2].reshape(2, tok, model)
                    dst = r.out_part.at[pl.ds(2 * i, 2)]
                else:
                    r.stage[n % 2, :step] = to_grad(act, rows_in, i)
                    src, dst = r.stage.at[n % 2, pl.ds(0, step)], out.at[pl.ds(i, step)]
                waiting[n % 2] = pltpu.make_async_copy(src, dst, r.stage_s.at[n % 2])
                waiting[n % 2].start()
                yield
            for one in waiting:
                one.wait()

        def fill(low, rows):
            part = hid[:, low : low + rows]
            rows_in = grad_all[...].reshape(tokens, model)
            r.reduce[0][low : low + rows] = dot(part, rows_in, TN).astype(BF16)

        down = reduce.steps(at, [None, r.grad_down] + r.reduce, fill)
        interleave(MIDDLE_ORDER, {0: chain(), 1: down, 2: products()})

    return rooms.run(body, "middle", 4, n_seq, n_fsdp)


BACK_ONE_ORDER = [2, 0, 3, 0, 1, 2, 2, 3, 2, 2, 1, 0, 2, 2, 3, 2, 0, 2, 1, 0, 2, 0, 2, 3, 0, 2, 0, 2]
BACK_ONE_ORDER += [0, 1, 2, 0, 2, 3, 0, 2, 0, 2, 0]


def back_one(n_seq, n_fsdp, da_cols, w_qkv, w_o, o_all, n1, saved, out_part, h1, grad):
    q, k, v, lse, cos, sin, pos_col, pos_row, doc_col, doc_row = saved
    (length, share), model = q.shape, w_qkv.shape[0]
    tok = length // n_seq
    rooms = Rooms()
    rooms.take(
        VMEM, da_cols=da_cols, h1=h1, q=q, k=k, v=v, lse=lse,
        cos=cos, sin=sin, pos_col=pos_col, pos_row=pos_row, doc_col=doc_col, doc_row=doc_row,
    )
    rooms.take(ANY, w_qkv=w_qkv, w_o=w_o, o_all=o_all, n1=n1, out_part=out_part, g_in=grad)
    rooms.give(ANY, g_out=like(grad.shape), dw_qkv=like((model, 3 * share)))
    rooms.give(
        VMEM,
        dn1_part=like((n_seq, tok, model)),
        dw_o=like((model // n_fsdp, share)),
        block_out=like((tok, model)),
    )
    o_block = like((n_fsdp, model // n_fsdp, share))
    line_o = ScatterLine(o_block, n_fsdp)
    halve = HalveSeq((n_seq, length, share), BF16, n_seq)
    line_out = ScatterLine(out_part, n_fsdp, 2, far=True)
    reduce = ReduceSeq(grad.shape, grad.dtype, n_seq)
    rooms.keep(
        line_o=line_o.scratch,
        line_out=line_out.scratch,
        mlp_out=room(tok, model, dtype=F32),
        reduce=reduce.scratch,
        dw_o_part=room(*o_block.shape),
        w_qkv_here=room(*w_qkv.shape),
        w_o_here=room(*w_o.shape),
        o_here=room(*o_all.shape),
        do_part=room(n_seq, length, share),
        halve=halve.scratch,
        do=room(length, share),
        dqkv=room(length, 3 * share),
        dk=room(length, 128, dtype=F32),
        dv=room(length, 128, dtype=F32),
        dw_stage=room(2, share, 3 * share),
        load=DMA((4,)),
        stage=DMA((2,)),
    )

    def body(at, r):
        def chain():
            loads = [
                pltpu.make_async_copy(a, b, r.load.at[i])
                for i, (a, b) in enumerate(
                    ((r.w_qkv, r.w_qkv_here), (r.w_o, r.w_o_here), (r.o_all, r.o_here), (r.n1, r.o_here))
                )
            ]
            for i in (1, 2, 0):
                loads[i].start()
            loads[1].wait()
            da_cols = r.da_cols
            w_qkv_here, w_o_here, o_here = r.w_qkv_here, r.w_o_here, r.o_here
            do_part = r.do_part
            for d in reversed(range(n_seq)):
                rows = pl.ds(pl.multiple_of(at.peer(d)[0] * share, share), share)
                do_part[d] = dot(da_cols[...], w_o_here[rows], NT).astype(BF16)
            exchange = halve.steps(at, do_part, r.do, r.halve)
            next(exchange)
            yield
            loads[2].wait()
            dw_o = r.dw_o_part
            per = n_fsdp // n_seq
            for j in range(n_seq):
                field = dot(o_here[j], da_cols[...], TN).astype(BF16)
                dw_o[j * per : (j + 1) * per] = field.reshape((per,) + dw_o.shape[1:])
            loads[3].start()
            running[1] = line_o.steps(at, [dw_o, r.dw_o] + r.line_o)
            yield
            for _ in exchange:
                yield
            do = r.do
            dqkv = r.dqkv
            masking = [r.pos_col, r.pos_row, r.doc_col, r.doc_row]
            for pair in range(share // 128):
                back_pair(
                    pair, do, r.q, r.k, r.v, r.lse, r.cos, r.sin,
                    dqkv, masking, r.dk, r.dv,
                )
                yield
            loads[3].wait()
            dw_qkv, stage, stage_s = r.dw_qkv, r.dw_stage, r.stage

            def put(j):
                return pltpu.make_async_copy(
                    stage.at[j % 2], dw_qkv.at[pl.ds(j * share, share)], stage_s.at[j % 2]
                )

            for j in range(n_seq):
                if j >= 2:
                    put(j - 2).wait()
                stage[j % 2] = dot(o_here[j], dqkv[...], TN).astype(BF16)
                put(j).start()
                yield
            loads[0].wait()
            dn1_part = r.dn1_part
            for j in range(n_seq):
                rows = slice(j * share, (j + 1) * share)
                field = dot(dqkv[...], w_qkv_here[rows], NT).astype(BF16)
                for i in range(n_seq):
                    dn1_part[jnp.bitwise_xor(at.s, i), :, rows] = field[i * tok : (i + 1) * tok]
                yield
            put(n_seq - 2).wait()
            put(n_seq - 1).wait()

        def rows_out():
            yield from line_out.steps(at, [r.out_part, r.mlp_out] + r.line_out)
            h1, mlp_out, block_out = r.h1, r.mlp_out, r.block_out

            def add(i, carry):
                rows = pl.ds(i * 16, 16)
                block_out[rows] = (h1[rows] + mlp_out[rows]).astype(BF16)
                return carry

            lax.fori_loop(0, tok // 16, add, 0)

        running = {
            0: chain(),
            3: rows_out(),
            2: reduce.steps(at, [r.g_in, r.g_out] + r.reduce),
        }
        interleave(BACK_ONE_ORDER, running)

    return rooms.run(body, "back_one", 2, n_seq, n_fsdp)


BACK_TWO_ORDER = [0, 2, 1, 3, 0, 2, 1, 1, 3, 2, 1, 1, 0, 2, 2, 1, 1, 2, 1, 1, 2, 0, 2, 1, 1, 0, 0, 2, 2]
BACK_TWO_ORDER += [1, 1, 1, 1, 3, 3, 0, 1, 1, 0]


def back_two(
    n_seq, n_fsdp, dn1_part, dw_qkv, dw_o, source, dh1, gain_a, gain_m_term, grad
):
    tok, model = source.shape
    rooms = Rooms()
    line = ScatterLine(dw_qkv, n_fsdp, 2, far=True)
    gain_block = like((n_fsdp, 8, model // n_fsdp), F32)
    line_gain = ScatterLine(gain_block, n_fsdp)
    scatter = HalveSeq(dn1_part.shape, BF16, n_seq)
    reduce = ReduceSeq(grad.shape, grad.dtype, n_seq)
    spread, spread_o = SpreadSeq(n_seq), SpreadSeq(n_seq)
    gather = GatherSeq(n_seq)
    rooms.take(
        VMEM, dn1_part=dn1_part, source=source, dh1=dh1,
        gain_a=gain_a, gain_m_term=gain_m_term,
    )
    rooms.take(ANY, dw_qkv=dw_qkv, dw_o=dw_o, g_in=grad)
    rooms.give(
        ANY,
        g_out=like(grad.shape),
        dw_qkv_all=like((n_seq,) + dw_qkv.shape[1:]),
        dw_o_all=like((n_seq,) + dw_o.shape),
    )
    rooms.give(
        VMEM,
        grad_in=like((tok, model)),
        gains=like(gain_block.shape[1:], F32),
    )
    rooms.keep(
        line=line.scratch,
        line_gain=line_gain.scratch,
        scatter=scatter.scratch,
        reduce=reduce.scratch,
        spread=spread.scratch,
        spread_o=spread_o.scratch,
        gather=gather.scratch,
        dw_own=room(*dw_qkv.shape[1:]),
        dn1=room(tok, model, dtype=F32),
        gain_part=room(*gain_block.shape, dtype=F32),
        gain_own=room(*gain_block.shape[1:], dtype=F32),
        gain_all=room(n_seq, *gain_block.shape[1:], dtype=F32),
        gain_sum=room(8, model, dtype=F32),
    )

    def body(at, r):
        def weights():
            yield from line.steps(at, [r.dw_qkv, r.dw_own] + r.line)
            yield from spread.steps(at, [r.dw_own, r.dw_qkv_all] + r.spread)

        def rows_in():
            yield from scatter.steps(at, r.dn1_part, r.dn1, r.scatter)
            source, dh1, dn1 = r.source, r.dh1, r.dn1
            gain_a, grad_in, gain_sum = r.gain_a, r.grad_in, r.gain_sum
            gain_sum[...] = jnp.zeros_like(gain_sum)

            def norm(i, carry):
                rows = pl.ds(i * 16, 16)
                x, grad = source[rows].astype(F32), dn1[rows]
                scale = lax.rsqrt(jnp.mean(x * x, axis=-1, keepdims=True) + NORM_EPS)
                wide = dh1[rows] + norm_back(grad, x, scale, gain_a[...])
                grad_in[rows] = wide.astype(BF16)
                term = grad * x * scale
                gain_sum[...] += term[:8] + term[8:]
                return carry

            lax.fori_loop(0, tok // 16, norm, 0)
            first = jnp.sum(gain_sum[...], axis=0, keepdims=True)
            second = jnp.sum(r.gain_m_term[...], axis=0, keepdims=True)
            row = lax.broadcasted_iota(jnp.int32, gain_sum.shape, 0)
            both = jnp.where(row == 0, first, jnp.where(row == 1, second, 0.0))
            part, width = r.gain_part, model // n_fsdp
            for f in range(n_fsdp):
                part[f] = both[:, f * width : (f + 1) * width]
            yield
            yield from line_gain.steps(at, [part, r.gain_own] + r.line_gain)
            yield from gather.steps(at, [r.gain_own, r.gain_all] + r.gather)
            total = r.gain_all[0]
            for j in range(1, n_seq):
                total = total + r.gain_all[j]
            r.gains[...] = total

        running = {
            0: weights(),
            1: reduce.steps(at, [r.g_in, r.g_out] + r.reduce),
            2: rows_in(),
            3: spread_o.steps(at, [r.dw_o, r.dw_o_all] + r.spread_o),
        }
        interleave(BACK_TWO_ORDER, running)

    return rooms.run(body, "back_two", 3, n_seq, n_fsdp)


def finish_kernel(gate, up, down, qkv, o, rows_out, rows_in, gains, mlp, attn, out, back, gain):
    for c, ref in enumerate((gate, up, down)):
        mlp[c] = ref[...].astype(F32)
    n_seq, rows, share = o.shape
    for s in range(n_seq):
        at = pl.ds(s * share, share)
        for c in range(3):
            attn[:, c, at] = qkv[s, :, c * share : (c + 1) * share].astype(F32)
        attn[:, 3, at] = o[s].astype(F32)
    out[...] = rows_out[...]
    back[...] = rows_in[...]
    gain[...] = gains[...]


def grid_call(kernel, name, grid, args, in_specs, outs, out_specs, scratch=(), aliases=None):
    return pl.pallas_call(
        kernel,
        grid=grid,
        out_shape=outs,
        in_specs=in_specs,
        out_specs=out_specs,
        scratch_shapes=list(scratch),
        input_output_aliases=aliases or {},
        compiler_params=pltpu.CompilerParams(vmem_limit_bytes=48 * 2**20),
        name=name,
    )(*args)


def on_device(
    n_seq, n_fsdp,
    hidden_in, gain_attn, attn_weights, gain_mlp, mlp_weights, out_grad, block_slots, doc_ids,
):
    tok, model = hidden_in.shape[1:]
    share = model // n_seq
    start = lax.axis_index("seq") * share
    w_own = lax.dynamic_slice_in_dim(attn_weights, start, share, 2).reshape(-1, 4 * share)
    mlp_w = mlp_weights.transpose(1, 0, 2)
    a = front(
        n_seq, n_fsdp, w_own, hidden_in[0], [gain_attn[None], gain_mlp[None]], out_grad[0], mlp_w,
        block_slots, doc_ids,
    )
    tables = (a.cos, a.sin, a.pos_col, a.pos_row, a.doc_col, a.doc_row)
    w_qkv, w_o = a.w_qkv_out.reshape(model, -1), a.w_o_out.reshape(model, -1)
    m = middle(
        n_seq, n_fsdp, a.hid, a.dg, a.du, a.n2_out, a.grad_out, mlp_w, a.middle, out_grad[0], a.gain_m
    )
    b = back_one(
        n_seq, n_fsdp, m.da_cols, w_qkv, w_o, a.o_out, a.n1_out,
        (a.q, a.k, a.v, a.lse, *tables), m.out_part, a.middle, m.grads[0],
    )
    c = back_two(
        n_seq, n_fsdp, b.dn1_part, b.dw_qkv.reshape(n_fsdp, -1, 3 * share), b.dw_o,
        hidden_in[0], m.dh1, a.gain_a, m.gain, m.grads[1],
    )
    own_rows, units = b.dw_o.shape[0], c.g_out.shape[0]
    steps = 8
    u, a_rows, t = units // steps, own_rows // steps, tok // steps
    flat = pl.BlockSpec((u, model), lambda i: (i, 0))
    row = pl.BlockSpec((t, model), lambda i: (i, 0))
    whole = pl.BlockSpec(c.gains.shape, lambda i: (0, 0))
    mlp_grad, attn_grad, block_out, grad_in, gains = grid_call(
        finish_kernel,
        "finish",
        (steps,),
        (b.g_out, c.g_out, m.grad_down, c.dw_qkv_all, c.dw_o_all, b.block_out, c.grad_in, c.gains),
        [flat] * 3
        + [pl.BlockSpec((n_seq, a_rows, n * share), lambda i: (0, i, 0)) for n in (3, 1)]
        + [row, row, whole],
        [
            like((3, units, model), F32),
            like((own_rows, 4, model), F32),
            like((tok, model)),
            like((tok, model)),
            like(c.gains.shape, F32),
        ],
        [
            pl.BlockSpec((3, u, model), lambda i: (0, i, 0)),
            pl.BlockSpec((a_rows, 4, model), lambda i: (i, 0, 0)),
            row,
            row,
            whole,
        ],
    )
    mlp_grad = mlp_grad.transpose(1, 0, 2)
    return (block_out[None], grad_in[None], gains[0], attn_grad, gains[1], mlp_grad)


def solution(mesh):
    return jax.shard_map(
        functools.partial(on_device, mesh.shape["seq"], mesh.shape["fsdp"]),
        mesh=mesh,
        in_specs=(
            P("fsdp", "seq", None),
            P("fsdp"),
            P("fsdp", None, None),
            P("fsdp"),
            P("fsdp", None, None),
            P("fsdp", "seq", None),
            P(),
            P("fsdp", None),
        ),
        out_specs=(
            P("fsdp", "seq", None),
            P("fsdp", "seq", None),
            P("fsdp"),
            P("fsdp", None, None),
            P("fsdp"),
            P("fsdp", None, None),
        ),
        check_vma=False,
    )
```

```python
import functools
import math
import types

import jax
import jax.numpy as jnp
from jax import lax
from jax.experimental import pallas as pl
from jax.experimental.pallas import tpu as pltpu
from jax.sharding import PartitionSpec as P

HEAD = 64


NORM_EPS = 1e-05
ROPE_BASE = 130000.0
MASKED_OUT = -1e30
F32 = jnp.float32
BF16 = jnp.bfloat16
MESH = pl.DeviceIdType.MESH
DMA = pltpu.SemaphoreType.DMA
ANY = pl.BlockSpec(memory_space=pl.ANY)
VMEM = pl.BlockSpec(memory_space=pltpu.VMEM)


def send(src, dst, send_sem, recv_sem, device):
    return pltpu.make_async_remote_copy(
        src_ref=src,
        dst_ref=dst,
        send_sem=send_sem,
        recv_sem=recv_sem,
        device_id=device,
        device_id_type=MESH,
    )


class Place:
    def __init__(self, n_seq, n_fsdp):
        self.n_seq, self.line = n_seq, n_fsdp // 2
        self.s = lax.axis_index("seq")
        self.f = lax.axis_index("fsdp")
        self.r = lax.div(self.f, 2)
        self.c = lax.rem(self.f, 2)
        self.up = (self.s, self.f + 2)
        self.down = (self.s, self.f - 2)
        self.sister = (self.s, 2 * self.r + 1 - self.c)

    def peer(self, d):
        return (jnp.bitwise_xor(self.s, d), self.f)

    def greet(self):
        barrier = pltpu.get_barrier_semaphore()
        wrap = 2 * self.line
        partners = [
            (self.s, lax.rem(self.f + 2, wrap)),
            (self.s, lax.rem(self.f + wrap - 2, wrap)),
            self.sister,
        ]
        partners += [self.peer(d) for d in range(1, self.n_seq)]
        for partner in partners:
            pl.semaphore_signal(barrier, inc=1, device_id=partner, device_id_type=MESH)
        pl.semaphore_wait(barrier, len(partners))


class GatherLine:
    def __init__(self, n_fsdp, parts=1):
        line = n_fsdp // 2
        self.scratch = [DMA((line, parts)) for _ in range(5)] + [DMA((1,))]
        self.parts = parts

    def steps(self, at, x, o, refs, use=None):
        line_r, sis_r, up_s, down_s, sis_s, own_s = refs
        parts, line, r, c = self.parts, at.line, at.r, at.c
        rows = o.shape[1] // parts

        def cut(ref, k):
            return ref.at[pl.ds(k * rows, rows)]

        def go_up(src, b, k):
            return send(src, cut(o.at[2 * b + c], k), up_s.at[b, k], line_r.at[b, k], at.up)

        def go_down(src, b, k):
            return send(src, cut(o.at[2 * b + c], k), down_s.at[b, k], line_r.at[b, k], at.down)

        def go_sister(src, b, k):
            return send(src, cut(o.at[2 * b + c], k), sis_s.at[b, k], sis_r.at[b, k], at.sister)

        def complete(b):
            for k in range(parts):
                src = cut(o.at[2 * b + 1 - c], k)
                send(src, src, sis_s.at[b, k], sis_r.at[b, k], at.sister).wait_recv()
            if use is not None:
                use(b)

        own = pltpu.make_async_copy(x, o.at[at.f], own_s.at[0])
        own.start()
        for k in range(parts):
            src = cut(x, k)
            pl.when(r < line - 1)(lambda: go_up(src, r, k).start())
            pl.when(r > 0)(lambda: go_down(src, r, k).start())
            go_sister(src, r, k).start()
        yield
        for t in range(1, line):
            for k in range(parts):
                low, high = r - t, r + t

                @pl.when(low >= 0)
                def _():
                    src = cut(o.at[2 * low + c], k)
                    go_up(src, low, k).wait_recv()
                    pl.when(r < line - 1)(lambda: go_up(src, low, k).start())
                    go_sister(src, low, k).start()

                @pl.when(high < line)
                def _():
                    src = cut(o.at[2 * high + c], k)
                    go_down(src, high, k).wait_recv()
                    pl.when(r > 0)(lambda: go_down(src, high, k).start())
                    go_sister(src, high, k).start()

            yield
            if t == 1:
                own.wait()
                complete(r)
            else:
                pl.when(r - t + 1 >= 0)(lambda: complete(r - t + 1))
                pl.when(r + t - 1 < line)(lambda: complete(r + t - 1))
        pl.when(r - line + 1 >= 0)(lambda: complete(r - line + 1))
        pl.when(r + line - 1 < line)(lambda: complete(r + line - 1))
        yield
        for b in range(line):
            for k in range(parts):
                src = cut(x, k)
                go_sister(src, b, k).wait_send()
                pl.when((b <= r) & (r < line - 1))(lambda: go_up(src, b, k).wait_send())
                pl.when((b >= r) & (r > 0))(lambda: go_down(src, b, k).wait_send())


class ScatterLine:
    def __init__(self, part, n_fsdp, parts=1, far=False):
        line = n_fsdp // 2
        block = part.shape[1:]
        self.scratch = [
            pltpu.VMEM((line,) + block, part.dtype),
            pltpu.VMEM((line + 1,) + block, part.dtype),
        ]
        self.scratch += [DMA((line, parts)), DMA((line, parts)), DMA((line, parts))]
        self.scratch += [DMA((line + 1, parts))]
        if far:
            self.scratch += [pltpu.VMEM((line,) + block, part.dtype), DMA((line,))]
        self.parts, self.far = parts, far

    def steps(self, at, refs):
        part, o, sis, come, sis_s, sis_r, line_s, line_r = refs[:8]
        near, near_s = refs[8:] if self.far else (None, None)
        parts, line, r, c = self.parts, at.line, at.r, at.c
        rows = part.shape[1] // parts
        tile = 16 if rows % 16 == 0 else rows

        def cut(ref, k):
            return ref.at[pl.ds(k * rows, rows)]

        def to_sister(b, k):
            return send(
                cut(part.at[2 * b + 1 - c], k),
                cut(sis.at[b], k),
                sis_s.at[b, k],
                sis_r.at[b, k],
                at.sister,
            )

        def slot(b, own):
            return jnp.where(b == own, line, b)

        def go_up(b, k):
            return send(cut(sis.at[b], k), cut(come.at[b], k), line_s.at[b, k], line_r.at[b, k], at.up)

        def go_down(b, k, own):
            i = slot(b, own)
            return send(
                cut(sis.at[b], k), cut(come.at[i], k), line_s.at[b, k], line_r.at[i, k], at.down
            )

        def add(b, k, came, out=None):
            def body(i, carry):
                at_rows = pl.ds(k * rows + i * tile, tile)
                own = near[b, at_rows] if self.far else part[2 * b + c, at_rows]
                total = own.astype(F32) + sis[b, at_rows].astype(F32)
                for j in came:
                    total = total + come[j, at_rows].astype(F32)
                if out is None:
                    sis[b, at_rows] = total.astype(sis.dtype)
                else:
                    out[at_rows] = total.astype(out.dtype)
                return carry

            lax.fori_loop(0, rows // tile, body, 0)

        order = []
        for j in range(line):
            order += [b for b in (line - 1 - j, j) if b not in order]
        for b in order:
            for k in range(parts):
                to_sister(b, k).start()
        if self.far:
            loads = [
                pltpu.make_async_copy(part.at[2 * b + c], near.at[b], near_s.at[b])
                for b in range(line)
            ]
            for one in loads:
                one.start()
            for one in loads:
                one.wait()
        yield
        for t in range(line - 1):
            for k in range(parts):
                high, low = line - 1 - t + r, t - (line - 1 - r)

                @pl.when(high < line)
                def _():
                    to_sister(high, k).wait_recv()

                    @pl.when(r > 0)
                    def _():
                        go_up(high, k).wait_recv()
                        add(high, k, [high])

                    pl.when(r == 0)(lambda: add(high, k, []))
                    go_up(high, k).start()

                @pl.when(low >= 0)
                def _():
                    to_sister(low, k).wait_recv()

                    @pl.when(r < line - 1)
                    def _():
                        go_down(low, k, -1).wait_recv()
                        add(low, k, [low])

                    pl.when(r == line - 1)(lambda: add(low, k, []))
                    go_down(low, k, r - 1).start()

            yield
        for k in range(parts):
            to_sister(r, k).wait_recv()
            pl.when(r > 0)(lambda: go_up(r, k).wait_recv())
            pl.when(r < line - 1)(lambda: go_down(r, k, r).wait_recv())
            pl.when(r == 0)(lambda: add(r, k, [line], o))
            pl.when(r == line - 1)(lambda: add(r, k, [r], o))
            pl.when((r > 0) & (r < line - 1))(lambda: add(r, k, [r, line], o))
        yield
        for b in range(line):
            for k in range(parts):
                to_sister(b, k).wait_send()
                pl.when(b != r)(lambda: go_up(b, k).wait_send())


class GatherSeq:
    def __init__(self, n_seq):
        self.scratch = [DMA((n_seq,)), DMA((n_seq,))]

    def steps(self, at, refs):
        x, o, s_sem, r_sem = refs

        def go(d):
            return send(x, o.at[at.s], s_sem.at[d], r_sem.at[d], at.peer(d))

        for d in reversed(range(1, at.n_seq)):
            go(d).start()
        own = pltpu.make_async_copy(x, o.at[at.s], s_sem.at[0])
        own.start()
        yield
        own.wait()
        for d in range(1, at.n_seq):
            go(d).wait()


class HalveSeq:
    def __init__(self, shape, dtype, n_seq):
        n, rows, cols = shape
        bits = n_seq.bit_length() - 1
        self.half = rows // 2
        self.orders = [[(i + p) % bits for i in range(bits)] for p in range(2)]
        self.scratch = [
            pltpu.VMEM((2, n - 1, self.half, cols), dtype), DMA((2, n - 1)), DMA((2, n - 1))
        ]

    def masks(self, p, i):
        out = [0]
        for b in self.orders[p][i + 1 :]:
            out += [m | (1 << b) for m in out]
        return out

    def slot(self, p, i, u):
        return sum(len(self.masks(p, j)) for j in range(i)) + self.masks(p, i).index(u)

    def steps(self, at, part, o, refs):
        land, s_sem, r_sem = refs
        half, bits = self.half, len(self.orders[0])
        tile = 16 if half % 16 == 0 else half

        def go(p, i, u):
            b = 1 << self.orders[p][i]
            if i == 0:
                src = part.at[b | u, pl.ds(p * half, half)]
            else:
                src = land.at[p, self.slot(p, 0, b | u)]
            n = self.slot(p, i, u)
            return send(src, land.at[p, n], s_sem.at[p, n], r_sem.at[p, n], at.peer(b))

        def add(p, u, upto, out, first):
            def body(k, carry):
                rows = pl.ds(pl.multiple_of(k * tile, tile), tile)
                total = part[u, pl.ds(pl.multiple_of(p * half + k * tile, tile), tile)].astype(F32)
                for i in range(upto):
                    total = total + land[p, self.slot(p, i, u), rows].astype(F32)
                out[pl.ds(pl.multiple_of(first + k * tile, tile), tile)] = total.astype(out.dtype)
                return carry

            lax.fori_loop(0, half // tile, body, 0)

        for p in range(2):
            for u in self.masks(p, 0):
                go(p, 0, u).start()
        yield
        for i in range(bits):
            for p in range(2):
                for u in self.masks(p, i):
                    go(p, i, u).wait_recv()
                if i + 1 < bits:
                    b = 1 << self.orders[p][i + 1]
                    for u in self.masks(p, i + 1):
                        add(p, b | u, i + 1, land.at[p, self.slot(p, 0, b | u)], 0)
                        go(p, i + 1, u).start()
                else:
                    add(p, 0, bits, o, p * half)
            yield
        for p in range(2):
            for i in range(bits):
                for u in self.masks(p, i):
                    go(p, i, u).wait_send()


class ReduceSeq:
    def __init__(self, shape, dtype, n_seq, parts=4):
        rows, cols = shape
        self.bits, self.parts = n_seq.bit_length() - 1, parts
        self.rows = rows // parts
        self.room = self.rows - (self.rows >> self.bits)
        self.scratch = [
            pltpu.VMEM(shape, dtype),
            pltpu.VMEM((parts * self.room, cols), dtype),
            DMA((parts,)),
            DMA((parts, self.bits)),
            DMA((parts, self.bits)),
            DMA((parts, n_seq)),
            DMA((parts, n_seq)),
            DMA((parts,)),
        ]

    def steps(self, at, refs, fill=None):
        g_in, o, g, land, load_s, rs_s, rs_r, ag_s, ag_r, own_s = refs
        bits, parts = self.bits, range(self.parts)
        orders = [[(i + p) % bits for i in range(bits)] for p in parts]
        mult = self.rows >> bits

        def bit(t, b):
            return jnp.bitwise_and(lax.shift_right_logical(t, b), 1)

        def base(p, t, n):
            low = p * self.rows
            for i in range(n):
                low = low + bit(t, orders[p][i]) * (self.rows >> (i + 1))
            return pl.multiple_of(low, mult)

        def load(p):
            part = pl.ds(p * self.rows, self.rows)
            return pltpu.make_async_copy(g_in.at[part], g.at[part], load_s.at[p])

        def slot(p, i):
            return p * self.room + sum(self.rows >> (j + 1) for j in range(i))

        def halve(p, i):
            size = self.rows >> (i + 1)
            other = jnp.bitwise_xor(at.s, 1 << orders[p][i])
            return send(
                g.at[pl.ds(base(p, other, i + 1), size)],
                land.at[pl.ds(slot(p, i), size)],
                rs_s.at[p, i],
                rs_r.at[p, i],
                (other, at.f),
            )

        def add(p, i):
            size = self.rows >> (i + 1)
            low, first = base(p, at.s, i + 1), slot(p, i)

            def body(j, carry):
                mine = pl.ds(pl.multiple_of(low + j * 16, 16), 16)
                came = pl.ds(pl.multiple_of(first + j * 16, 16), 16)
                total = g[mine].astype(F32) + land[came].astype(F32)
                g[mine] = total.astype(g.dtype)
                return carry

            lax.fori_loop(0, size // 16, body, 0)

        def masks(p, j):
            out = [0]
            for i in range(j):
                out += [m | (1 << orders[p][bits - 1 - i]) for m in out]
            return out

        def double(p, j, mask):
            b = orders[p][bits - 1 - j]
            piece = pl.ds(base(p, jnp.bitwise_xor(at.s, mask), bits), mult)
            src = g.at[piece] if mask == 0 else o.at[piece]
            i = (1 << b) | mask
            return send(
                src, o.at[piece], ag_s.at[p, i], ag_r.at[p, i], (jnp.bitwise_xor(at.s, 1 << b), at.f)
            )

        def arrive(p, j, mask):
            b = orders[p][bits - 1 - j]
            piece = pl.ds(base(p, jnp.bitwise_xor(at.s, (1 << b) | mask), bits), mult)
            i = (1 << b) | mask
            return send(
                o.at[piece], o.at[piece], ag_s.at[p, i], ag_r.at[p, i],
                (jnp.bitwise_xor(at.s, 1 << b), at.f),
            )

        def own(p):
            piece = pl.ds(base(p, at.s, bits), mult)
            return pltpu.make_async_copy(g.at[piece], o.at[piece], own_s.at[p])

        if g_in is not None:
            for p in parts:
                load(p).start()
        for p in parts:
            if g_in is not None:
                load(p).wait()
            if fill is not None:
                fill(p * self.rows, self.rows)
            halve(p, 0).start()
        yield
        for i in range(bits):
            for p in parts:
                halve(p, i).wait_recv()
                add(p, i)
                if i + 1 < bits:
                    halve(p, i + 1).start()
                else:
                    for j in range(bits):
                        double(p, j, 0).start()
                    own(p).start()
                yield
        for j in range(bits):
            for p in parts:
                for mask in masks(p, j):
                    arrive(p, j, mask).wait_recv()
                    came = (1 << orders[p][bits - 1 - j]) | mask
                    for later in range(j + 1, bits):
                        double(p, later, came).start()
                yield
        for p in parts:
            own(p).wait()
            for i in range(bits):
                halve(p, i).wait_send()
            for j in range(bits):
                for mask in masks(p, j):
                    double(p, j, mask).wait_send()


class SpreadSeq:
    def __init__(self, n_seq):
        self.bits = n_seq.bit_length() - 1
        self.scratch = [DMA((2, n_seq)), DMA((2, n_seq)), DMA((1,))]

    def steps(self, at, refs):
        x, o, s_sem, r_sem, own_s = refs
        bits, half = self.bits, x.shape[0] // 2
        orders = [[(i + p) % bits for i in range(bits)] for p in range(2)]

        def known(p, j):
            out = [0]
            for i in range(j):
                out += [m | (1 << orders[p][i]) for m in out]
            return out

        def piece(p, mask):
            return o.at[jnp.bitwise_xor(at.s, mask), pl.ds(p * half, half)]

        def go(p, j, mask):
            b = 1 << orders[p][j]
            src = x.at[pl.ds(p * half, half)] if mask == 0 else piece(p, mask)
            i = b | mask
            return send(src, piece(p, mask), s_sem.at[p, i], r_sem.at[p, i], at.peer(b))

        def arrive(p, j, mask):
            b = 1 << orders[p][j]
            i = b | mask
            here = piece(p, i)
            return send(here, here, s_sem.at[p, i], r_sem.at[p, i], at.peer(b))

        for p in range(2):
            for j in range(bits):
                go(p, j, 0).start()
        own = pltpu.make_async_copy(x, o.at[at.s], own_s.at[0])
        own.start()
        yield
        for j in range(bits):
            for p in range(2):
                for mask in known(p, j):
                    arrive(p, j, mask).wait_recv()
                    for later in range(j + 1, bits):
                        go(p, later, (1 << orders[p][j]) | mask).start()
            yield
        own.wait()
        for j in range(bits):
            for p in range(2):
                for mask in known(p, j):
                    go(p, j, mask).wait_send()


def interleave(order, running):
    for name in order:
        if name in running and next(running[name], END) is END:
            del running[name]
    while running:
        for name in list(running):
            if next(running[name], END) is END:
                del running[name]


END = object()


class Rooms:
    def __init__(self):
        self.args, self.in_specs, self.outs, self.out_specs, self.scratch = [], [], [], [], []
        self.names = ([], [], [])
        self.brought, self.posted = [], []

    def note(self, group, name, x):
        many = isinstance(x, (list, tuple))
        self.names[group].append((name, len(x) if many else None))
        return list(x) if many else [x]

    def take(self, spec, **arrays):
        for name, x in arrays.items():
            new = self.note(0, name, x)
            self.args += new
            self.in_specs += [spec] * len(new)

    def give(self, spec, **shapes):
        for name, x in shapes.items():
            new = self.note(1, name, x)
            self.outs += new
            self.out_specs += [spec] * len(new)

    def keep(self, **kinds):
        for name, x in kinds.items():
            self.scratch += self.note(2, name, x)

    def bring(self, **arrays):
        names = list(arrays)
        self.take(ANY, **{far(n): x for n, x in arrays.items()})
        self.keep(**{n: pltpu.VMEM(x.shape, x.dtype) for n, x in arrays.items()})
        self.brought = names

    def post(self, **shapes):
        self.give(ANY, **{far(n): x for n, x in shapes.items()})
        self.keep(**{n: pltpu.VMEM(x.shape, x.dtype) for n, x in shapes.items()})
        self.posted = list(shapes)

    def bind(self, refs, groups):
        table, refs = types.SimpleNamespace(), list(refs)
        for group in groups:
            for name, many in self.names[group]:
                count = 1 if many is None else many
                mine, refs = refs[:count], refs[count:]
                setattr(table, name, mine[0] if many is None else mine)
        return table

    def run(self, body, name, collective_id, n_seq, n_fsdp):
        if self.brought:
            self.keep(brought_s=DMA((len(self.brought),)))
        if self.posted:
            self.keep(posted_s=DMA((len(self.posted),)))

        def kernel(*refs):
            at = Place(n_seq, n_fsdp)
            r = self.bind(refs, (0, 1, 2))
            loads = [
                pltpu.make_async_copy(getattr(r, far(n)), getattr(r, n), r.brought_s.at[i])
                for i, n in enumerate(self.brought)
            ]
            stores = [
                pltpu.make_async_copy(getattr(r, n), getattr(r, far(n)), r.posted_s.at[i])
                for i, n in enumerate(self.posted)
            ]
            for one in loads:
                one.start()

            def arrive():
                for one in loads:
                    one.wait()

            def leave(*mine):
                for n, one in zip(self.posted, stores):
                    if any(getattr(r, n) is ref for ref in mine):
                        one.start()

            r.arrive, r.leave = arrive, leave
            at.greet()
            body(at, r)
            for one in stores:
                one.wait()

        out = pl.pallas_call(
            kernel,
            out_shape=self.outs,
            in_specs=self.in_specs,
            out_specs=self.out_specs,
            scratch_shapes=self.scratch,
            compiler_params=pltpu.CompilerParams(
                collective_id=collective_id, has_side_effects=True, vmem_limit_bytes=62 * 2**20
            ),
            name=name,
        )(*self.args)
        results = self.bind(out, (1,))
        for n in self.posted:
            setattr(results, n, getattr(results, far(n)))
        return results


def far(name):
    return name + "_far"


def like(shape, dtype=BF16):
    return jax.ShapeDtypeStruct(tuple(shape), dtype)


def room(*shape, dtype=BF16):
    return pltpu.VMEM(shape, dtype)


def dot(a, b, dims):
    return lax.dot_general(a, b, (dims, ((), ())), preferred_element_type=F32)


NN = ((1,), (0,))
NT = ((1,), (1,))
TN = ((0,), (0,))


def turned(x, cos, sin):
    lane = lax.broadcasted_iota(jnp.int32, x.shape, 1)
    other = jnp.where(lane % HEAD < HEAD // 2, pltpu.roll(x, 96, 1), pltpu.roll(x, 32, 1))
    return x * cos + other * sin


def head_masks():
    lane = lax.broadcasted_iota(jnp.int32, (1, 128), 1)
    first = (lane < HEAD).astype(F32)
    return first, 1.0 - first


def back_pair(pair, do, q, k, v, lse, cos, sin, dqkv, masking, dk, dv):
    pos_col, pos_row, doc_col, doc_row = masking
    length, share = q.shape
    span = 256
    masks = head_masks()
    lane = lax.broadcasted_iota(jnp.int32, (span, 128), 1)
    lanes = slice(pair * 128, pair * 128 + 128)
    dk[...] = jnp.zeros_like(dk)
    dv[...] = jnp.zeros_like(dv)

    def one_span(i, carry):
        rows = pl.ds(pl.multiple_of(i * span, span), span)
        allowed = (pos_row[...] <= pos_col[rows]) & (doc_row[...] == doc_col[rows])
        bias = jnp.where(allowed, 0.0, MASKED_OUT)
        dq = jnp.zeros((span, 128), F32)
        for h in range(2):
            mask = masks[h].astype(BF16)
            field, grad = q[rows, lanes] * mask, do[rows, lanes] * mask
            log_total = jnp.sum(
                jnp.where(lane == 2 * pair + h, lse[rows], 0.0), axis=-1, keepdims=True
            )
            z = dot(field, k[:, lanes], NT) * 0.125 + bias
            prob = jnp.exp(z - log_total)
            dp = dot(grad, v[:, lanes], NT)
            delta = jnp.sum(prob * dp, axis=-1, keepdims=True)
            dz = (prob * (dp - delta)).astype(BF16)
            dq = dq + dot(dz, k[:, lanes], NN) * masks[h]
            dk[...] += dot(dz, field, TN)
            dv[...] += dot(prob.astype(BF16), grad, TN)
        dqkv[rows, lanes] = turned(dq * 0.125, cos[rows], -sin[rows]).astype(BF16)
        return carry

    lax.fori_loop(0, length // span, one_span, 0)
    at = share + pair * 128
    dqkv[:, at : at + 128] = turned(dk[...] * 0.125, cos[...], -sin[...]).astype(BF16)
    at = 2 * share + pair * 128
    dqkv[:, at : at + 128] = dv[...].astype(BF16)


def norm_back(grad_normed, value, scale, gain):
    weighted = grad_normed * gain
    inner_mean = jnp.mean(weighted * value, axis=-1, keepdims=True)
    return scale * (weighted - value * scale * scale * inner_mean)


def scale_of(value):
    return lax.rsqrt(jnp.mean(value * value, axis=-1, keepdims=True) + NORM_EPS)


def fill_tables(slots, docs, r):
    length = docs.shape[1]
    block = length // (2 * slots.shape[1])

    def place(shape, axis):
        i = lax.broadcasted_iota(jnp.int32, shape, axis)
        slot = jnp.zeros(shape, jnp.int32)
        for j in range(2 * slots.shape[1]):
            slot = jnp.where(i // block == j, slots[j % 2, j // 2], slot)
        return slot * block + i % block

    r.pos_col[...] = place((length, 1), 0)
    r.pos_row[...] = place((1, length), 1)
    lane = lax.broadcasted_iota(jnp.int32, (1, 128), 1)
    half = HEAD // 2
    steps = (lane % half).astype(F32) / half
    freqs = jnp.exp(steps * -math.log(ROPE_BASE))
    sign = jnp.where(lane % HEAD < half, -1.0, 1.0)
    r.doc_row[...] = jnp.zeros((1, length), jnp.int32)

    def body(i, carry):
        rows = pl.ds(pl.multiple_of(i * 128, 128), 128)
        pos = r.pos_col[rows]
        turn = pos.astype(F32) * freqs
        r.cos[rows] = jnp.cos(turn)
        r.sin[rows] = jnp.sin(turn) * sign
        at = lax.broadcasted_iota(jnp.int32, (128, length), 1)
        own = jnp.sum(jnp.where(at == pos, docs[...], 0), axis=1, keepdims=True)
        r.doc_col[rows] = own
        here = lax.broadcasted_iota(jnp.int32, (128, length), 0) + i * 128
        r.doc_row[...] += jnp.sum(jnp.where(at == here, own, 0), axis=0, keepdims=True)
        return carry

    lax.fori_loop(0, length // 128, body, 0)


FRONT_ORDER = [0, 0, 0, 1, 0, 0, 1, 0, 1, 0, 1, 0, 1, 1, 2, 0, 0, 2, 0, 0, 0, 0, 2, 0, 2, 0]


def front(n_seq, n_fsdp, w_own, hidden, own_gains, out_grad, mlp_w, slots, docs):
    tok, model = hidden.shape
    length, share = n_seq * tok, w_own.shape[1] // 4
    line, rows_f, units = n_fsdp // 2, w_own.shape[0], mlp_w.shape[1]
    qkv_shape, o_shape = (n_fsdp, rows_f, 3 * share), (n_fsdp, rows_f, share)
    per = n_fsdp // n_seq
    n_pairs = share // 128
    span = 256
    get_w, get_o = GatherLine(n_fsdp, 2), GatherLine(n_fsdp)
    get_gain, get_grad, get_n2 = GatherLine(n_fsdp), GatherLine(n_fsdp, 2), GatherLine(n_fsdp, 2)
    get_x = GatherSeq(n_seq)
    rooms = Rooms()
    rooms.take(VMEM, hidden=hidden, own_gains=own_gains, docs=docs)
    rooms.take(pl.BlockSpec(memory_space=pltpu.SMEM), slots=slots)
    rooms.take(ANY, w_own=w_own, out_grad=out_grad, mlp_w=mlp_w)
    rooms.give(
        ANY,
        w_qkv_out=like(qkv_shape),
        w_o_out=like(o_shape),
        n1_out=like((n_seq, length, share)),
        o_out=like((n_seq, length, share)),
        n2_out=like((n_fsdp, tok, model)),
        grad_out=like((n_fsdp, tok, model)),
        hid=like((n_fsdp * tok, units)),
        dg=like((n_fsdp * tok, units)),
        du=like((n_fsdp * tok, units)),
    )
    rooms.post(
        q=like((length, share)),
        k=like((length, share)),
        v=like((length, share)),
        lse=like((length, 128), F32),
        middle=like((tok, model), F32),
        cos=like((length, 128), F32),
        sin=like((length, 128), F32),
    )
    rooms.give(
        VMEM,
        gain_a=like((1, model), F32),
        gain_m=like((1, model), F32),
        pos_col=like((length, 1), jnp.int32),
        pos_row=like((1, length), jnp.int32),
        doc_col=like((length, 1), jnp.int32),
        doc_row=like((1, length), jnp.int32),
    )
    rooms.keep(
        gains=room(32, rows_f),
        get_w=get_w.scratch, get_o=get_o.scratch, get_gain=get_gain.scratch,
        get_grad=get_grad.scratch, get_n2=get_n2.scratch, get_x=get_x.scratch,
        w_qkv_all=room(*qkv_shape),
        w_o_all=room(*o_shape),
        gains_all=room(n_fsdp, 32, rows_f),
        x_all=room(n_seq, tok, model),
        n1=room(n_fsdp, length, rows_f),
        o_all=room(n_seq, length, share),
        y_total=room(length, share, dtype=F32),
        y=room(n_seq, tok, share),
        y_land=room(n_seq, tok, share),
        n2=room(tok, model),
        n2_all=room(n_fsdp, tok, model),
        grad_all=room(n_fsdp, tok, model),
        w_gate=room(units, model),
        w_up=room(units, model),
        w_down=room(units, model),
        act=room(n_fsdp * tok, units, dtype=F32),
        stage=room(line, 3, 2 * tok, units),
        load=DMA((3,)),
        save=DMA((6 + n_fsdp,)),
        stage_s=DMA((line, 3)),
        o_s=DMA((n_pairs, n_seq)),
        o_r=DMA((n_pairs, n_seq)),
        y_s=DMA((n_seq,)),
        y_r=DMA((n_seq,)),
    )

    def body(at, r):
        loads = [
            pltpu.make_async_copy(r.mlp_w.at[i], w, r.load.at[i])
            for i, w in enumerate((r.w_gate, r.w_up, r.w_down))
        ]
        saves = []
        w_qkv, w_o = r.w_own.at[:, pl.ds(0, 3 * share)], r.w_own.at[:, pl.ds(3 * share, share)]

        def save(src, dst):
            saves.append(pltpu.make_async_copy(src, dst, r.save.at[len(saves)]))
            saves[-1].start()

        def total(c, rows, cols):
            low, left = (c // 2) * length, (c % 2) * share
            return (
                slice(low + rows.start, low + rows.stop), slice(left + cols.start, left + cols.stop)
            )

        def project(b):
            for f in (2 * b, 2 * b + 1):
                for c in range(3):
                    weights = r.w_qkv_all[f, :, c * share : (c + 1) * share]
                    for i in range(0, length, span):
                        part = dot(r.n1[f, i : i + span], weights, NN)
                        r.act[total(c, slice(i, i + span), slice(0, share))] += part

        def grad_of(b):
            rows = pl.ds(pl.multiple_of(2 * tok * b, 2 * tok), 2 * tok)
            grad = r.grad_all[pl.ds(2 * b, 2)].reshape(2 * tok, model)
            r.act[rows] = dot(grad, r.w_down[...], NT)

        def stored(b, k):
            rows = pl.ds(pl.multiple_of(2 * tok * b, 2 * tok), 2 * tok)
            return pltpu.make_async_copy(
                r.stage.at[b, k], (r.hid, r.dg, r.du)[k].at[rows], r.stage_s.at[b, k]
            )

        def activate(b):
            rows = pl.ds(pl.multiple_of(2 * tok * b, 2 * tok), 2 * tok)
            n2 = r.n2_all[pl.ds(2 * b, 2)].reshape(2 * tok, model)
            gate = dot(n2, r.w_gate[...], NT)
            up = dot(n2, r.w_up[...], NT)
            grad = r.act[rows]
            sigma = jax.nn.sigmoid(gate)
            silu = gate * sigma
            r.stage[b, 0] = (silu * up).astype(BF16)
            r.stage[b, 1] = (grad * up * sigma * (1.0 + gate * (1.0 - sigma))).astype(BF16)
            r.stage[b, 2] = (grad * silu).astype(BF16)
            for k in range(3):
                stored(b, k).start()

        def attend(pair):
            lanes = slice(pair * 128, pair * 128 + 128)
            masks = head_masks()
            lane = lax.broadcasted_iota(jnp.int32, (span, 128), 1)

            def one_span(i, carry):
                rows = pl.ds(pl.multiple_of(i * span, span), span)
                allowed = (r.pos_row[...] <= r.pos_col[rows]) & (r.doc_row[...] == r.doc_col[rows])
                bias = jnp.where(allowed, 0.0, MASKED_OUT)
                parts = []
                for h in range(2):
                    field = r.q[rows, lanes] * masks[h].astype(BF16)
                    z = dot(field, r.k[:, lanes], NT) * 0.125 + bias
                    top = jnp.max(z, axis=-1, keepdims=True)
                    e = jnp.exp(z - top)
                    sum_e = jnp.sum(e, axis=-1, keepdims=True)
                    prob = (e * (1.0 / sum_e)).astype(BF16)
                    parts.append(dot(prob, r.v[:, lanes], NN) * masks[h])
                    here = lane == 2 * pair + h
                    r.lse[rows] = jnp.where(here, top + jnp.log(sum_e), r.lse[rows])
                r.o_all[at.s, rows, lanes] = (parts[0] + parts[1]).astype(BF16)
                return carry

            lax.fori_loop(0, length // span, one_span, 0)

        def go_o(pair, d, owner):
            here = r.o_all.at[owner, :, pl.ds(pair * 128, 128)]
            return send(here, here, r.o_s.at[pair, d], r.o_r.at[pair, d], at.peer(d))

        def go_y(d):
            peer = at.peer(d)
            return send(r.y.at[peer[0]], r.y_land.at[d], r.y_s.at[d], r.y_r.at[d], peer)

        def chain():
            weights = get_w.steps(at, w_qkv, r.w_qkv_all, r.get_w, project)
            next(weights)
            rows_in = get_x.steps(at, [r.hidden, r.x_all] + r.get_x)
            next(rows_in)
            for one in loads:
                one.start()
            r.act[...] = jnp.zeros_like(r.act)
            for i in range(2):
                gain = r.own_gains[i : i + 1]
                r.gains[16 * i : 16 * i + 16] = jnp.broadcast_to(gain, (16, rows_f)).astype(BF16)
            gain_steps = get_gain.steps(at, r.gains, r.gains_all, r.get_gain)
            next(gain_steps)
            fill_tables(r.slots, r.docs, r)
            r.leave(r.cos, r.sin)
            for _ in gain_steps:
                pass
            for f in range(n_fsdp):
                cols = slice(f * rows_f, (f + 1) * rows_f)
                r.gain_a[:, cols] = r.gains_all[f, 0:1].astype(F32)
                r.gain_m[:, cols] = r.gains_all[f, 16:17].astype(F32)
            next(weights)
            for _ in rows_in:
                pass
            r.lse[...] = jnp.zeros_like(r.lse)

            def norm(i, carry):
                j, k = i // (tok // 16), i % (tok // 16)
                x = r.x_all[j, pl.ds(pl.multiple_of(k * 16, 16), 16)].astype(F32)
                normed = (x * scale_of(x) * r.gain_a[...]).astype(BF16)
                rows = pl.ds(pl.multiple_of(i * 16, 16), 16)
                for f in range(n_fsdp):
                    r.n1[f, rows] = normed[:, f * rows_f : (f + 1) * rows_f]
                return carry

            lax.fori_loop(0, length // 16, norm, 0)
            for f in range(n_fsdp):
                save(r.n1.at[f], r.n1_out.at[f // per, :, pl.ds((f % per) * rows_f, rows_f)])
            yield
            for _ in weights:
                yield
            save(r.w_qkv_all, r.w_qkv_out)
            for c, out in enumerate((r.q, r.k)):
                for j in range(0, share, 128):
                    field = r.act[total(c, slice(0, length), slice(j, j + 128))]
                    out[:, j : j + 128] = turned(field, r.cos[...], r.sin[...]).astype(BF16)
            r.v[...] = r.act[total(2, slice(0, length), slice(0, share))].astype(BF16)
            r.leave(r.q, r.k, r.v)
            projected.append(True)
            yield
            for pair in range(n_pairs):
                attend(pair)
                for d in reversed(range(1, n_seq)):
                    go_o(pair, d, at.s).start()
                yield
            r.leave(r.lse)
            for _ in out_weights:
                pass
            for d in range(n_seq):
                owner = at.peer(d)[0]
                if d:
                    for pair in range(n_pairs):
                        go_o(pair, d, owner).wait_recv()
                for h in range(per):
                    part = dot(
                        r.o_all[owner, :, h * rows_f : (h + 1) * rows_f],
                        r.w_o_all[owner * per + h],
                        NN,
                    )
                    if d == 0 and h == 0:
                        r.y_total[...] = part
                    else:
                        r.y_total[...] += part
                yield
            for j in range(n_seq):
                r.y[j] = r.y_total[j * tok : (j + 1) * tok].astype(BF16)
            for d in reversed(range(1, n_seq)):
                go_y(d).start()
            save(r.o_all, r.o_out)
            save(r.w_o_all, r.w_o_out)
            r.y_land[0] = r.y[at.s]
            yield
            for d in range(1, n_seq):
                go_y(d).wait()

            def middle(i, carry):
                rows = pl.ds(pl.multiple_of(i * 16, 16), 16)
                for j in range(n_seq):
                    cols = slice(j * share, (j + 1) * share)
                    branch = r.y_land[jnp.bitwise_xor(at.s, j), rows].astype(F32)
                    r.middle[rows, cols] = r.hidden[rows, cols].astype(F32) + branch
                h = r.middle[rows]
                r.n2[rows] = (h * scale_of(h) * r.gain_m[...]).astype(BF16)
                return carry

            lax.fori_loop(0, tok // 16, middle, 0)
            r.leave(r.middle)
            yield
            tokens = get_n2.steps(at, r.n2, r.n2_all, r.get_n2, activate)
            next(tokens)
            yield
            next(tokens)
            for _ in grads:
                pass
            for one in loads[:2]:
                one.wait()
            for _ in tokens:
                yield

        def cotangents():
            blocks = get_grad.steps(at, r.out_grad, r.grad_all, r.get_grad, grad_of)
            next(blocks)
            yield
            next(blocks)
            yield
            while not projected:
                yield
            loads[2].wait()
            for _ in blocks:
                yield
            save(r.grad_all, r.grad_out)

        projected = []
        out_weights = get_o.steps(at, w_o, r.w_o_all, r.get_o)
        grads = cotangents()
        interleave(FRONT_ORDER, {0: chain(), 1: out_weights, 2: grads})
        for pair in range(n_pairs):
            for d in range(1, n_seq):
                go_o(pair, d, at.s).wait_send()
        save(r.n2_all, r.n2_out)
        for b in range(line):
            for k in range(3):
                stored(b, k).wait()
        for one in saves:
            one.wait()

    return rooms.run(body, "front", 1, n_seq, n_fsdp)


MIDDLE_ORDER = [0, 0, 1, 1, 2, 2, 2, 2, 0, 1, 1, 2, 2, 0, 1, 1, 2, 2, 0, 1, 1, 0, 1, 1]


def middle(n_seq, n_fsdp, hid, dg, du, n2_all, grad_all, mlp_w, h1, out_grad, gain_m):
    tok, model = h1.shape
    tokens, units = hid.shape
    share, length, line = model // n_seq, n_seq * tok, n_fsdp // 2
    step = min(256, units)
    rooms = Rooms()
    rooms.bring(h1=h1, out_grad=out_grad)
    rooms.take(VMEM, gain_m=gain_m)
    rooms.take(ANY, far=[hid, grad_all, dg, du, n2_all], mlp_w=mlp_w)
    rooms.give(
        ANY,
        grad_down=like((units, model)),
        grads=[like((units, model))] * 2,
        out_part=like((n_fsdp, tok, model)),
    )
    rooms.give(
        VMEM, dh1=like((tok, model), F32), gain=like((8, model), F32), da_cols=like((length, share))
    )
    scatter = ScatterLine(like((n_fsdp, tok, model)), n_fsdp, 2)
    reduce = ReduceSeq((units, model), BF16, n_seq)
    rooms.keep(
        scatter=scatter.scratch,
        reduce=reduce.scratch,
        near=[room(*x.shape) for x in (hid, grad_all, dg, du, n2_all)],
        weights=[room(units, model)] * 3,
        dn2_part=room(n_fsdp, tok, model),
        dn2=room(tok, model, dtype=F32),
        da=room(tok, model),
        stage=room(2, 2 * tok, model),
        load=DMA((8,)),
        stage_s=DMA((2,)),
        swap=[DMA((n_seq,)), DMA((n_seq,))],
    )

    def body(at, r):
        hid, grad_all, dg, du, n2_all = r.near
        gate_w, up_w, down_w = r.weights
        loads = [
            pltpu.make_async_copy(a, b, r.load.at[i])
            for i, (a, b) in enumerate(
                list(zip(r.far, r.near)) + [(r.mlp_w.at[i], w) for i, w in enumerate(r.weights)]
            )
        ]

        def ready(*which):
            for i in which:
                loads[i].wait()

        def to_grad(act, rows_in, i):
            return dot(act[:, i : i + step], rows_in[...].reshape(tokens, model), TN).astype(BF16)

        def chain():
            for i in (0, 1, 2, 3, 5, 6, 4, 7):
                loads[i].start()
            ready(0, 1)
            next(down)
            yield
            ready(2, 3, 5, 6)
            for b in range(line):
                rows = slice(2 * tok * b, 2 * tok * (b + 1))
                part = dot(dg[rows], gate_w[...], NN) + dot(du[rows], up_w[...], NN)
                r.dn2_part[2 * b : 2 * b + 2] = part.astype(BF16).reshape(2, tok, model)
            yield from scatter.steps(at, [r.dn2_part, r.dn2] + r.scatter)
            r.arrive()
            h1, out_grad, gain_m = r.h1, r.out_grad, r.gain_m
            dn2, dh1, da, gain = r.dn2, r.dh1, r.da, r.gain
            gain[...] = jnp.zeros_like(gain)

            def norm(i, carry):
                rows = pl.ds(i * 16, 16)
                h, grad = h1[rows], dn2[rows]
                scale = lax.rsqrt(jnp.mean(h * h, axis=-1, keepdims=True) + NORM_EPS)
                wide = out_grad[rows].astype(F32) + norm_back(grad, h, scale, gain_m[...])
                dh1[rows] = wide
                da[rows] = wide.astype(BF16)
                term = grad * h * scale
                gain[...] += term[:8] + term[8:]
                return carry

            lax.fori_loop(0, tok // 16, norm, 0)
            da_cols = r.da_cols
            swap_s, swap_r = r.swap

            def swap(d):
                peer = at.peer(d)
                cols = pl.ds(pl.multiple_of(peer[0] * share, 128), share)
                rows = pl.ds(pl.multiple_of(at.s * tok, tok), tok)
                return send(da.at[:, cols], da_cols.at[rows], swap_s.at[d], swap_r.at[d], peer)

            for d in reversed(range(1, n_seq)):
                swap(d).start()
            cols = pl.ds(pl.multiple_of(at.s * share, 128), share)
            rows = pl.ds(pl.multiple_of(at.s * tok, tok), tok)
            da_cols[rows] = da[:, cols]
            yield
            for d in range(1, n_seq):
                swap(d).wait()

        def products():
            ready(4, 7)
            jobs = [(r.grads[0], dg, n2_all, i) for i in range(0, units, step)]
            jobs += [(r.grads[1], du, n2_all, i) for i in range(0, units, step)]
            jobs += [(None, None, None, b) for b in range(line)]
            waiting = [None, None]
            for n, (out, act, rows_in, i) in enumerate(jobs):
                if waiting[n % 2] is not None:
                    waiting[n % 2].wait()
                if out is None:
                    rows = slice(2 * tok * i, 2 * tok * (i + 1))
                    r.stage[n % 2] = dot(hid[rows], down_w[...], NN).astype(BF16)
                    src = r.stage.at[n % 2].reshape(2, tok, model)
                    dst = r.out_part.at[pl.ds(2 * i, 2)]
                else:
                    r.stage[n % 2, :step] = to_grad(act, rows_in, i)
                    src, dst = r.stage.at[n % 2, pl.ds(0, step)], out.at[pl.ds(i, step)]
                waiting[n % 2] = pltpu.make_async_copy(src, dst, r.stage_s.at[n % 2])
                waiting[n % 2].start()
                yield
            for one in waiting:
                one.wait()

        def fill(low, rows):
            part = hid[:, low : low + rows]
            rows_in = grad_all[...].reshape(tokens, model)
            r.reduce[0][low : low + rows] = dot(part, rows_in, TN).astype(BF16)

        down = reduce.steps(at, [None, r.grad_down] + r.reduce, fill)
        interleave(MIDDLE_ORDER, {0: chain(), 1: down, 2: products()})

    return rooms.run(body, "middle", 4, n_seq, n_fsdp)


BACK_ONE_ORDER = [2, 0, 3, 0, 1, 2, 2, 3, 2, 2, 1, 0, 2, 2, 3, 2, 0, 2, 1, 0, 2, 0, 2, 3, 0, 2, 0, 2]
BACK_ONE_ORDER += [0, 1, 2, 0, 2, 3, 0, 2, 0, 2, 0]


def back_one(n_seq, n_fsdp, da_cols, w_qkv, w_o, o_all, n1, saved, out_part, h1, grad):
    q, k, v, lse, cos, sin, pos_col, pos_row, doc_col, doc_row = saved
    (length, share), model = q.shape, w_qkv.shape[0]
    tok = length // n_seq
    rooms = Rooms()
    rooms.bring(h1=h1, q=q, k=k, v=v, lse=lse, cos=cos, sin=sin)
    rooms.take(
        VMEM, da_cols=da_cols, pos_col=pos_col, pos_row=pos_row, doc_col=doc_col, doc_row=doc_row
    )
    rooms.take(ANY, w_qkv=w_qkv, w_o=w_o, o_all=o_all, n1=n1, out_part=out_part, g_in=grad)
    rooms.give(ANY, g_out=like(grad.shape), dw_qkv=like((model, 3 * share)))
    rooms.give(
        VMEM,
        dn1_part=like((n_seq, tok, model)),
        dw_o=like((model // n_fsdp, share)),
        block_out=like((tok, model)),
    )
    o_block = like((n_fsdp, model // n_fsdp, share))
    line_o = ScatterLine(o_block, n_fsdp)
    halve = HalveSeq((n_seq, length, share), BF16, n_seq)
    line_out = ScatterLine(out_part, n_fsdp, 2, far=True)
    reduce = ReduceSeq(grad.shape, grad.dtype, n_seq)
    rooms.keep(
        line_o=line_o.scratch,
        line_out=line_out.scratch,
        mlp_out=room(tok, model, dtype=F32),
        reduce=reduce.scratch,
        dw_o_part=room(*o_block.shape),
        w_qkv_here=room(*w_qkv.shape),
        w_o_here=room(*w_o.shape),
        o_here=room(*o_all.shape),
        do_part=room(n_seq, length, share),
        halve=halve.scratch,
        do=room(length, share),
        dqkv=room(length, 3 * share),
        dk=room(length, 128, dtype=F32),
        dv=room(length, 128, dtype=F32),
        dw_stage=room(2, share, 3 * share),
        load=DMA((4,)),
        stage=DMA((2,)),
    )

    def body(at, r):
        begun = []

        def chain():
            loads = [
                pltpu.make_async_copy(a, b, r.load.at[i])
                for i, (a, b) in enumerate(
                    ((r.w_qkv, r.w_qkv_here), (r.w_o, r.w_o_here), (r.o_all, r.o_here), (r.n1, r.o_here))
                )
            ]
            for i in (1, 2, 0):
                loads[i].start()
            loads[1].wait()
            da_cols = r.da_cols
            w_qkv_here, w_o_here, o_here = r.w_qkv_here, r.w_o_here, r.o_here
            do_part = r.do_part
            for d in reversed(range(n_seq)):
                rows = pl.ds(pl.multiple_of(at.peer(d)[0] * share, share), share)
                do_part[d] = dot(da_cols[...], w_o_here[rows], NT).astype(BF16)
            exchange = halve.steps(at, do_part, r.do, r.halve)
            next(exchange)
            yield
            loads[2].wait()
            dw_o = r.dw_o_part
            per = n_fsdp // n_seq
            for j in range(n_seq):
                field = dot(o_here[j], da_cols[...], TN).astype(BF16)
                dw_o[j * per : (j + 1) * per] = field.reshape((per,) + dw_o.shape[1:])
            loads[3].start()
            running[1] = line_o.steps(at, [dw_o, r.dw_o] + r.line_o)
            yield
            r.arrive()
            begun.append(True)
            for _ in exchange:
                yield
            do = r.do
            dqkv = r.dqkv
            masking = [r.pos_col, r.pos_row, r.doc_col, r.doc_row]
            for pair in range(share // 128):
                back_pair(
                    pair, do, r.q, r.k, r.v, r.lse, r.cos, r.sin,
                    dqkv, masking, r.dk, r.dv,
                )
                yield
            loads[3].wait()
            dw_qkv, stage, stage_s = r.dw_qkv, r.dw_stage, r.stage

            def put(j):
                return pltpu.make_async_copy(
                    stage.at[j % 2], dw_qkv.at[pl.ds(j * share, share)], stage_s.at[j % 2]
                )

            for j in range(n_seq):
                if j >= 2:
                    put(j - 2).wait()
                stage[j % 2] = dot(o_here[j], dqkv[...], TN).astype(BF16)
                put(j).start()
                yield
            loads[0].wait()
            dn1_part = r.dn1_part
            for j in range(n_seq):
                rows = slice(j * share, (j + 1) * share)
                field = dot(dqkv[...], w_qkv_here[rows], NT).astype(BF16)
                for i in range(n_seq):
                    dn1_part[jnp.bitwise_xor(at.s, i), :, rows] = field[i * tok : (i + 1) * tok]
                yield
            put(n_seq - 2).wait()
            put(n_seq - 1).wait()

        def rows_out():
            yield from line_out.steps(at, [r.out_part, r.mlp_out] + r.line_out)
            while not begun:
                yield
            h1, mlp_out, block_out = r.h1, r.mlp_out, r.block_out

            def add(i, carry):
                rows = pl.ds(i * 16, 16)
                block_out[rows] = (h1[rows] + mlp_out[rows]).astype(BF16)
                return carry

            lax.fori_loop(0, tok // 16, add, 0)

        running = {
            0: chain(),
            3: rows_out(),
            2: reduce.steps(at, [r.g_in, r.g_out] + r.reduce),
        }
        interleave(BACK_ONE_ORDER, running)

    return rooms.run(body, "back_one", 2, n_seq, n_fsdp)


BACK_TWO_ORDER = [0, 2, 1, 3, 0, 2, 1, 1, 3, 2, 1, 1, 0, 2, 2, 1, 1, 2, 1, 1, 2, 0, 2, 1, 1, 0, 0, 2, 2]
BACK_TWO_ORDER += [1, 1, 1, 1, 3, 3, 0, 1, 1, 0]


def back_two(
    n_seq, n_fsdp, dn1_part, dw_qkv, dw_o, source, dh1, gain_a, gain_m_term, grad
):
    tok, model = source.shape
    rooms = Rooms()
    line = ScatterLine(dw_qkv, n_fsdp, 2, far=True)
    gain_block = like((n_fsdp, 8, model // n_fsdp), F32)
    line_gain = ScatterLine(gain_block, n_fsdp)
    scatter = HalveSeq(dn1_part.shape, BF16, n_seq)
    reduce = ReduceSeq(grad.shape, grad.dtype, n_seq)
    spread, spread_o = SpreadSeq(n_seq), SpreadSeq(n_seq)
    gather = GatherSeq(n_seq)
    rooms.take(
        VMEM, dn1_part=dn1_part, gain_a=gain_a, gain_m_term=gain_m_term,
    )
    rooms.bring(source=source, dh1=dh1)
    rooms.take(ANY, dw_qkv=dw_qkv, dw_o=dw_o, g_in=grad)
    rooms.give(
        ANY,
        g_out=like(grad.shape),
        dw_qkv_all=like((n_seq,) + dw_qkv.shape[1:]),
        dw_o_all=like((n_seq,) + dw_o.shape),
    )
    rooms.give(
        VMEM,
        grad_in=like((tok, model)),
        gains=like(gain_block.shape[1:], F32),
    )
    rooms.keep(
        line=line.scratch,
        line_gain=line_gain.scratch,
        scatter=scatter.scratch,
        reduce=reduce.scratch,
        spread=spread.scratch,
        spread_o=spread_o.scratch,
        gather=gather.scratch,
        dw_own=room(*dw_qkv.shape[1:]),
        dn1=room(tok, model, dtype=F32),
        gain_part=room(*gain_block.shape, dtype=F32),
        gain_own=room(*gain_block.shape[1:], dtype=F32),
        gain_all=room(n_seq, *gain_block.shape[1:], dtype=F32),
        gain_sum=room(8, model, dtype=F32),
    )

    def body(at, r):
        def weights():
            yield from line.steps(at, [r.dw_qkv, r.dw_own] + r.line)
            yield from spread.steps(at, [r.dw_own, r.dw_qkv_all] + r.spread)

        def rows_in():
            yield from scatter.steps(at, r.dn1_part, r.dn1, r.scatter)
            r.arrive()
            source, dh1, dn1 = r.source, r.dh1, r.dn1
            gain_a, grad_in, gain_sum = r.gain_a, r.grad_in, r.gain_sum
            gain_sum[...] = jnp.zeros_like(gain_sum)

            def norm(i, carry):
                rows = pl.ds(i * 16, 16)
                x, grad = source[rows].astype(F32), dn1[rows]
                scale = lax.rsqrt(jnp.mean(x * x, axis=-1, keepdims=True) + NORM_EPS)
                wide = dh1[rows] + norm_back(grad, x, scale, gain_a[...])
                grad_in[rows] = wide.astype(BF16)
                term = grad * x * scale
                gain_sum[...] += term[:8] + term[8:]
                return carry

            lax.fori_loop(0, tok // 16, norm, 0)
            first = jnp.sum(gain_sum[...], axis=0, keepdims=True)
            second = jnp.sum(r.gain_m_term[...], axis=0, keepdims=True)
            row = lax.broadcasted_iota(jnp.int32, gain_sum.shape, 0)
            both = jnp.where(row == 0, first, jnp.where(row == 1, second, 0.0))
            part, width = r.gain_part, model // n_fsdp
            for f in range(n_fsdp):
                part[f] = both[:, f * width : (f + 1) * width]
            yield
            yield from line_gain.steps(at, [part, r.gain_own] + r.line_gain)
            yield from gather.steps(at, [r.gain_own, r.gain_all] + r.gather)
            total = r.gain_all[0]
            for j in range(1, n_seq):
                total = total + r.gain_all[j]
            r.gains[...] = total

        running = {
            0: weights(),
            1: reduce.steps(at, [r.g_in, r.g_out] + r.reduce),
            2: rows_in(),
            3: spread_o.steps(at, [r.dw_o, r.dw_o_all] + r.spread_o),
        }
        interleave(BACK_TWO_ORDER, running)

    return rooms.run(body, "back_two", 3, n_seq, n_fsdp)


def finish_kernel(gate, up, down, qkv, o, rows_out, rows_in, gains, mlp, attn, out, back, gain):
    for c, ref in enumerate((gate, up, down)):
        mlp[c] = ref[...].astype(F32)
    n_seq, rows, share = o.shape
    for s in range(n_seq):
        at = pl.ds(s * share, share)
        for c in range(3):
            attn[:, c, at] = qkv[s, :, c * share : (c + 1) * share].astype(F32)
        attn[:, 3, at] = o[s].astype(F32)
    out[...] = rows_out[...]
    back[...] = rows_in[...]
    gain[...] = gains[...]


def grid_call(kernel, name, grid, args, in_specs, outs, out_specs, scratch=(), aliases=None):
    return pl.pallas_call(
        kernel,
        grid=grid,
        out_shape=outs,
        in_specs=in_specs,
        out_specs=out_specs,
        scratch_shapes=list(scratch),
        input_output_aliases=aliases or {},
        compiler_params=pltpu.CompilerParams(vmem_limit_bytes=62 * 2**20),
        name=name,
    )(*args)


def on_device(
    n_seq, n_fsdp,
    hidden_in, gain_attn, attn_weights, gain_mlp, mlp_weights, out_grad, block_slots, doc_ids,
):
    tok, model = hidden_in.shape[1:]
    share = model // n_seq
    start = lax.axis_index("seq") * share
    w_own = lax.dynamic_slice_in_dim(attn_weights, start, share, 2).reshape(-1, 4 * share)
    mlp_w = mlp_weights.transpose(1, 0, 2)
    a = front(
        n_seq, n_fsdp, w_own, hidden_in[0], jnp.stack([gain_attn, gain_mlp]).astype(F32), out_grad[0],
        mlp_w,
        block_slots.T, doc_ids,
    )
    tables = (a.cos, a.sin, a.pos_col, a.pos_row, a.doc_col, a.doc_row)
    w_qkv, w_o = a.w_qkv_out.reshape(model, -1), a.w_o_out.reshape(model, -1)
    m = middle(
        n_seq, n_fsdp, a.hid, a.dg, a.du, a.n2_out, a.grad_out, mlp_w, a.middle, out_grad[0], a.gain_m
    )
    b = back_one(
        n_seq, n_fsdp, m.da_cols, w_qkv, w_o, a.o_out, a.n1_out,
        (a.q, a.k, a.v, a.lse, *tables), m.out_part, a.middle, m.grads[0],
    )
    c = back_two(
        n_seq, n_fsdp, b.dn1_part, b.dw_qkv.reshape(n_fsdp, -1, 3 * share), b.dw_o,
        hidden_in[0], m.dh1, a.gain_a, m.gain, m.grads[1],
    )
    own_rows, units = b.dw_o.shape[0], c.g_out.shape[0]
    steps = 8
    u, a_rows, t = units // steps, own_rows // steps, tok // steps
    flat = pl.BlockSpec((u, model), lambda i: (i, 0))
    row = pl.BlockSpec((t, model), lambda i: (i, 0))
    whole = pl.BlockSpec(c.gains.shape, lambda i: (0, 0))
    mlp_grad, attn_grad, block_out, grad_in, gains = grid_call(
        finish_kernel,
        "finish",
        (steps,),
        (b.g_out, c.g_out, m.grad_down, c.dw_qkv_all, c.dw_o_all, b.block_out, c.grad_in, c.gains),
        [flat] * 3
        + [pl.BlockSpec((n_seq, a_rows, n * share), lambda i: (0, i, 0)) for n in (3, 1)]
        + [row, row, whole],
        [
            like((3, units, model), F32),
            like((own_rows, 4, model), F32),
            like((tok, model)),
            like((tok, model)),
            like(c.gains.shape, F32),
        ],
        [
            pl.BlockSpec((3, u, model), lambda i: (0, i, 0)),
            pl.BlockSpec((a_rows, 4, model), lambda i: (i, 0, 0)),
            row,
            row,
            whole,
        ],
    )
    mlp_grad = mlp_grad.transpose(1, 0, 2)
    return (block_out[None], grad_in[None], gains[0], attn_grad, gains[1], mlp_grad)


def solution(mesh):
    return jax.shard_map(
        functools.partial(on_device, mesh.shape["seq"], mesh.shape["fsdp"]),
        mesh=mesh,
        in_specs=(
            P("fsdp", "seq", None),
            P("fsdp"),
            P("fsdp", None, None),
            P("fsdp"),
            P("fsdp", None, None),
            P("fsdp", "seq", None),
            P(),
            P("fsdp", None),
        ),
        out_specs=(
            P("fsdp", "seq", None),
            P("fsdp", "seq", None),
            P("fsdp"),
            P("fsdp", None, None),
            P("fsdp"),
            P("fsdp", None, None),
        ),
        check_vma=False,
    )
```

```python
import functools
import math
import types

import jax
import jax.numpy as jnp
from jax import lax
from jax.experimental import pallas as pl
from jax.experimental.pallas import tpu as pltpu
from jax.sharding import PartitionSpec as P

HEAD = 64


NORM_EPS = 1e-05
ROPE_BASE = 130000.0
MASKED_OUT = -1e30
F32 = jnp.float32
BF16 = jnp.bfloat16
MESH = pl.DeviceIdType.MESH
DMA = pltpu.SemaphoreType.DMA
ANY = pl.BlockSpec(memory_space=pl.ANY)
VMEM = pl.BlockSpec(memory_space=pltpu.VMEM)


def send(src, dst, send_sem, recv_sem, device):
    return pltpu.make_async_remote_copy(
        src_ref=src,
        dst_ref=dst,
        send_sem=send_sem,
        recv_sem=recv_sem,
        device_id=device,
        device_id_type=MESH,
    )


class Place:
    def __init__(self, n_seq, n_fsdp):
        self.n_seq, self.line = n_seq, n_fsdp // 2
        self.s = lax.axis_index("seq")
        self.f = lax.axis_index("fsdp")
        self.r = lax.div(self.f, 2)
        self.c = lax.rem(self.f, 2)
        self.up = (self.s, self.f + 2)
        self.down = (self.s, self.f - 2)
        self.sister = (self.s, 2 * self.r + 1 - self.c)

    def peer(self, d):
        return (jnp.bitwise_xor(self.s, d), self.f)

    def greet(self):
        barrier = pltpu.get_barrier_semaphore()
        wrap = 2 * self.line
        partners = [
            (self.s, lax.rem(self.f + 2, wrap)),
            (self.s, lax.rem(self.f + wrap - 2, wrap)),
            self.sister,
        ]
        partners += [self.peer(d) for d in range(1, self.n_seq)]
        for partner in partners:
            pl.semaphore_signal(barrier, inc=1, device_id=partner, device_id_type=MESH)
        pl.semaphore_wait(barrier, len(partners))


class GatherLine:
    def __init__(self, n_fsdp, parts=1):
        line = n_fsdp // 2
        self.scratch = [DMA((line, parts)) for _ in range(5)] + [DMA((1,))]
        self.parts = parts

    def steps(self, at, x, o, refs, use=None):
        line_r, sis_r, up_s, down_s, sis_s, own_s = refs
        parts, line, r, c = self.parts, at.line, at.r, at.c
        rows = o.shape[1] // parts

        def cut(ref, k):
            return ref.at[pl.ds(k * rows, rows)]

        def go_up(src, b, k):
            return send(src, cut(o.at[2 * b + c], k), up_s.at[b, k], line_r.at[b, k], at.up)

        def go_down(src, b, k):
            return send(src, cut(o.at[2 * b + c], k), down_s.at[b, k], line_r.at[b, k], at.down)

        def go_sister(src, b, k):
            return send(src, cut(o.at[2 * b + c], k), sis_s.at[b, k], sis_r.at[b, k], at.sister)

        def complete(b):
            for k in range(parts):
                src = cut(o.at[2 * b + 1 - c], k)
                send(src, src, sis_s.at[b, k], sis_r.at[b, k], at.sister).wait_recv()
            if use is not None:
                use(b)

        own = pltpu.make_async_copy(x, o.at[at.f], own_s.at[0])
        own.start()
        for k in range(parts):
            src = cut(x, k)
            pl.when(r < line - 1)(lambda: go_up(src, r, k).start())
            pl.when(r > 0)(lambda: go_down(src, r, k).start())
            go_sister(src, r, k).start()
        yield
        for t in range(1, line):
            for k in range(parts):
                low, high = r - t, r + t

                @pl.when(low >= 0)
                def _():
                    src = cut(o.at[2 * low + c], k)
                    go_up(src, low, k).wait_recv()
                    pl.when(r < line - 1)(lambda: go_up(src, low, k).start())
                    go_sister(src, low, k).start()

                @pl.when(high < line)
                def _():
                    src = cut(o.at[2 * high + c], k)
                    go_down(src, high, k).wait_recv()
                    pl.when(r > 0)(lambda: go_down(src, high, k).start())
                    go_sister(src, high, k).start()

            yield
            if t == 1:
                own.wait()
                complete(r)
            else:
                pl.when(r - t + 1 >= 0)(lambda: complete(r - t + 1))
                pl.when(r + t - 1 < line)(lambda: complete(r + t - 1))
        pl.when(r - line + 1 >= 0)(lambda: complete(r - line + 1))
        pl.when(r + line - 1 < line)(lambda: complete(r + line - 1))
        yield
        for b in range(line):
            for k in range(parts):
                src = cut(x, k)
                go_sister(src, b, k).wait_send()
                pl.when((b <= r) & (r < line - 1))(lambda: go_up(src, b, k).wait_send())
                pl.when((b >= r) & (r > 0))(lambda: go_down(src, b, k).wait_send())


class ScatterLine:
    def __init__(self, part, n_fsdp, parts=1, far=False):
        line = n_fsdp // 2
        block = part.shape[1:]
        self.scratch = [
            pltpu.VMEM((line,) + block, part.dtype),
            pltpu.VMEM((line + 1,) + block, part.dtype),
        ]
        self.scratch += [DMA((line, parts)), DMA((line, parts)), DMA((line, parts))]
        self.scratch += [DMA((line + 1, parts))]
        if far:
            self.scratch += [pltpu.VMEM((line,) + block, part.dtype), DMA((line,))]
        self.parts, self.far = parts, far

    def steps(self, at, refs):
        part, o, sis, come, sis_s, sis_r, line_s, line_r = refs[:8]
        near, near_s = refs[8:] if self.far else (None, None)
        parts, line, r, c = self.parts, at.line, at.r, at.c
        rows = part.shape[1] // parts
        tile = 16 if rows % 16 == 0 else rows

        def cut(ref, k):
            return ref.at[pl.ds(k * rows, rows)]

        def to_sister(b, k):
            return send(
                cut(part.at[2 * b + 1 - c], k),
                cut(sis.at[b], k),
                sis_s.at[b, k],
                sis_r.at[b, k],
                at.sister,
            )

        def slot(b, own):
            return jnp.where(b == own, line, b)

        def go_up(b, k):
            return send(cut(sis.at[b], k), cut(come.at[b], k), line_s.at[b, k], line_r.at[b, k], at.up)

        def go_down(b, k, own):
            i = slot(b, own)
            return send(
                cut(sis.at[b], k), cut(come.at[i], k), line_s.at[b, k], line_r.at[i, k], at.down
            )

        def add(b, k, came, out=None):
            def body(i, carry):
                at_rows = pl.ds(k * rows + i * tile, tile)
                own = near[b, at_rows] if self.far else part[2 * b + c, at_rows]
                total = own.astype(F32) + sis[b, at_rows].astype(F32)
                for j in came:
                    total = total + come[j, at_rows].astype(F32)
                if out is None:
                    sis[b, at_rows] = total.astype(sis.dtype)
                else:
                    out[at_rows] = total.astype(out.dtype)
                return carry

            lax.fori_loop(0, rows // tile, body, 0)

        order = []
        for j in range(line):
            order += [b for b in (line - 1 - j, j) if b not in order]
        for b in order:
            for k in range(parts):
                to_sister(b, k).start()
        if self.far:
            loads = [
                pltpu.make_async_copy(part.at[2 * b + c], near.at[b], near_s.at[b])
                for b in range(line)
            ]
            for one in loads:
                one.start()
            for one in loads:
                one.wait()
        yield
        for t in range(line - 1):
            for k in range(parts):
                high, low = line - 1 - t + r, t - (line - 1 - r)

                @pl.when(high < line)
                def _():
                    to_sister(high, k).wait_recv()

                    @pl.when(r > 0)
                    def _():
                        go_up(high, k).wait_recv()
                        add(high, k, [high])

                    pl.when(r == 0)(lambda: add(high, k, []))
                    go_up(high, k).start()

                @pl.when(low >= 0)
                def _():
                    to_sister(low, k).wait_recv()

                    @pl.when(r < line - 1)
                    def _():
                        go_down(low, k, -1).wait_recv()
                        add(low, k, [low])

                    pl.when(r == line - 1)(lambda: add(low, k, []))
                    go_down(low, k, r - 1).start()

            yield
        for k in range(parts):
            to_sister(r, k).wait_recv()
            pl.when(r > 0)(lambda: go_up(r, k).wait_recv())
            pl.when(r < line - 1)(lambda: go_down(r, k, r).wait_recv())
            pl.when(r == 0)(lambda: add(r, k, [line], o))
            pl.when(r == line - 1)(lambda: add(r, k, [r], o))
            pl.when((r > 0) & (r < line - 1))(lambda: add(r, k, [r, line], o))
        yield
        for b in range(line):
            for k in range(parts):
                to_sister(b, k).wait_send()
                pl.when(b != r)(lambda: go_up(b, k).wait_send())


class GatherSeq:
    def __init__(self, n_seq):
        self.scratch = [DMA((n_seq,)), DMA((n_seq,))]

    def steps(self, at, refs):
        x, o, s_sem, r_sem = refs

        def go(d):
            return send(x, o.at[at.s], s_sem.at[d], r_sem.at[d], at.peer(d))

        for d in reversed(range(1, at.n_seq)):
            go(d).start()
        own = pltpu.make_async_copy(x, o.at[at.s], s_sem.at[0])
        own.start()
        yield
        own.wait()
        for d in range(1, at.n_seq):
            go(d).wait()


class HalveSeq:
    def __init__(self, shape, dtype, n_seq):
        n, rows, cols = shape
        bits = n_seq.bit_length() - 1
        self.half = rows // 2
        self.orders = [[(i + p) % bits for i in range(bits)] for p in range(2)]
        self.scratch = [
            pltpu.VMEM((2, n - 1, self.half, cols), dtype), DMA((2, n - 1)), DMA((2, n - 1))
        ]

    def masks(self, p, i):
        out = [0]
        for b in self.orders[p][i + 1 :]:
            out += [m | (1 << b) for m in out]
        return out

    def slot(self, p, i, u):
        return sum(len(self.masks(p, j)) for j in range(i)) + self.masks(p, i).index(u)

    def steps(self, at, part, o, refs):
        land, s_sem, r_sem = refs
        half, bits = self.half, len(self.orders[0])
        tile = 16 if half % 16 == 0 else half

        def go(p, i, u):
            b = 1 << self.orders[p][i]
            if i == 0:
                src = part.at[b | u, pl.ds(p * half, half)]
            else:
                src = land.at[p, self.slot(p, 0, b | u)]
            n = self.slot(p, i, u)
            return send(src, land.at[p, n], s_sem.at[p, n], r_sem.at[p, n], at.peer(b))

        def add(p, u, upto, out, first):
            def body(k, carry):
                rows = pl.ds(pl.multiple_of(k * tile, tile), tile)
                total = part[u, pl.ds(pl.multiple_of(p * half + k * tile, tile), tile)].astype(F32)
                for i in range(upto):
                    total = total + land[p, self.slot(p, i, u), rows].astype(F32)
                out[pl.ds(pl.multiple_of(first + k * tile, tile), tile)] = total.astype(out.dtype)
                return carry

            lax.fori_loop(0, half // tile, body, 0)

        for p in range(2):
            for u in self.masks(p, 0):
                go(p, 0, u).start()
        yield
        for i in range(bits):
            for p in range(2):
                for u in self.masks(p, i):
                    go(p, i, u).wait_recv()
                if i + 1 < bits:
                    b = 1 << self.orders[p][i + 1]
                    for u in self.masks(p, i + 1):
                        add(p, b | u, i + 1, land.at[p, self.slot(p, 0, b | u)], 0)
                        go(p, i + 1, u).start()
                else:
                    add(p, 0, bits, o, p * half)
            yield
        for p in range(2):
            for i in range(bits):
                for u in self.masks(p, i):
                    go(p, i, u).wait_send()


class ReduceSeq:
    def __init__(self, shape, dtype, n_seq, parts=4):
        rows, cols = shape
        self.bits, self.parts = n_seq.bit_length() - 1, parts
        self.rows = rows // parts
        self.room = self.rows - (self.rows >> self.bits)
        self.scratch = [
            pltpu.VMEM(shape, dtype),
            pltpu.VMEM((parts * self.room, cols), dtype),
            DMA((parts,)),
            DMA((parts, self.bits)),
            DMA((parts, self.bits)),
            DMA((parts, n_seq)),
            DMA((parts, n_seq)),
            DMA((parts,)),
        ]

    def steps(self, at, refs, fill=None):
        g_in, o, g, land, load_s, rs_s, rs_r, ag_s, ag_r, own_s = refs
        bits, parts = self.bits, range(self.parts)
        orders = [[(i + p) % bits for i in range(bits)] for p in parts]
        mult = self.rows >> bits

        def bit(t, b):
            return jnp.bitwise_and(lax.shift_right_logical(t, b), 1)

        def base(p, t, n):
            low = p * self.rows
            for i in range(n):
                low = low + bit(t, orders[p][i]) * (self.rows >> (i + 1))
            return pl.multiple_of(low, mult)

        def load(p):
            part = pl.ds(p * self.rows, self.rows)
            return pltpu.make_async_copy(g_in.at[part], g.at[part], load_s.at[p])

        def slot(p, i):
            return p * self.room + sum(self.rows >> (j + 1) for j in range(i))

        def halve(p, i):
            size = self.rows >> (i + 1)
            other = jnp.bitwise_xor(at.s, 1 << orders[p][i])
            return send(
                g.at[pl.ds(base(p, other, i + 1), size)],
                land.at[pl.ds(slot(p, i), size)],
                rs_s.at[p, i],
                rs_r.at[p, i],
                (other, at.f),
            )

        def add(p, i):
            size = self.rows >> (i + 1)
            low, first = base(p, at.s, i + 1), slot(p, i)

            def body(j, carry):
                mine = pl.ds(pl.multiple_of(low + j * 16, 16), 16)
                came = pl.ds(pl.multiple_of(first + j * 16, 16), 16)
                total = g[mine].astype(F32) + land[came].astype(F32)
                g[mine] = total.astype(g.dtype)
                return carry

            lax.fori_loop(0, size // 16, body, 0)

        def masks(p, j):
            out = [0]
            for i in range(j):
                out += [m | (1 << orders[p][bits - 1 - i]) for m in out]
            return out

        def double(p, j, mask):
            b = orders[p][bits - 1 - j]
            piece = pl.ds(base(p, jnp.bitwise_xor(at.s, mask), bits), mult)
            src = g.at[piece] if mask == 0 else o.at[piece]
            i = (1 << b) | mask
            return send(
                src, o.at[piece], ag_s.at[p, i], ag_r.at[p, i], (jnp.bitwise_xor(at.s, 1 << b), at.f)
            )

        def arrive(p, j, mask):
            b = orders[p][bits - 1 - j]
            piece = pl.ds(base(p, jnp.bitwise_xor(at.s, (1 << b) | mask), bits), mult)
            i = (1 << b) | mask
            return send(
                o.at[piece], o.at[piece], ag_s.at[p, i], ag_r.at[p, i],
                (jnp.bitwise_xor(at.s, 1 << b), at.f),
            )

        def own(p):
            piece = pl.ds(base(p, at.s, bits), mult)
            return pltpu.make_async_copy(g.at[piece], o.at[piece], own_s.at[p])

        if g_in is not None:
            for p in parts:
                load(p).start()
        for p in parts:
            if g_in is not None:
                load(p).wait()
            if fill is not None:
                fill(p * self.rows, self.rows)
            halve(p, 0).start()
        yield
        for i in range(bits):
            for p in parts:
                halve(p, i).wait_recv()
                add(p, i)
                if i + 1 < bits:
                    halve(p, i + 1).start()
                else:
                    for j in range(bits):
                        double(p, j, 0).start()
                    own(p).start()
                yield
        for j in range(bits):
            for p in parts:
                for mask in masks(p, j):
                    arrive(p, j, mask).wait_recv()
                    came = (1 << orders[p][bits - 1 - j]) | mask
                    for later in range(j + 1, bits):
                        double(p, later, came).start()
                yield
        for p in parts:
            own(p).wait()
            for i in range(bits):
                halve(p, i).wait_send()
            for j in range(bits):
                for mask in masks(p, j):
                    double(p, j, mask).wait_send()


class SpreadSeq:
    def __init__(self, n_seq):
        self.bits = n_seq.bit_length() - 1
        self.scratch = [DMA((2, n_seq)), DMA((2, n_seq)), DMA((1,))]

    def steps(self, at, refs):
        x, o, s_sem, r_sem, own_s = refs
        bits, half = self.bits, x.shape[0] // 2
        orders = [[(i + p) % bits for i in range(bits)] for p in range(2)]

        def known(p, j):
            out = [0]
            for i in range(j):
                out += [m | (1 << orders[p][i]) for m in out]
            return out

        def piece(p, mask):
            return o.at[jnp.bitwise_xor(at.s, mask), pl.ds(p * half, half)]

        def go(p, j, mask):
            b = 1 << orders[p][j]
            src = x.at[pl.ds(p * half, half)] if mask == 0 else piece(p, mask)
            i = b | mask
            return send(src, piece(p, mask), s_sem.at[p, i], r_sem.at[p, i], at.peer(b))

        def arrive(p, j, mask):
            b = 1 << orders[p][j]
            i = b | mask
            here = piece(p, i)
            return send(here, here, s_sem.at[p, i], r_sem.at[p, i], at.peer(b))

        for p in range(2):
            for j in range(bits):
                go(p, j, 0).start()
        own = pltpu.make_async_copy(x, o.at[at.s], own_s.at[0])
        own.start()
        yield
        for j in range(bits):
            for p in range(2):
                for mask in known(p, j):
                    arrive(p, j, mask).wait_recv()
                    for later in range(j + 1, bits):
                        go(p, later, (1 << orders[p][j]) | mask).start()
            yield
        own.wait()
        for j in range(bits):
            for p in range(2):
                for mask in known(p, j):
                    go(p, j, mask).wait_send()


def interleave(order, running):
    for name in order:
        if name in running and next(running[name], END) is END:
            del running[name]
    while running:
        for name in list(running):
            if next(running[name], END) is END:
                del running[name]


END = object()


class Rooms:
    def __init__(self):
        self.args, self.in_specs, self.outs, self.out_specs, self.scratch = [], [], [], [], []
        self.names = ([], [], [])
        self.brought, self.posted = [], []

    def note(self, group, name, x):
        many = isinstance(x, (list, tuple))
        self.names[group].append((name, len(x) if many else None))
        return list(x) if many else [x]

    def take(self, spec, **arrays):
        for name, x in arrays.items():
            new = self.note(0, name, x)
            self.args += new
            self.in_specs += [spec] * len(new)

    def give(self, spec, **shapes):
        for name, x in shapes.items():
            new = self.note(1, name, x)
            self.outs += new
            self.out_specs += [spec] * len(new)

    def keep(self, **kinds):
        for name, x in kinds.items():
            self.scratch += self.note(2, name, x)

    def bring(self, **arrays):
        names = list(arrays)
        self.take(ANY, **{far(n): x for n, x in arrays.items()})
        self.keep(**{n: pltpu.VMEM(x.shape, x.dtype) for n, x in arrays.items()})
        self.brought = names

    def post(self, **shapes):
        self.give(ANY, **{far(n): x for n, x in shapes.items()})
        self.keep(**{n: pltpu.VMEM(x.shape, x.dtype) for n, x in shapes.items()})
        self.posted = list(shapes)

    def bind(self, refs, groups):
        table, refs = types.SimpleNamespace(), list(refs)
        for group in groups:
            for name, many in self.names[group]:
                count = 1 if many is None else many
                mine, refs = refs[:count], refs[count:]
                setattr(table, name, mine[0] if many is None else mine)
        return table

    def run(self, body, name, collective_id, n_seq, n_fsdp):
        if self.brought:
            self.keep(brought_s=DMA((len(self.brought),)))
        if self.posted:
            self.keep(posted_s=DMA((len(self.posted),)))

        def kernel(*refs):
            at = Place(n_seq, n_fsdp)
            r = self.bind(refs, (0, 1, 2))
            loads = [
                pltpu.make_async_copy(getattr(r, far(n)), getattr(r, n), r.brought_s.at[i])
                for i, n in enumerate(self.brought)
            ]
            stores = [
                pltpu.make_async_copy(getattr(r, n), getattr(r, far(n)), r.posted_s.at[i])
                for i, n in enumerate(self.posted)
            ]
            for one in loads:
                one.start()

            def arrive():
                for one in loads:
                    one.wait()

            def leave(*mine):
                for n, one in zip(self.posted, stores):
                    if any(getattr(r, n) is ref for ref in mine):
                        one.start()

            r.arrive, r.leave = arrive, leave
            at.greet()
            body(at, r)
            for one in stores:
                one.wait()

        out = pl.pallas_call(
            kernel,
            out_shape=self.outs,
            in_specs=self.in_specs,
            out_specs=self.out_specs,
            scratch_shapes=self.scratch,
            compiler_params=pltpu.CompilerParams(
                collective_id=collective_id, has_side_effects=True, vmem_limit_bytes=62 * 2**20
            ),
            name=name,
        )(*self.args)
        results = self.bind(out, (1,))
        for n in self.posted:
            setattr(results, n, getattr(results, far(n)))
        return results


def far(name):
    return name + "_far"


def like(shape, dtype=BF16):
    return jax.ShapeDtypeStruct(tuple(shape), dtype)


def room(*shape, dtype=BF16):
    return pltpu.VMEM(shape, dtype)


def dot(a, b, dims):
    return lax.dot_general(a, b, (dims, ((), ())), preferred_element_type=F32)


NN = ((1,), (0,))
NT = ((1,), (1,))
TN = ((0,), (0,))


def turned(x, cos, sin):
    lane = lax.broadcasted_iota(jnp.int32, x.shape, 1)
    other = jnp.where(lane % HEAD < HEAD // 2, pltpu.roll(x, 96, 1), pltpu.roll(x, 32, 1))
    return x * cos + other * sin


def head_masks():
    lane = lax.broadcasted_iota(jnp.int32, (1, 128), 1)
    first = (lane < HEAD).astype(F32)
    return first, 1.0 - first


def back_pair(pair, do, q, k, v, lse, cos, sin, dqkv, masking, dk, dv):
    pos_col, pos_row, doc_col, doc_row = masking
    length, share = q.shape
    span = 256
    masks = head_masks()
    lane = lax.broadcasted_iota(jnp.int32, (span, 128), 1)
    lanes = slice(pair * 128, pair * 128 + 128)
    dk[...] = jnp.zeros_like(dk)
    dv[...] = jnp.zeros_like(dv)

    def one_span(i, carry):
        rows = pl.ds(pl.multiple_of(i * span, span), span)
        allowed = (pos_row[...] <= pos_col[rows]) & (doc_row[...] == doc_col[rows])
        bias = jnp.where(allowed, 0.0, MASKED_OUT)
        dq = jnp.zeros((span, 128), F32)
        for h in range(2):
            mask = masks[h].astype(BF16)
            field, grad = q[rows, lanes] * mask, do[rows, lanes] * mask
            log_total = jnp.sum(
                jnp.where(lane == 2 * pair + h, lse[rows], 0.0), axis=-1, keepdims=True
            )
            z = dot(field, k[:, lanes], NT) * 0.125 + bias
            prob = jnp.exp(z - log_total)
            dp = dot(grad, v[:, lanes], NT)
            delta = jnp.sum(prob * dp, axis=-1, keepdims=True)
            dz = (prob * (dp - delta)).astype(BF16)
            dq = dq + dot(dz, k[:, lanes], NN) * masks[h]
            dk[...] += dot(dz, field, TN)
            dv[...] += dot(prob.astype(BF16), grad, TN)
        dqkv[rows, lanes] = turned(dq * 0.125, cos[rows], -sin[rows]).astype(BF16)
        return carry

    lax.fori_loop(0, length // span, one_span, 0)
    at = share + pair * 128
    dqkv[:, at : at + 128] = turned(dk[...] * 0.125, cos[...], -sin[...]).astype(BF16)
    at = 2 * share + pair * 128
    dqkv[:, at : at + 128] = dv[...].astype(BF16)


def norm_back(grad_normed, value, scale, gain):
    weighted = grad_normed * gain
    inner_mean = jnp.mean(weighted * value, axis=-1, keepdims=True)
    return scale * (weighted - value * scale * scale * inner_mean)


def scale_of(value):
    return lax.rsqrt(jnp.mean(value * value, axis=-1, keepdims=True) + NORM_EPS)


def fill_tables(slots, docs, r):
    length = docs.shape[1]
    block = length // (2 * slots.shape[1])

    def place(shape, axis):
        i = lax.broadcasted_iota(jnp.int32, shape, axis)
        slot = jnp.zeros(shape, jnp.int32)
        for j in range(2 * slots.shape[1]):
            slot = jnp.where(i // block == j, slots[j % 2, j // 2], slot)
        return slot * block + i % block

    r.pos_col[...] = place((length, 1), 0)
    r.pos_row[...] = place((1, length), 1)
    lane = lax.broadcasted_iota(jnp.int32, (1, 128), 1)
    half = HEAD // 2
    steps = (lane % half).astype(F32) / half
    freqs = jnp.exp(steps * -math.log(ROPE_BASE))
    sign = jnp.where(lane % HEAD < half, -1.0, 1.0)
    r.doc_row[...] = jnp.zeros((1, length), jnp.int32)

    def body(i, carry):
        rows = pl.ds(pl.multiple_of(i * 128, 128), 128)
        pos = r.pos_col[rows]
        turn = pos.astype(F32) * freqs
        r.cos[rows] = jnp.cos(turn)
        r.sin[rows] = jnp.sin(turn) * sign
        at = lax.broadcasted_iota(jnp.int32, (128, length), 1)
        own = jnp.sum(jnp.where(at == pos, docs[...], 0), axis=1, keepdims=True)
        r.doc_col[rows] = own
        here = lax.broadcasted_iota(jnp.int32, (128, length), 0) + i * 128
        r.doc_row[...] += jnp.sum(jnp.where(at == here, own, 0), axis=0, keepdims=True)
        return carry

    lax.fori_loop(0, length // 128, body, 0)


FRONT_ORDER = [0, 0, 0, 1, 0, 0, 1, 0, 1, 0, 1, 0, 1, 1, 2, 0, 0, 2, 0, 0, 0, 0, 2, 0, 2, 0]


def front(n_seq, n_fsdp, w_own, hidden, own_gains, out_grad, mlp_w, slots, docs):
    tok, model = hidden.shape
    length, share = n_seq * tok, w_own.shape[1] // 4
    line, rows_f, units = n_fsdp // 2, w_own.shape[0], mlp_w.shape[1]
    qkv_shape, o_shape = (n_fsdp, rows_f, 3 * share), (n_fsdp, rows_f, share)
    per = n_fsdp // n_seq
    n_pairs = share // 128
    span = 256
    get_w, get_o = GatherLine(n_fsdp, 2), GatherLine(n_fsdp)
    get_gain, get_grad, get_n2 = GatherLine(n_fsdp), GatherLine(n_fsdp, 2), GatherLine(n_fsdp, 2)
    get_x = GatherSeq(n_seq)
    rooms = Rooms()
    rooms.take(VMEM, hidden=hidden, own_gains=own_gains, docs=docs)
    rooms.take(pl.BlockSpec(memory_space=pltpu.SMEM), slots=slots)
    rooms.take(ANY, w_own=w_own, out_grad=out_grad, mlp_w=mlp_w)
    rooms.give(
        ANY,
        w_qkv_out=like(qkv_shape),
        w_o_out=like(o_shape),
        n1_out=like((n_seq, length, share)),
        o_out=like((n_seq, length, share)),
        n2_out=like((n_fsdp, tok, model)),
        grad_out=like((n_fsdp, tok, model)),
        hid=like((n_fsdp * tok, units)),
        dg=like((n_fsdp * tok, units)),
        du=like((n_fsdp * tok, units)),
    )
    rooms.post(
        q=like((length, share)),
        k=like((length, share)),
        v=like((length, share)),
        lse=like((length, 128), F32),
        middle=like((tok, model), F32),
        cos=like((length, 128), F32),
        sin=like((length, 128), F32),
    )
    rooms.give(
        VMEM,
        gain_a=like((1, model), F32),
        gain_m=like((1, model), F32),
        pos_col=like((length, 1), jnp.int32),
        pos_row=like((1, length), jnp.int32),
        doc_col=like((length, 1), jnp.int32),
        doc_row=like((1, length), jnp.int32),
    )
    rooms.keep(
        gains=room(32, rows_f),
        get_w=get_w.scratch, get_o=get_o.scratch, get_gain=get_gain.scratch,
        get_grad=get_grad.scratch, get_n2=get_n2.scratch, get_x=get_x.scratch,
        w_qkv_all=room(*qkv_shape),
        w_o_all=room(*o_shape),
        gains_all=room(n_fsdp, 32, rows_f),
        x_all=room(n_seq, tok, model),
        n1=room(n_fsdp, length, rows_f),
        o_all=room(n_seq, length, share),
        y_total=room(length, share, dtype=F32),
        y=room(n_seq, tok, share),
        y_land=room(n_seq, tok, share),
        n2=room(tok, model),
        n2_all=room(n_fsdp, tok, model),
        grad_all=room(n_fsdp, tok, model),
        w_gate=room(units, model),
        w_up=room(units, model),
        w_down=room(units, model),
        act=room(n_fsdp * tok, units, dtype=F32),
        stage=room(line, 3, 2 * tok, units),
        load=DMA((3,)),
        save=DMA((6 + n_fsdp,)),
        stage_s=DMA((line, 3)),
        o_s=DMA((n_pairs, n_seq)),
        o_r=DMA((n_pairs, n_seq)),
        y_s=DMA((n_seq,)),
        y_r=DMA((n_seq,)),
    )

    def body(at, r):
        loads = [
            pltpu.make_async_copy(r.mlp_w.at[i], w, r.load.at[i])
            for i, w in enumerate((r.w_gate, r.w_up, r.w_down))
        ]
        saves = []
        w_qkv, w_o = r.w_own.at[:, pl.ds(0, 3 * share)], r.w_own.at[:, pl.ds(3 * share, share)]

        def save(src, dst):
            saves.append(pltpu.make_async_copy(src, dst, r.save.at[len(saves)]))
            saves[-1].start()

        def total(c, rows, cols):
            low, left = (c // 2) * length, (c % 2) * share
            return (
                slice(low + rows.start, low + rows.stop), slice(left + cols.start, left + cols.stop)
            )

        def project(b):
            for f in (2 * b, 2 * b + 1):
                for c in range(3):
                    weights = r.w_qkv_all[f, :, c * share : (c + 1) * share]
                    for i in range(0, length, span):
                        part = dot(r.n1[f, i : i + span], weights, NN)
                        r.act[total(c, slice(i, i + span), slice(0, share))] += part

        def grad_of(b):
            rows = pl.ds(pl.multiple_of(2 * tok * b, 2 * tok), 2 * tok)
            grad = r.grad_all[pl.ds(2 * b, 2)].reshape(2 * tok, model)
            r.act[rows] = dot(grad, r.w_down[...], NT)

        def stored(b, k):
            rows = pl.ds(pl.multiple_of(2 * tok * b, 2 * tok), 2 * tok)
            return pltpu.make_async_copy(
                r.stage.at[b, k], (r.hid, r.dg, r.du)[k].at[rows], r.stage_s.at[b, k]
            )

        def activate(b):
            rows = pl.ds(pl.multiple_of(2 * tok * b, 2 * tok), 2 * tok)
            n2 = r.n2_all[pl.ds(2 * b, 2)].reshape(2 * tok, model)
            gate = dot(n2, r.w_gate[...], NT)
            up = dot(n2, r.w_up[...], NT)
            grad = r.act[rows]
            sigma = jax.nn.sigmoid(gate)
            silu = gate * sigma
            r.stage[b, 0] = (silu * up).astype(BF16)
            r.stage[b, 1] = (grad * up * sigma * (1.0 + gate * (1.0 - sigma))).astype(BF16)
            r.stage[b, 2] = (grad * silu).astype(BF16)
            for k in range(3):
                stored(b, k).start()

        def attend(pair):
            lanes = slice(pair * 128, pair * 128 + 128)
            masks = head_masks()
            lane = lax.broadcasted_iota(jnp.int32, (span, 128), 1)

            def one_span(i, carry):
                rows = pl.ds(pl.multiple_of(i * span, span), span)
                allowed = (r.pos_row[...] <= r.pos_col[rows]) & (r.doc_row[...] == r.doc_col[rows])
                bias = jnp.where(allowed, 0.0, MASKED_OUT)
                parts = []
                for h in range(2):
                    field = r.q[rows, lanes] * masks[h].astype(BF16)
                    z = dot(field, r.k[:, lanes], NT) * 0.125 + bias
                    top = jnp.max(z, axis=-1, keepdims=True)
                    e = jnp.exp(z - top)
                    sum_e = jnp.sum(e, axis=-1, keepdims=True)
                    prob = (e * (1.0 / sum_e)).astype(BF16)
                    parts.append(dot(prob, r.v[:, lanes], NN) * masks[h])
                    here = lane == 2 * pair + h
                    r.lse[rows] = jnp.where(here, top + jnp.log(sum_e), r.lse[rows])
                r.o_all[at.s, rows, lanes] = (parts[0] + parts[1]).astype(BF16)
                return carry

            lax.fori_loop(0, length // span, one_span, 0)

        def go_o(pair, d, owner):
            here = r.o_all.at[owner, :, pl.ds(pair * 128, 128)]
            return send(here, here, r.o_s.at[pair, d], r.o_r.at[pair, d], at.peer(d))

        def go_y(d):
            peer = at.peer(d)
            return send(r.y.at[peer[0]], r.y_land.at[d], r.y_s.at[d], r.y_r.at[d], peer)

        def chain():
            weights = get_w.steps(at, w_qkv, r.w_qkv_all, r.get_w, project)
            next(weights)
            rows_in = get_x.steps(at, [r.hidden, r.x_all] + r.get_x)
            next(rows_in)
            for one in loads:
                one.start()
            r.act[...] = jnp.zeros_like(r.act)
            for i in range(2):
                gain = r.own_gains[i : i + 1]
                r.gains[16 * i : 16 * i + 16] = jnp.broadcast_to(gain, (16, rows_f)).astype(BF16)
            gain_steps = get_gain.steps(at, r.gains, r.gains_all, r.get_gain)
            next(gain_steps)
            fill_tables(r.slots, r.docs, r)
            r.leave(r.cos, r.sin)
            for _ in gain_steps:
                pass
            for f in range(n_fsdp):
                cols = slice(f * rows_f, (f + 1) * rows_f)
                r.gain_a[:, cols] = r.gains_all[f, 0:1].astype(F32)
                r.gain_m[:, cols] = r.gains_all[f, 16:17].astype(F32)
            next(weights)
            for _ in rows_in:
                pass
            r.lse[...] = jnp.zeros_like(r.lse)

            def norm(i, carry):
                j, k = i // (tok // 16), i % (tok // 16)
                x = r.x_all[j, pl.ds(pl.multiple_of(k * 16, 16), 16)].astype(F32)
                normed = (x * scale_of(x) * r.gain_a[...]).astype(BF16)
                rows = pl.ds(pl.multiple_of(i * 16, 16), 16)
                for f in range(n_fsdp):
                    r.n1[f, rows] = normed[:, f * rows_f : (f + 1) * rows_f]
                return carry

            lax.fori_loop(0, length // 16, norm, 0)
            for f in range(n_fsdp):
                save(r.n1.at[f], r.n1_out.at[f // per, :, pl.ds((f % per) * rows_f, rows_f)])
            yield
            for _ in weights:
                yield
            save(r.w_qkv_all, r.w_qkv_out)
            for c, out in enumerate((r.q, r.k)):
                for j in range(0, share, 128):
                    field = r.act[total(c, slice(0, length), slice(j, j + 128))]
                    out[:, j : j + 128] = turned(field, r.cos[...], r.sin[...]).astype(BF16)
            r.v[...] = r.act[total(2, slice(0, length), slice(0, share))].astype(BF16)
            r.leave(r.q, r.k, r.v)
            projected.append(True)
            yield
            for pair in range(n_pairs):
                attend(pair)
                for d in reversed(range(1, n_seq)):
                    go_o(pair, d, at.s).start()
                yield
            r.leave(r.lse)
            for _ in out_weights:
                pass
            for d in range(n_seq):
                owner = at.peer(d)[0]
                if d:
                    for pair in range(n_pairs):
                        go_o(pair, d, owner).wait_recv()
                for h in range(per):
                    part = dot(
                        r.o_all[owner, :, h * rows_f : (h + 1) * rows_f],
                        r.w_o_all[owner * per + h],
                        NN,
                    )
                    if d == 0 and h == 0:
                        r.y_total[...] = part
                    else:
                        r.y_total[...] += part
                yield
            for j in range(n_seq):
                r.y[j] = r.y_total[j * tok : (j + 1) * tok].astype(BF16)
            for d in reversed(range(1, n_seq)):
                go_y(d).start()
            save(r.o_all, r.o_out)
            save(r.w_o_all, r.w_o_out)
            r.y_land[0] = r.y[at.s]
            yield
            for d in range(1, n_seq):
                go_y(d).wait()

            def middle(i, carry):
                rows = pl.ds(pl.multiple_of(i * 16, 16), 16)
                for j in range(n_seq):
                    cols = slice(j * share, (j + 1) * share)
                    branch = r.y_land[jnp.bitwise_xor(at.s, j), rows].astype(F32)
                    r.middle[rows, cols] = r.hidden[rows, cols].astype(F32) + branch
                h = r.middle[rows]
                r.n2[rows] = (h * scale_of(h) * r.gain_m[...]).astype(BF16)
                return carry

            lax.fori_loop(0, tok // 16, middle, 0)
            r.leave(r.middle)
            yield
            tokens = get_n2.steps(at, r.n2, r.n2_all, r.get_n2, activate)
            next(tokens)
            yield
            next(tokens)
            for _ in grads:
                pass
            for one in loads[:2]:
                one.wait()
            for _ in tokens:
                yield

        def cotangents():
            blocks = get_grad.steps(at, r.out_grad, r.grad_all, r.get_grad, grad_of)
            next(blocks)
            yield
            next(blocks)
            yield
            while not projected:
                yield
            loads[2].wait()
            for _ in blocks:
                yield
            save(r.grad_all, r.grad_out)

        projected = []
        out_weights = get_o.steps(at, w_o, r.w_o_all, r.get_o)
        grads = cotangents()
        interleave(FRONT_ORDER, {0: chain(), 1: out_weights, 2: grads})
        for pair in range(n_pairs):
            for d in range(1, n_seq):
                go_o(pair, d, at.s).wait_send()
        save(r.n2_all, r.n2_out)
        for b in range(line):
            for k in range(3):
                stored(b, k).wait()
        for one in saves:
            one.wait()

    return rooms.run(body, "front", 1, n_seq, n_fsdp)


MIDDLE_ORDER = [0, 0, 1, 1, 2, 0, 1, 1, 2, 0, 1, 1, 2, 0, 1, 1, 2, 0, 1, 1, 2, 0, 1, 1, 2, 2, 2, 2, 2, 2]
MIDDLE_ORDER += [2]


def middle(n_seq, n_fsdp, hid, dg, du, n2_all, grad_all, mlp_w, h1, out_grad, gain_m):
    tok, model = h1.shape
    tokens, units = hid.shape
    share, length, line = model // n_seq, n_seq * tok, n_fsdp // 2
    step = min(256, units)
    rooms = Rooms()
    rooms.bring(h1=h1, out_grad=out_grad)
    rooms.take(VMEM, gain_m=gain_m)
    rooms.take(ANY, far=[hid, grad_all, dg, du, n2_all], mlp_w=mlp_w)
    rooms.give(
        ANY,
        grad_down=like((units, model)),
        grads=[like((units, model))] * 2,
        out_part=like((n_fsdp, tok, model)),
    )
    rooms.give(
        VMEM, dh1=like((tok, model), F32), gain=like((8, model), F32), da_cols=like((length, share))
    )
    scatter = ScatterLine(like((n_fsdp, tok, model)), n_fsdp, 2)
    reduce = ReduceSeq((units, model), BF16, n_seq)
    rooms.keep(
        scatter=scatter.scratch,
        reduce=reduce.scratch,
        near=[room(*x.shape) for x in (hid, grad_all, dg, du, n2_all)],
        weights=[room(units, model)] * 3,
        dn2_part=room(n_fsdp, tok, model),
        dn2=room(tok, model, dtype=F32),
        da=room(tok, model),
        stage=room(2, 2 * tok, model),
        load=DMA((8,)),
        stage_s=DMA((2,)),
        swap=[DMA((n_seq,)), DMA((n_seq,))],
    )

    def body(at, r):
        hid, grad_all, dg, du, n2_all = r.near
        gate_w, up_w, down_w = r.weights
        loads = [
            pltpu.make_async_copy(a, b, r.load.at[i])
            for i, (a, b) in enumerate(
                list(zip(r.far, r.near)) + [(r.mlp_w.at[i], w) for i, w in enumerate(r.weights)]
            )
        ]

        def ready(*which):
            for i in which:
                loads[i].wait()

        def to_grad(act, rows_in, i):
            return dot(act[:, i : i + step], rows_in[...].reshape(tokens, model), TN).astype(BF16)

        def chain():
            for i in (0, 1, 2, 3, 5, 6, 4, 7):
                loads[i].start()
            ready(0, 1)
            next(down)
            yield
            ready(2, 3, 5, 6)
            for b in range(line):
                rows = slice(2 * tok * b, 2 * tok * (b + 1))
                part = dot(dg[rows], gate_w[...], NN) + dot(du[rows], up_w[...], NN)
                r.dn2_part[2 * b : 2 * b + 2] = part.astype(BF16).reshape(2, tok, model)
            yield from scatter.steps(at, [r.dn2_part, r.dn2] + r.scatter)
            r.arrive()
            h1, out_grad, gain_m = r.h1, r.out_grad, r.gain_m
            dn2, dh1, da, gain = r.dn2, r.dh1, r.da, r.gain
            gain[...] = jnp.zeros_like(gain)

            def norm(i, carry):
                rows = pl.ds(i * 16, 16)
                h, grad = h1[rows], dn2[rows]
                scale = lax.rsqrt(jnp.mean(h * h, axis=-1, keepdims=True) + NORM_EPS)
                wide = out_grad[rows].astype(F32) + norm_back(grad, h, scale, gain_m[...])
                dh1[rows] = wide
                da[rows] = wide.astype(BF16)
                term = grad * h * scale
                gain[...] += term[:8] + term[8:]
                return carry

            lax.fori_loop(0, tok // 16, norm, 0)
            da_cols = r.da_cols
            swap_s, swap_r = r.swap

            def swap(d):
                peer = at.peer(d)
                cols = pl.ds(pl.multiple_of(peer[0] * share, 128), share)
                rows = pl.ds(pl.multiple_of(at.s * tok, tok), tok)
                return send(da.at[:, cols], da_cols.at[rows], swap_s.at[d], swap_r.at[d], peer)

            for d in reversed(range(1, n_seq)):
                swap(d).start()
            cols = pl.ds(pl.multiple_of(at.s * share, 128), share)
            rows = pl.ds(pl.multiple_of(at.s * tok, tok), tok)
            da_cols[rows] = da[:, cols]
            yield
            for d in range(1, n_seq):
                swap(d).wait()

        def products():
            ready(4, 7)
            jobs = [(r.grads[0], dg, n2_all, i) for i in range(0, units, step)]
            jobs += [(r.grads[1], du, n2_all, i) for i in range(0, units, step)]
            jobs += [(None, None, None, b) for b in range(line)]
            waiting = [None, None]
            for n, (out, act, rows_in, i) in enumerate(jobs):
                if waiting[n % 2] is not None:
                    waiting[n % 2].wait()
                if out is None:
                    rows = slice(2 * tok * i, 2 * tok * (i + 1))
                    r.stage[n % 2] = dot(hid[rows], down_w[...], NN).astype(BF16)
                    src = r.stage.at[n % 2].reshape(2, tok, model)
                    dst = r.out_part.at[pl.ds(2 * i, 2)]
                else:
                    r.stage[n % 2, :step] = to_grad(act, rows_in, i)
                    src, dst = r.stage.at[n % 2, pl.ds(0, step)], out.at[pl.ds(i, step)]
                waiting[n % 2] = pltpu.make_async_copy(src, dst, r.stage_s.at[n % 2])
                waiting[n % 2].start()
                yield
            for one in waiting:
                one.wait()

        def fill(low, rows):
            part = hid[:, low : low + rows]
            rows_in = grad_all[...].reshape(tokens, model)
            r.reduce[0][low : low + rows] = dot(part, rows_in, TN).astype(BF16)

        down = reduce.steps(at, [None, r.grad_down] + r.reduce, fill)
        interleave(MIDDLE_ORDER, {0: chain(), 1: down, 2: products()})

    return rooms.run(body, "middle", 4, n_seq, n_fsdp)


BACK_ONE_ORDER = [2, 0, 3, 0, 1, 2, 2, 3, 2, 2, 1, 0, 2, 2, 0, 2, 3, 0, 1, 0, 0, 2, 2, 3, 0, 0, 2, 1, 0, 0]
BACK_ONE_ORDER += [2, 2, 0, 0, 3, 0, 2]


def back_one(n_seq, n_fsdp, da_cols, w_qkv, w_o, o_all, n1, saved, out_part, h1, grad):
    q, k, v, lse, cos, sin, pos_col, pos_row, doc_col, doc_row = saved
    (length, share), model = q.shape, w_qkv.shape[0]
    tok = length // n_seq
    rooms = Rooms()
    rooms.bring(h1=h1, q=q, k=k, v=v, lse=lse, cos=cos, sin=sin)
    rooms.take(
        VMEM, da_cols=da_cols, pos_col=pos_col, pos_row=pos_row, doc_col=doc_col, doc_row=doc_row
    )
    rooms.take(ANY, w_qkv=w_qkv, w_o=w_o, o_all=o_all, n1=n1, out_part=out_part, g_in=grad)
    rooms.give(ANY, g_out=like(grad.shape), dw_qkv=like((model, 3 * share)))
    rooms.give(
        VMEM,
        dn1_part=like((n_seq, tok, model)),
        dw_o=like((model // n_fsdp, share)),
        block_out=like((tok, model)),
    )
    o_block = like((n_fsdp, model // n_fsdp, share))
    line_o = ScatterLine(o_block, n_fsdp)
    halve = HalveSeq((n_seq, length, share), BF16, n_seq)
    line_out = ScatterLine(out_part, n_fsdp, 2, far=True)
    reduce = ReduceSeq(grad.shape, grad.dtype, n_seq)
    rooms.keep(
        line_o=line_o.scratch,
        line_out=line_out.scratch,
        mlp_out=room(tok, model, dtype=F32),
        reduce=reduce.scratch,
        dw_o_part=room(*o_block.shape),
        w_qkv_here=room(*w_qkv.shape),
        w_o_here=room(*w_o.shape),
        o_here=room(*o_all.shape),
        do_part=room(n_seq, length, share),
        halve=halve.scratch,
        do=room(length, share),
        dqkv=room(length, 3 * share),
        dk=room(length, 128, dtype=F32),
        dv=room(length, 128, dtype=F32),
        dw_stage=room(2, share, 3 * share),
        load=DMA((4,)),
        stage=DMA((2,)),
    )

    def body(at, r):
        begun = []

        def chain():
            loads = [
                pltpu.make_async_copy(a, b, r.load.at[i])
                for i, (a, b) in enumerate(
                    ((r.w_qkv, r.w_qkv_here), (r.w_o, r.w_o_here), (r.o_all, r.o_here), (r.n1, r.o_here))
                )
            ]
            for i in (1, 2, 0):
                loads[i].start()
            loads[1].wait()
            da_cols = r.da_cols
            w_qkv_here, w_o_here, o_here = r.w_qkv_here, r.w_o_here, r.o_here
            do_part = r.do_part
            for d in reversed(range(n_seq)):
                rows = pl.ds(pl.multiple_of(at.peer(d)[0] * share, share), share)
                do_part[d] = dot(da_cols[...], w_o_here[rows], NT).astype(BF16)
            exchange = halve.steps(at, do_part, r.do, r.halve)
            next(exchange)
            yield
            loads[2].wait()
            dw_o = r.dw_o_part
            per = n_fsdp // n_seq
            for j in range(n_seq):
                field = dot(o_here[j], da_cols[...], TN).astype(BF16)
                dw_o[j * per : (j + 1) * per] = field.reshape((per,) + dw_o.shape[1:])
            loads[3].start()
            running[1] = line_o.steps(at, [dw_o, r.dw_o] + r.line_o)
            yield
            r.arrive()
            begun.append(True)
            for _ in exchange:
                yield
            do = r.do
            dqkv = r.dqkv
            masking = [r.pos_col, r.pos_row, r.doc_col, r.doc_row]
            for pair in range(share // 128):
                back_pair(
                    pair, do, r.q, r.k, r.v, r.lse, r.cos, r.sin,
                    dqkv, masking, r.dk, r.dv,
                )
                yield
            loads[3].wait()
            dw_qkv, stage, stage_s = r.dw_qkv, r.dw_stage, r.stage

            def put(j):
                return pltpu.make_async_copy(
                    stage.at[j % 2], dw_qkv.at[pl.ds(j * share, share)], stage_s.at[j % 2]
                )

            for j in range(n_seq):
                if j >= 2:
                    put(j - 2).wait()
                stage[j % 2] = dot(o_here[j], dqkv[...], TN).astype(BF16)
                put(j).start()
                yield
            loads[0].wait()
            dn1_part = r.dn1_part
            for j in range(n_seq):
                rows = slice(j * share, (j + 1) * share)
                field = dot(dqkv[...], w_qkv_here[rows], NT).astype(BF16)
                for i in range(n_seq):
                    dn1_part[jnp.bitwise_xor(at.s, i), :, rows] = field[i * tok : (i + 1) * tok]
                yield
            put(n_seq - 2).wait()
            put(n_seq - 1).wait()

        def rows_out():
            yield from line_out.steps(at, [r.out_part, r.mlp_out] + r.line_out)
            while not begun:
                yield
            h1, mlp_out, block_out = r.h1, r.mlp_out, r.block_out

            def add(i, carry):
                rows = pl.ds(i * 16, 16)
                block_out[rows] = (h1[rows] + mlp_out[rows]).astype(BF16)
                return carry

            lax.fori_loop(0, tok // 16, add, 0)

        running = {
            0: chain(),
            3: rows_out(),
            2: reduce.steps(at, [r.g_in, r.g_out] + r.reduce),
        }
        interleave(BACK_ONE_ORDER, running)

    return rooms.run(body, "back_one", 2, n_seq, n_fsdp)


BACK_TWO_ORDER = [0, 2, 3, 1, 0, 2, 1, 1, 3, 2, 1, 1, 0, 2, 2, 2, 1, 1, 2, 1, 1, 2, 0, 0, 0, 1, 1, 2, 2, 1]
BACK_TWO_ORDER += [1, 0, 1, 1, 3, 0]


def back_two(
    n_seq, n_fsdp, dn1_part, dw_qkv, dw_o, source, dh1, gain_a, gain_m_term, grad
):
    tok, model = source.shape
    rooms = Rooms()
    line = ScatterLine(dw_qkv, n_fsdp, 2, far=True)
    gain_block = like((n_fsdp, 8, model // n_fsdp), F32)
    line_gain = ScatterLine(gain_block, n_fsdp)
    scatter = HalveSeq(dn1_part.shape, BF16, n_seq)
    reduce = ReduceSeq(grad.shape, grad.dtype, n_seq)
    spread, spread_o = SpreadSeq(n_seq), SpreadSeq(n_seq)
    gather = GatherSeq(n_seq)
    rooms.take(
        VMEM, dn1_part=dn1_part, gain_a=gain_a, gain_m_term=gain_m_term,
    )
    rooms.bring(source=source, dh1=dh1)
    rooms.take(ANY, dw_qkv=dw_qkv, dw_o=dw_o, g_in=grad)
    rooms.give(
        ANY,
        g_out=like(grad.shape),
        dw_qkv_all=like((n_seq,) + dw_qkv.shape[1:]),
        dw_o_all=like((n_seq,) + dw_o.shape),
    )
    rooms.give(
        VMEM,
        grad_in=like((tok, model)),
        gains=like(gain_block.shape[1:], F32),
    )
    rooms.keep(
        line=line.scratch,
        line_gain=line_gain.scratch,
        scatter=scatter.scratch,
        reduce=reduce.scratch,
        spread=spread.scratch,
        spread_o=spread_o.scratch,
        gather=gather.scratch,
        dw_own=room(*dw_qkv.shape[1:]),
        dn1=room(tok, model, dtype=F32),
        gain_part=room(*gain_block.shape, dtype=F32),
        gain_own=room(*gain_block.shape[1:], dtype=F32),
        gain_all=room(n_seq, *gain_block.shape[1:], dtype=F32),
        gain_sum=room(8, model, dtype=F32),
    )

    def body(at, r):
        def weights():
            yield from line.steps(at, [r.dw_qkv, r.dw_own] + r.line)
            yield from spread.steps(at, [r.dw_own, r.dw_qkv_all] + r.spread)

        def rows_in():
            yield from scatter.steps(at, r.dn1_part, r.dn1, r.scatter)
            r.arrive()
            source, dh1, dn1 = r.source, r.dh1, r.dn1
            gain_a, grad_in, gain_sum = r.gain_a, r.grad_in, r.gain_sum
            gain_sum[...] = jnp.zeros_like(gain_sum)

            def norm(i, carry):
                rows = pl.ds(i * 16, 16)
                x, grad = source[rows].astype(F32), dn1[rows]
                scale = lax.rsqrt(jnp.mean(x * x, axis=-1, keepdims=True) + NORM_EPS)
                wide = dh1[rows] + norm_back(grad, x, scale, gain_a[...])
                grad_in[rows] = wide.astype(BF16)
                term = grad * x * scale
                gain_sum[...] += term[:8] + term[8:]
                return carry

            lax.fori_loop(0, tok // 16, norm, 0)
            first = jnp.sum(gain_sum[...], axis=0, keepdims=True)
            second = jnp.sum(r.gain_m_term[...], axis=0, keepdims=True)
            row = lax.broadcasted_iota(jnp.int32, gain_sum.shape, 0)
            both = jnp.where(row == 0, first, jnp.where(row == 1, second, 0.0))
            part, width = r.gain_part, model // n_fsdp
            for f in range(n_fsdp):
                part[f] = both[:, f * width : (f + 1) * width]
            yield
            yield from line_gain.steps(at, [part, r.gain_own] + r.line_gain)
            yield from gather.steps(at, [r.gain_own, r.gain_all] + r.gather)
            total = r.gain_all[0]
            for j in range(1, n_seq):
                total = total + r.gain_all[j]
            r.gains[...] = total

        running = {
            0: weights(),
            1: reduce.steps(at, [r.g_in, r.g_out] + r.reduce),
            2: rows_in(),
            3: spread_o.steps(at, [r.dw_o, r.dw_o_all] + r.spread_o),
        }
        interleave(BACK_TWO_ORDER, running)

    return rooms.run(body, "back_two", 3, n_seq, n_fsdp)


def finish_kernel(gate, up, down, qkv, o, rows_out, rows_in, gains, mlp, attn, out, back, gain):
    for c, ref in enumerate((gate, up, down)):
        mlp[c] = ref[...].astype(F32)
    n_seq, rows, share = o.shape
    for s in range(n_seq):
        at = pl.ds(s * share, share)
        for c in range(3):
            attn[:, c, at] = qkv[s, :, c * share : (c + 1) * share].astype(F32)
        attn[:, 3, at] = o[s].astype(F32)
    out[...] = rows_out[...]
    back[...] = rows_in[...]
    gain[...] = gains[...]


def grid_call(kernel, name, grid, args, in_specs, outs, out_specs, scratch=(), aliases=None):
    return pl.pallas_call(
        kernel,
        grid=grid,
        out_shape=outs,
        in_specs=in_specs,
        out_specs=out_specs,
        scratch_shapes=list(scratch),
        input_output_aliases=aliases or {},
        compiler_params=pltpu.CompilerParams(vmem_limit_bytes=62 * 2**20),
        name=name,
    )(*args)


def on_device(
    n_seq, n_fsdp,
    hidden_in, gain_attn, attn_weights, gain_mlp, mlp_weights, out_grad, block_slots, doc_ids,
):
    tok, model = hidden_in.shape[1:]
    share = model // n_seq
    start = lax.axis_index("seq") * share
    w_own = lax.dynamic_slice_in_dim(attn_weights, start, share, 2).reshape(-1, 4 * share)
    mlp_w = mlp_weights.transpose(1, 0, 2)
    a = front(
        n_seq, n_fsdp, w_own, hidden_in[0], jnp.stack([gain_attn, gain_mlp]).astype(F32), out_grad[0],
        mlp_w,
        block_slots.T, doc_ids,
    )
    tables = (a.cos, a.sin, a.pos_col, a.pos_row, a.doc_col, a.doc_row)
    w_qkv, w_o = a.w_qkv_out.reshape(model, -1), a.w_o_out.reshape(model, -1)
    m = middle(
        n_seq, n_fsdp, a.hid, a.dg, a.du, a.n2_out, a.grad_out, mlp_w, a.middle, out_grad[0], a.gain_m
    )
    b = back_one(
        n_seq, n_fsdp, m.da_cols, w_qkv, w_o, a.o_out, a.n1_out,
        (a.q, a.k, a.v, a.lse, *tables), m.out_part, a.middle, m.grads[0],
    )
    c = back_two(
        n_seq, n_fsdp, b.dn1_part, b.dw_qkv.reshape(n_fsdp, -1, 3 * share), b.dw_o,
        hidden_in[0], m.dh1, a.gain_a, m.gain, m.grads[1],
    )
    own_rows, units = b.dw_o.shape[0], c.g_out.shape[0]
    steps = 8
    u, a_rows, t = units // steps, own_rows // steps, tok // steps
    flat = pl.BlockSpec((u, model), lambda i: (i, 0))
    row = pl.BlockSpec((t, model), lambda i: (i, 0))
    whole = pl.BlockSpec(c.gains.shape, lambda i: (0, 0))
    mlp_grad, attn_grad, block_out, grad_in, gains = grid_call(
        finish_kernel,
        "finish",
        (steps,),
        (b.g_out, c.g_out, m.grad_down, c.dw_qkv_all, c.dw_o_all, b.block_out, c.grad_in, c.gains),
        [flat] * 3
        + [pl.BlockSpec((n_seq, a_rows, n * share), lambda i: (0, i, 0)) for n in (3, 1)]
        + [row, row, whole],
        [
            like((3, units, model), F32),
            like((own_rows, 4, model), F32),
            like((tok, model)),
            like((tok, model)),
            like(c.gains.shape, F32),
        ],
        [
            pl.BlockSpec((3, u, model), lambda i: (0, i, 0)),
            pl.BlockSpec((a_rows, 4, model), lambda i: (i, 0, 0)),
            row,
            row,
            whole,
        ],
    )
    mlp_grad = mlp_grad.transpose(1, 0, 2)
    return (block_out[None], grad_in[None], gains[0], attn_grad, gains[1], mlp_grad)


def solution(mesh):
    return jax.shard_map(
        functools.partial(on_device, mesh.shape["seq"], mesh.shape["fsdp"]),
        mesh=mesh,
        in_specs=(
            P("fsdp", "seq", None),
            P("fsdp"),
            P("fsdp", None, None),
            P("fsdp"),
            P("fsdp", None, None),
            P("fsdp", "seq", None),
            P(),
            P("fsdp", None),
        ),
        out_specs=(
            P("fsdp", "seq", None),
            P("fsdp", "seq", None),
            P("fsdp"),
            P("fsdp", None, None),
            P("fsdp"),
            P("fsdp", None, None),
        ),
        check_vma=False,
    )
```

```python
import functools
import math
import types

import jax
import jax.numpy as jnp
from jax import lax
from jax.experimental import pallas as pl
from jax.experimental.pallas import tpu as pltpu
from jax.sharding import PartitionSpec as P

HEAD = 64


NORM_EPS = 1e-05
ROPE_BASE = 130000.0
MASKED_OUT = -1e30
F32 = jnp.float32
BF16 = jnp.bfloat16
MESH = pl.DeviceIdType.MESH
DMA = pltpu.SemaphoreType.DMA
ANY = pl.BlockSpec(memory_space=pl.ANY)
VMEM = pl.BlockSpec(memory_space=pltpu.VMEM)


def send(src, dst, send_sem, recv_sem, device):
    return pltpu.make_async_remote_copy(
        src_ref=src,
        dst_ref=dst,
        send_sem=send_sem,
        recv_sem=recv_sem,
        device_id=device,
        device_id_type=MESH,
    )


class Place:
    def __init__(self, n_seq, n_fsdp):
        self.n_seq, self.line = n_seq, n_fsdp // 2
        self.s = lax.axis_index("seq")
        self.f = lax.axis_index("fsdp")
        self.r = lax.div(self.f, 2)
        self.c = lax.rem(self.f, 2)
        self.up = (self.s, lax.rem(self.f + 2, n_fsdp))
        self.down = (self.s, lax.rem(self.f + n_fsdp - 2, n_fsdp))
        self.sister = (self.s, 2 * self.r + 1 - self.c)

    def peer(self, d):
        return (jnp.bitwise_xor(self.s, d), self.f)

    def greet(self):
        barrier = pltpu.get_barrier_semaphore()
        wrap = 2 * self.line
        partners = [
            (self.s, lax.rem(self.f + 2, wrap)),
            (self.s, lax.rem(self.f + wrap - 2, wrap)),
            self.sister,
        ]
        partners += [self.peer(d) for d in range(1, self.n_seq)]
        for partner in partners:
            pl.semaphore_signal(barrier, inc=1, device_id=partner, device_id_type=MESH)
        pl.semaphore_wait(barrier, len(partners))


class GatherLine:
    def __init__(self, n_fsdp, parts=1):
        line = n_fsdp // 2
        self.scratch = [DMA((line, parts)) for _ in range(5)] + [DMA((1,))]
        self.parts = parts

    def steps(self, at, x, o, refs, use=None):
        line_r, sis_r, up_s, down_s, sis_s, own_s = refs
        parts, line, r, c = self.parts, at.line, at.r, at.c
        rows = o.shape[1] // parts

        def cut(ref, k):
            return ref.at[pl.ds(k * rows, rows)]

        def go_up(src, b, k):
            return send(src, cut(o.at[2 * b + c], k), up_s.at[b, k], line_r.at[b, k], at.up)

        def go_down(src, b, k):
            return send(src, cut(o.at[2 * b + c], k), down_s.at[b, k], line_r.at[b, k], at.down)

        def go_sister(src, b, k):
            return send(src, cut(o.at[2 * b + c], k), sis_s.at[b, k], sis_r.at[b, k], at.sister)

        def complete(b):
            for k in range(parts):
                src = cut(o.at[2 * b + 1 - c], k)
                send(src, src, sis_s.at[b, k], sis_r.at[b, k], at.sister).wait_recv()
            if use is not None:
                use(b)

        own = pltpu.make_async_copy(x, o.at[at.f], own_s.at[0])
        own.start()
        for k in range(parts):
            src = cut(x, k)
            pl.when(r < line - 1)(lambda: go_up(src, r, k).start())
            pl.when(r > 0)(lambda: go_down(src, r, k).start())
            go_sister(src, r, k).start()
        yield
        for t in range(1, line):
            for k in range(parts):
                low, high = r - t, r + t

                @pl.when(low >= 0)
                def _():
                    src = cut(o.at[2 * low + c], k)
                    go_up(src, low, k).wait_recv()
                    pl.when(r < line - 1)(lambda: go_up(src, low, k).start())
                    go_sister(src, low, k).start()

                @pl.when(high < line)
                def _():
                    src = cut(o.at[2 * high + c], k)
                    go_down(src, high, k).wait_recv()
                    pl.when(r > 0)(lambda: go_down(src, high, k).start())
                    go_sister(src, high, k).start()

            yield
            if t == 1:
                own.wait()
                complete(r)
            else:
                pl.when(r - t + 1 >= 0)(lambda: complete(r - t + 1))
                pl.when(r + t - 1 < line)(lambda: complete(r + t - 1))
        pl.when(r - line + 1 >= 0)(lambda: complete(r - line + 1))
        pl.when(r + line - 1 < line)(lambda: complete(r + line - 1))
        yield
        for b in range(line):
            for k in range(parts):
                src = cut(x, k)
                go_sister(src, b, k).wait_send()
                pl.when((b <= r) & (r < line - 1))(lambda: go_up(src, b, k).wait_send())
                pl.when((b >= r) & (r > 0))(lambda: go_down(src, b, k).wait_send())


class ScatterLine:
    def __init__(self, part, n_fsdp, parts=1, far=False):
        line = n_fsdp // 2
        block = part.shape[1:]
        self.scratch = [
            pltpu.VMEM((line,) + block, part.dtype),
            pltpu.VMEM((line + 1,) + block, part.dtype),
        ]
        self.scratch += [DMA((line, parts)), DMA((line, parts)), DMA((line, parts))]
        self.scratch += [DMA((line + 1, parts))]
        if far:
            self.scratch += [pltpu.VMEM((line,) + block, part.dtype), DMA((line,))]
        self.parts, self.far = parts, far

    def steps(self, at, refs):
        part, o, sis, come, sis_s, sis_r, line_s, line_r = refs[:8]
        near, near_s = refs[8:] if self.far else (None, None)
        parts, line, r, c = self.parts, at.line, at.r, at.c
        rows = part.shape[1] // parts
        tile = 16 if rows % 16 == 0 else rows

        def cut(ref, k):
            return ref.at[pl.ds(k * rows, rows)]

        def to_sister(b, k):
            return send(
                cut(part.at[2 * b + 1 - c], k),
                cut(sis.at[b], k),
                sis_s.at[b, k],
                sis_r.at[b, k],
                at.sister,
            )

        def slot(b, own):
            return jnp.where(b == own, line, b)

        def go_up(b, k):
            return send(cut(sis.at[b], k), cut(come.at[b], k), line_s.at[b, k], line_r.at[b, k], at.up)

        def go_down(b, k, own):
            i = slot(b, own)
            return send(
                cut(sis.at[b], k), cut(come.at[i], k), line_s.at[b, k], line_r.at[i, k], at.down
            )

        def add(b, k, came, out=None):
            def body(i, carry):
                at_rows = pl.ds(k * rows + i * tile, tile)
                own = near[b, at_rows] if self.far else part[2 * b + c, at_rows]
                total = own.astype(F32) + sis[b, at_rows].astype(F32)
                for j in came:
                    total = total + come[j, at_rows].astype(F32)
                if out is None:
                    sis[b, at_rows] = total.astype(sis.dtype)
                else:
                    out[at_rows] = total.astype(out.dtype)
                return carry

            lax.fori_loop(0, rows // tile, body, 0)

        order = []
        for j in range(line):
            order += [b for b in (line - 1 - j, j) if b not in order]
        for b in order:
            for k in range(parts):
                to_sister(b, k).start()
        if self.far:
            loads = [
                pltpu.make_async_copy(part.at[2 * b + c], near.at[b], near_s.at[b])
                for b in range(line)
            ]
            for one in loads:
                one.start()
            for one in loads:
                one.wait()
        yield
        for t in range(line - 1):
            for k in range(parts):
                high, low = line - 1 - t + r, t - (line - 1 - r)

                @pl.when(high < line)
                def _():
                    to_sister(high, k).wait_recv()

                    @pl.when(r > 0)
                    def _():
                        go_up(high, k).wait_recv()
                        add(high, k, [high])

                    pl.when(r == 0)(lambda: add(high, k, []))
                    go_up(high, k).start()

                @pl.when(low >= 0)
                def _():
                    to_sister(low, k).wait_recv()

                    @pl.when(r < line - 1)
                    def _():
                        go_down(low, k, -1).wait_recv()
                        add(low, k, [low])

                    pl.when(r == line - 1)(lambda: add(low, k, []))
                    go_down(low, k, r - 1).start()

            yield
        for k in range(parts):
            to_sister(r, k).wait_recv()
            pl.when(r > 0)(lambda: go_up(r, k).wait_recv())
            pl.when(r < line - 1)(lambda: go_down(r, k, r).wait_recv())
            pl.when(r == 0)(lambda: add(r, k, [line], o))
            pl.when(r == line - 1)(lambda: add(r, k, [r], o))
            pl.when((r > 0) & (r < line - 1))(lambda: add(r, k, [r, line], o))
        yield
        for b in range(line):
            for k in range(parts):
                to_sister(b, k).wait_send()
                pl.when(b != r)(lambda: go_up(b, k).wait_send())


class GatherSeq:
    def __init__(self, n_seq):
        self.scratch = [DMA((n_seq,)), DMA((n_seq,))]

    def steps(self, at, refs):
        x, o, s_sem, r_sem = refs

        def go(d):
            return send(x, o.at[at.s], s_sem.at[d], r_sem.at[d], at.peer(d))

        for d in reversed(range(1, at.n_seq)):
            go(d).start()
        own = pltpu.make_async_copy(x, o.at[at.s], s_sem.at[0])
        own.start()
        yield
        own.wait()
        for d in range(1, at.n_seq):
            go(d).wait()


class HalveSeq:
    def __init__(self, shape, dtype, n_seq):
        n, rows, cols = shape
        bits = n_seq.bit_length() - 1
        self.half = rows // 2
        self.orders = [[(i + p) % bits for i in range(bits)] for p in range(2)]
        self.scratch = [
            pltpu.VMEM((2, n - 1, self.half, cols), dtype), DMA((2, n - 1)), DMA((2, n - 1))
        ]

    def masks(self, p, i):
        out = [0]
        for b in self.orders[p][i + 1 :]:
            out += [m | (1 << b) for m in out]
        return out

    def slot(self, p, i, u):
        return sum(len(self.masks(p, j)) for j in range(i)) + self.masks(p, i).index(u)

    def steps(self, at, part, o, refs):
        land, s_sem, r_sem = refs
        half, bits = self.half, len(self.orders[0])
        tile = 16 if half % 16 == 0 else half

        def go(p, i, u):
            b = 1 << self.orders[p][i]
            if i == 0:
                src = part.at[b | u, pl.ds(p * half, half)]
            else:
                src = land.at[p, self.slot(p, 0, b | u)]
            n = self.slot(p, i, u)
            return send(src, land.at[p, n], s_sem.at[p, n], r_sem.at[p, n], at.peer(b))

        def add(p, u, upto, out, first):
            def body(k, carry):
                rows = pl.ds(pl.multiple_of(k * tile, tile), tile)
                total = part[u, pl.ds(pl.multiple_of(p * half + k * tile, tile), tile)].astype(F32)
                for i in range(upto):
                    total = total + land[p, self.slot(p, i, u), rows].astype(F32)
                out[pl.ds(pl.multiple_of(first + k * tile, tile), tile)] = total.astype(out.dtype)
                return carry

            lax.fori_loop(0, half // tile, body, 0)

        for p in range(2):
            for u in self.masks(p, 0):
                go(p, 0, u).start()
        yield
        for i in range(bits):
            for p in range(2):
                for u in self.masks(p, i):
                    go(p, i, u).wait_recv()
                if i + 1 < bits:
                    b = 1 << self.orders[p][i + 1]
                    for u in self.masks(p, i + 1):
                        add(p, b | u, i + 1, land.at[p, self.slot(p, 0, b | u)], 0)
                        go(p, i + 1, u).start()
                else:
                    add(p, 0, bits, o, p * half)
            yield
        for p in range(2):
            for i in range(bits):
                for u in self.masks(p, i):
                    go(p, i, u).wait_send()


class ReduceSeq:
    def __init__(self, shape, dtype, n_seq, parts=4):
        rows, cols = shape
        self.bits, self.parts = n_seq.bit_length() - 1, parts
        self.rows = rows // parts
        self.room = self.rows - (self.rows >> self.bits)
        self.scratch = [
            pltpu.VMEM(shape, dtype),
            pltpu.VMEM((parts * self.room, cols), dtype),
            DMA((parts,)),
            DMA((parts, self.bits)),
            DMA((parts, self.bits)),
            DMA((parts, n_seq)),
            DMA((parts, n_seq)),
            DMA((parts,)),
        ]

    def steps(self, at, refs, fill=None):
        g_in, o, g, land, load_s, rs_s, rs_r, ag_s, ag_r, own_s = refs
        bits, parts = self.bits, range(self.parts)
        orders = [[(i + p) % bits for i in range(bits)] for p in parts]
        mult = self.rows >> bits

        def bit(t, b):
            return jnp.bitwise_and(lax.shift_right_logical(t, b), 1)

        def base(p, t, n):
            low = p * self.rows
            for i in range(n):
                low = low + bit(t, orders[p][i]) * (self.rows >> (i + 1))
            return pl.multiple_of(low, mult)

        def load(p):
            part = pl.ds(p * self.rows, self.rows)
            return pltpu.make_async_copy(g_in.at[part], g.at[part], load_s.at[p])

        def slot(p, i):
            return p * self.room + sum(self.rows >> (j + 1) for j in range(i))

        def halve(p, i):
            size = self.rows >> (i + 1)
            other = jnp.bitwise_xor(at.s, 1 << orders[p][i])
            return send(
                g.at[pl.ds(base(p, other, i + 1), size)],
                land.at[pl.ds(slot(p, i), size)],
                rs_s.at[p, i],
                rs_r.at[p, i],
                (other, at.f),
            )

        def add(p, i):
            size = self.rows >> (i + 1)
            low, first = base(p, at.s, i + 1), slot(p, i)

            def body(j, carry):
                mine = pl.ds(pl.multiple_of(low + j * 16, 16), 16)
                came = pl.ds(pl.multiple_of(first + j * 16, 16), 16)
                total = g[mine].astype(F32) + land[came].astype(F32)
                g[mine] = total.astype(g.dtype)
                return carry

            lax.fori_loop(0, size // 16, body, 0)

        def masks(p, j):
            out = [0]
            for i in range(j):
                out += [m | (1 << orders[p][bits - 1 - i]) for m in out]
            return out

        def double(p, j, mask):
            b = orders[p][bits - 1 - j]
            piece = pl.ds(base(p, jnp.bitwise_xor(at.s, mask), bits), mult)
            src = g.at[piece] if mask == 0 else o.at[piece]
            i = (1 << b) | mask
            return send(
                src, o.at[piece], ag_s.at[p, i], ag_r.at[p, i], (jnp.bitwise_xor(at.s, 1 << b), at.f)
            )

        def arrive(p, j, mask):
            b = orders[p][bits - 1 - j]
            piece = pl.ds(base(p, jnp.bitwise_xor(at.s, (1 << b) | mask), bits), mult)
            i = (1 << b) | mask
            return send(
                o.at[piece], o.at[piece], ag_s.at[p, i], ag_r.at[p, i],
                (jnp.bitwise_xor(at.s, 1 << b), at.f),
            )

        def own(p):
            piece = pl.ds(base(p, at.s, bits), mult)
            return pltpu.make_async_copy(g.at[piece], o.at[piece], own_s.at[p])

        if g_in is not None:
            for p in parts:
                load(p).start()
        for p in parts:
            if g_in is not None:
                load(p).wait()
            if fill is not None:
                fill(p * self.rows, self.rows)
            halve(p, 0).start()
        yield
        for i in range(bits):
            for p in parts:
                halve(p, i).wait_recv()
                add(p, i)
                if i + 1 < bits:
                    halve(p, i + 1).start()
                else:
                    for j in range(bits):
                        double(p, j, 0).start()
                    own(p).start()
                yield
        for j in range(bits):
            for p in parts:
                for mask in masks(p, j):
                    arrive(p, j, mask).wait_recv()
                    came = (1 << orders[p][bits - 1 - j]) | mask
                    for later in range(j + 1, bits):
                        double(p, later, came).start()
                yield
        for p in parts:
            own(p).wait()
            for i in range(bits):
                halve(p, i).wait_send()
            for j in range(bits):
                for mask in masks(p, j):
                    double(p, j, mask).wait_send()


class SpreadSeq:
    def __init__(self, n_seq):
        self.bits = n_seq.bit_length() - 1
        self.scratch = [DMA((2, n_seq)), DMA((2, n_seq)), DMA((1,))]

    def steps(self, at, refs):
        x, o, s_sem, r_sem, own_s = refs
        bits, half = self.bits, x.shape[0] // 2
        orders = [[(i + p) % bits for i in range(bits)] for p in range(2)]

        def known(p, j):
            out = [0]
            for i in range(j):
                out += [m | (1 << orders[p][i]) for m in out]
            return out

        def piece(p, mask):
            return o.at[jnp.bitwise_xor(at.s, mask), pl.ds(p * half, half)]

        def go(p, j, mask):
            b = 1 << orders[p][j]
            src = x.at[pl.ds(p * half, half)] if mask == 0 else piece(p, mask)
            i = b | mask
            return send(src, piece(p, mask), s_sem.at[p, i], r_sem.at[p, i], at.peer(b))

        def arrive(p, j, mask):
            b = 1 << orders[p][j]
            i = b | mask
            here = piece(p, i)
            return send(here, here, s_sem.at[p, i], r_sem.at[p, i], at.peer(b))

        for p in range(2):
            for j in range(bits):
                go(p, j, 0).start()
        own = pltpu.make_async_copy(x, o.at[at.s], own_s.at[0])
        own.start()
        yield
        for j in range(bits):
            for p in range(2):
                for mask in known(p, j):
                    arrive(p, j, mask).wait_recv()
                    for later in range(j + 1, bits):
                        go(p, later, (1 << orders[p][j]) | mask).start()
            yield
        own.wait()
        for j in range(bits):
            for p in range(2):
                for mask in known(p, j):
                    go(p, j, mask).wait_send()


def interleave(order, running):
    for name in order:
        if name in running and next(running[name], END) is END:
            del running[name]
    while running:
        for name in list(running):
            if next(running[name], END) is END:
                del running[name]


END = object()


class Rooms:
    def __init__(self):
        self.args, self.in_specs, self.outs, self.out_specs, self.scratch = [], [], [], [], []
        self.names = ([], [], [])
        self.brought, self.posted = [], []

    def note(self, group, name, x):
        many = isinstance(x, (list, tuple))
        self.names[group].append((name, len(x) if many else None))
        return list(x) if many else [x]

    def take(self, spec, **arrays):
        for name, x in arrays.items():
            new = self.note(0, name, x)
            self.args += new
            self.in_specs += [spec] * len(new)

    def give(self, spec, **shapes):
        for name, x in shapes.items():
            new = self.note(1, name, x)
            self.outs += new
            self.out_specs += [spec] * len(new)

    def keep(self, **kinds):
        for name, x in kinds.items():
            self.scratch += self.note(2, name, x)

    def bring(self, **arrays):
        names = list(arrays)
        self.take(ANY, **{far(n): x for n, x in arrays.items()})
        self.keep(**{n: pltpu.VMEM(x.shape, x.dtype) for n, x in arrays.items()})
        self.brought = names

    def post(self, **shapes):
        self.give(ANY, **{far(n): x for n, x in shapes.items()})
        self.keep(**{n: pltpu.VMEM(x.shape, x.dtype) for n, x in shapes.items()})
        self.posted = list(shapes)

    def bind(self, refs, groups):
        table, refs = types.SimpleNamespace(), list(refs)
        for group in groups:
            for name, many in self.names[group]:
                count = 1 if many is None else many
                mine, refs = refs[:count], refs[count:]
                setattr(table, name, mine[0] if many is None else mine)
        return table

    def run(self, body, name, collective_id, n_seq, n_fsdp):
        if self.brought:
            self.keep(brought_s=DMA((len(self.brought),)))
        if self.posted:
            self.keep(posted_s=DMA((len(self.posted),)))

        def kernel(*refs):
            at = Place(n_seq, n_fsdp)
            r = self.bind(refs, (0, 1, 2))
            loads = [
                pltpu.make_async_copy(getattr(r, far(n)), getattr(r, n), r.brought_s.at[i])
                for i, n in enumerate(self.brought)
            ]
            stores = [
                pltpu.make_async_copy(getattr(r, n), getattr(r, far(n)), r.posted_s.at[i])
                for i, n in enumerate(self.posted)
            ]
            for one in loads:
                one.start()

            def arrive():
                for one in loads:
                    one.wait()

            def leave(*mine):
                for n, one in zip(self.posted, stores):
                    if any(getattr(r, n) is ref for ref in mine):
                        one.start()

            r.arrive, r.leave = arrive, leave
            at.greet()
            body(at, r)
            for one in stores:
                one.wait()

        out = pl.pallas_call(
            kernel,
            out_shape=self.outs,
            in_specs=self.in_specs,
            out_specs=self.out_specs,
            scratch_shapes=self.scratch,
            compiler_params=pltpu.CompilerParams(
                collective_id=collective_id, has_side_effects=True, vmem_limit_bytes=62 * 2**20
            ),
            name=name,
        )(*self.args)
        results = self.bind(out, (1,))
        for n in self.posted:
            setattr(results, n, getattr(results, far(n)))
        return results


def far(name):
    return name + "_far"


def like(shape, dtype=BF16):
    return jax.ShapeDtypeStruct(tuple(shape), dtype)


def room(*shape, dtype=BF16):
    return pltpu.VMEM(shape, dtype)


def dot(a, b, dims):
    return lax.dot_general(a, b, (dims, ((), ())), preferred_element_type=F32)


NN = ((1,), (0,))
NT = ((1,), (1,))
TN = ((0,), (0,))


def turned(x, cos, sin):
    lane = lax.broadcasted_iota(jnp.int32, x.shape, 1)
    other = jnp.where(lane % HEAD < HEAD // 2, pltpu.roll(x, 96, 1), pltpu.roll(x, 32, 1))
    return x * cos + other * sin


def head_masks():
    lane = lax.broadcasted_iota(jnp.int32, (1, 128), 1)
    first = (lane < HEAD).astype(F32)
    return first, 1.0 - first


def back_pair(pair, do, q, k, v, lse, cos, sin, dqkv, masking, dk, dv):
    pos_col, pos_row, doc_col, doc_row = masking
    length, share = q.shape
    span = 256
    masks = head_masks()
    lane = lax.broadcasted_iota(jnp.int32, (span, 128), 1)
    lanes = slice(pair * 128, pair * 128 + 128)
    dk[...] = jnp.zeros_like(dk)
    dv[...] = jnp.zeros_like(dv)

    def one_span(i, carry):
        rows = pl.ds(pl.multiple_of(i * span, span), span)
        allowed = (pos_row[...] <= pos_col[rows]) & (doc_row[...] == doc_col[rows])
        bias = jnp.where(allowed, 0.0, MASKED_OUT)
        dq = jnp.zeros((span, 128), F32)
        for h in range(2):
            mask = masks[h].astype(BF16)
            field, grad = q[rows, lanes] * mask, do[rows, lanes] * mask
            log_total = jnp.sum(
                jnp.where(lane == 2 * pair + h, lse[rows], 0.0), axis=-1, keepdims=True
            )
            z = dot(field, k[:, lanes], NT) * 0.125 + bias
            prob = jnp.exp(z - log_total)
            dp = dot(grad, v[:, lanes], NT)
            delta = jnp.sum(prob * dp, axis=-1, keepdims=True)
            dz = (prob * (dp - delta)).astype(BF16)
            dq = dq + dot(dz, k[:, lanes], NN) * masks[h]
            dk[...] += dot(dz, field, TN)
            dv[...] += dot(prob.astype(BF16), grad, TN)
        dqkv[rows, lanes] = turned(dq * 0.125, cos[rows], -sin[rows]).astype(BF16)
        return carry

    lax.fori_loop(0, length // span, one_span, 0)
    at = share + pair * 128
    dqkv[:, at : at + 128] = turned(dk[...] * 0.125, cos[...], -sin[...]).astype(BF16)
    at = 2 * share + pair * 128
    dqkv[:, at : at + 128] = dv[...].astype(BF16)


def norm_back(grad_normed, value, scale, gain):
    weighted = grad_normed * gain
    inner_mean = jnp.mean(weighted * value, axis=-1, keepdims=True)
    return scale * (weighted - value * scale * scale * inner_mean)


def scale_of(value):
    return lax.rsqrt(jnp.mean(value * value, axis=-1, keepdims=True) + NORM_EPS)


def fill_tables(slots, docs, r):
    length = docs.shape[1]
    block = length // (2 * slots.shape[1])

    def place(shape, axis):
        i = lax.broadcasted_iota(jnp.int32, shape, axis)
        slot = jnp.zeros(shape, jnp.int32)
        for j in range(2 * slots.shape[1]):
            slot = jnp.where(i // block == j, slots[j % 2, j // 2], slot)
        return slot * block + i % block

    r.pos_col[...] = place((length, 1), 0)
    r.pos_row[...] = place((1, length), 1)
    lane = lax.broadcasted_iota(jnp.int32, (1, 128), 1)
    half = HEAD // 2
    steps = (lane % half).astype(F32) / half
    freqs = jnp.exp(steps * -math.log(ROPE_BASE))
    sign = jnp.where(lane % HEAD < half, -1.0, 1.0)
    r.doc_row[...] = jnp.zeros((1, length), jnp.int32)

    def body(i, carry):
        rows = pl.ds(pl.multiple_of(i * 128, 128), 128)
        pos = r.pos_col[rows]
        turn = pos.astype(F32) * freqs
        r.cos[rows] = jnp.cos(turn)
        r.sin[rows] = jnp.sin(turn) * sign
        at = lax.broadcasted_iota(jnp.int32, (128, length), 1)
        own = jnp.sum(jnp.where(at == pos, docs[...], 0), axis=1, keepdims=True)
        r.doc_col[rows] = own
        here = lax.broadcasted_iota(jnp.int32, (128, length), 0) + i * 128
        r.doc_row[...] += jnp.sum(jnp.where(at == here, own, 0), axis=0, keepdims=True)
        return carry

    lax.fori_loop(0, length // 128, body, 0)


FRONT_ORDER = [0, 0, 0, 1, 0, 0, 1, 0, 1, 0, 1, 0, 1, 1, 2, 0, 0, 2, 0, 0, 0, 0, 2, 0, 2, 0]


def front(n_seq, n_fsdp, w_own, hidden, own_gains, out_grad, mlp_w, slots, docs):
    tok, model = hidden.shape
    length, share = n_seq * tok, w_own.shape[1] // 4
    line, rows_f, units = n_fsdp // 2, w_own.shape[0], mlp_w.shape[1]
    qkv_shape, o_shape = (n_fsdp, rows_f, 3 * share), (n_fsdp, rows_f, share)
    per = n_fsdp // n_seq
    n_pairs = share // 128
    span = 256
    get_w, get_o = GatherLine(n_fsdp, 2), GatherLine(n_fsdp)
    get_gain, get_grad, get_n2 = GatherLine(n_fsdp), GatherLine(n_fsdp, 2), GatherLine(n_fsdp, 2)
    get_x = GatherSeq(n_seq)
    rooms = Rooms()
    rooms.take(VMEM, hidden=hidden, own_gains=own_gains, docs=docs)
    rooms.take(pl.BlockSpec(memory_space=pltpu.SMEM), slots=slots)
    rooms.take(ANY, w_own=w_own, out_grad=out_grad, mlp_w=mlp_w)
    rooms.give(
        ANY,
        w_qkv_out=like(qkv_shape),
        w_o_out=like(o_shape),
        n1_out=like((n_seq, length, share)),
        o_out=like((n_seq, length, share)),
        n2_out=like((n_fsdp, tok, model)),
        grad_out=like((n_fsdp, tok, model)),
        hid=like((n_fsdp * tok, units)),
        dg=like((n_fsdp * tok, units)),
        du=like((n_fsdp * tok, units)),
    )
    rooms.post(
        q=like((length, share)),
        k=like((length, share)),
        v=like((length, share)),
        lse=like((length, 128), F32),
        middle=like((tok, model), F32),
        cos=like((length, 128), F32),
        sin=like((length, 128), F32),
    )
    rooms.give(
        VMEM,
        gain_a=like((1, model), F32),
        gain_m=like((1, model), F32),
        pos_col=like((length, 1), jnp.int32),
        pos_row=like((1, length), jnp.int32),
        doc_col=like((length, 1), jnp.int32),
        doc_row=like((1, length), jnp.int32),
    )
    rooms.keep(
        gains=room(32, rows_f),
        get_w=get_w.scratch, get_o=get_o.scratch, get_gain=get_gain.scratch,
        get_grad=get_grad.scratch, get_n2=get_n2.scratch, get_x=get_x.scratch,
        w_qkv_all=room(*qkv_shape),
        w_o_all=room(*o_shape),
        gains_all=room(n_fsdp, 32, rows_f),
        x_all=room(n_seq, tok, model),
        n1=room(n_fsdp, length, rows_f),
        o_all=room(n_seq, length, share),
        y_total=room(length, share, dtype=F32),
        y=room(n_seq, tok, share),
        y_land=room(n_seq, tok, share),
        n2=room(tok, model),
        n2_all=room(n_fsdp, tok, model),
        grad_all=room(n_fsdp, tok, model),
        w_gate=room(units, model),
        w_up=room(units, model),
        w_down=room(units, model),
        act=room(n_fsdp * tok, units, dtype=F32),
        stage=room(line, 3, 2 * tok, units),
        load=DMA((3,)),
        save=DMA((6 + n_fsdp,)),
        stage_s=DMA((line, 3)),
        o_s=DMA((n_pairs, n_seq)),
        o_r=DMA((n_pairs, n_seq)),
        y_s=DMA((n_seq,)),
        y_r=DMA((n_seq,)),
    )

    def body(at, r):
        loads = [
            pltpu.make_async_copy(r.mlp_w.at[i], w, r.load.at[i])
            for i, w in enumerate((r.w_gate, r.w_up, r.w_down))
        ]
        saves = []
        w_qkv, w_o = r.w_own.at[:, pl.ds(0, 3 * share)], r.w_own.at[:, pl.ds(3 * share, share)]

        def save(src, dst):
            saves.append(pltpu.make_async_copy(src, dst, r.save.at[len(saves)]))
            saves[-1].start()

        def total(c, rows, cols):
            low, left = (c // 2) * length, (c % 2) * share
            return (
                slice(low + rows.start, low + rows.stop), slice(left + cols.start, left + cols.stop)
            )

        def project(b):
            for f in (2 * b, 2 * b + 1):
                for c in range(3):
                    weights = r.w_qkv_all[f, :, c * share : (c + 1) * share]
                    for i in range(0, length, span):
                        part = dot(r.n1[f, i : i + span], weights, NN)
                        r.act[total(c, slice(i, i + span), slice(0, share))] += part

        def grad_of(b):
            rows = pl.ds(pl.multiple_of(2 * tok * b, 2 * tok), 2 * tok)
            grad = r.grad_all[pl.ds(2 * b, 2)].reshape(2 * tok, model)
            r.act[rows] = dot(grad, r.w_down[...], NT)

        def stored(b, k):
            rows = pl.ds(pl.multiple_of(2 * tok * b, 2 * tok), 2 * tok)
            return pltpu.make_async_copy(
                r.stage.at[b, k], (r.hid, r.dg, r.du)[k].at[rows], r.stage_s.at[b, k]
            )

        def activate(b):
            rows = pl.ds(pl.multiple_of(2 * tok * b, 2 * tok), 2 * tok)
            n2 = r.n2_all[pl.ds(2 * b, 2)].reshape(2 * tok, model)
            gate = dot(n2, r.w_gate[...], NT)
            up = dot(n2, r.w_up[...], NT)
            grad = r.act[rows]
            sigma = jax.nn.sigmoid(gate)
            silu = gate * sigma
            r.stage[b, 0] = (silu * up).astype(BF16)
            r.stage[b, 1] = (grad * up * sigma * (1.0 + gate * (1.0 - sigma))).astype(BF16)
            r.stage[b, 2] = (grad * silu).astype(BF16)
            for k in range(3):
                stored(b, k).start()

        def attend(pair):
            lanes = slice(pair * 128, pair * 128 + 128)
            masks = head_masks()
            lane = lax.broadcasted_iota(jnp.int32, (span, 128), 1)

            def one_span(i, carry):
                rows = pl.ds(pl.multiple_of(i * span, span), span)
                allowed = (r.pos_row[...] <= r.pos_col[rows]) & (r.doc_row[...] == r.doc_col[rows])
                bias = jnp.where(allowed, 0.0, MASKED_OUT)
                parts = []
                for h in range(2):
                    field = r.q[rows, lanes] * masks[h].astype(BF16)
                    z = dot(field, r.k[:, lanes], NT) * 0.125 + bias
                    top = jnp.max(z, axis=-1, keepdims=True)
                    e = jnp.exp(z - top)
                    sum_e = jnp.sum(e, axis=-1, keepdims=True)
                    prob = (e * (1.0 / sum_e)).astype(BF16)
                    parts.append(dot(prob, r.v[:, lanes], NN) * masks[h])
                    here = lane == 2 * pair + h
                    r.lse[rows] = jnp.where(here, top + jnp.log(sum_e), r.lse[rows])
                r.o_all[at.s, rows, lanes] = (parts[0] + parts[1]).astype(BF16)
                return carry

            lax.fori_loop(0, length // span, one_span, 0)

        def go_o(pair, d, owner):
            here = r.o_all.at[owner, :, pl.ds(pair * 128, 128)]
            return send(here, here, r.o_s.at[pair, d], r.o_r.at[pair, d], at.peer(d))

        def go_y(d):
            peer = at.peer(d)
            return send(r.y.at[peer[0]], r.y_land.at[d], r.y_s.at[d], r.y_r.at[d], peer)

        def chain():
            weights = get_w.steps(at, w_qkv, r.w_qkv_all, r.get_w, project)
            next(weights)
            rows_in = get_x.steps(at, [r.hidden, r.x_all] + r.get_x)
            next(rows_in)
            for one in loads:
                one.start()
            r.act[...] = jnp.zeros_like(r.act)
            for i in range(2):
                gain = r.own_gains[i : i + 1]
                r.gains[16 * i : 16 * i + 16] = jnp.broadcast_to(gain, (16, rows_f)).astype(BF16)
            gain_steps = get_gain.steps(at, r.gains, r.gains_all, r.get_gain)
            next(gain_steps)
            fill_tables(r.slots, r.docs, r)
            r.leave(r.cos, r.sin)
            for _ in gain_steps:
                pass
            for f in range(n_fsdp):
                cols = slice(f * rows_f, (f + 1) * rows_f)
                r.gain_a[:, cols] = r.gains_all[f, 0:1].astype(F32)
                r.gain_m[:, cols] = r.gains_all[f, 16:17].astype(F32)
            next(weights)
            for _ in rows_in:
                pass
            r.lse[...] = jnp.zeros_like(r.lse)

            def norm(i, carry):
                j, k = i // (tok // 16), i % (tok // 16)
                x = r.x_all[j, pl.ds(pl.multiple_of(k * 16, 16), 16)].astype(F32)
                normed = (x * scale_of(x) * r.gain_a[...]).astype(BF16)
                rows = pl.ds(pl.multiple_of(i * 16, 16), 16)
                for f in range(n_fsdp):
                    r.n1[f, rows] = normed[:, f * rows_f : (f + 1) * rows_f]
                return carry

            lax.fori_loop(0, length // 16, norm, 0)
            for f in range(n_fsdp):
                save(r.n1.at[f], r.n1_out.at[f // per, :, pl.ds((f % per) * rows_f, rows_f)])
            yield
            for _ in weights:
                yield
            save(r.w_qkv_all, r.w_qkv_out)
            for c, out in enumerate((r.q, r.k)):
                for j in range(0, share, 128):
                    field = r.act[total(c, slice(0, length), slice(j, j + 128))]
                    out[:, j : j + 128] = turned(field, r.cos[...], r.sin[...]).astype(BF16)
            r.v[...] = r.act[total(2, slice(0, length), slice(0, share))].astype(BF16)
            r.leave(r.q, r.k, r.v)
            projected.append(True)
            yield
            for pair in range(n_pairs):
                attend(pair)
                for d in reversed(range(1, n_seq)):
                    go_o(pair, d, at.s).start()
                yield
            r.leave(r.lse)
            for _ in out_weights:
                pass
            for d in range(n_seq):
                owner = at.peer(d)[0]
                if d:
                    for pair in range(n_pairs):
                        go_o(pair, d, owner).wait_recv()
                for h in range(per):
                    part = dot(
                        r.o_all[owner, :, h * rows_f : (h + 1) * rows_f],
                        r.w_o_all[owner * per + h],
                        NN,
                    )
                    if d == 0 and h == 0:
                        r.y_total[...] = part
                    else:
                        r.y_total[...] += part
                yield
            for j in range(n_seq):
                r.y[j] = r.y_total[j * tok : (j + 1) * tok].astype(BF16)
            for d in reversed(range(1, n_seq)):
                go_y(d).start()
            save(r.o_all, r.o_out)
            save(r.w_o_all, r.w_o_out)
            r.y_land[0] = r.y[at.s]
            yield
            for d in range(1, n_seq):
                go_y(d).wait()

            def middle(i, carry):
                rows = pl.ds(pl.multiple_of(i * 16, 16), 16)
                for j in range(n_seq):
                    cols = slice(j * share, (j + 1) * share)
                    branch = r.y_land[jnp.bitwise_xor(at.s, j), rows].astype(F32)
                    r.middle[rows, cols] = r.hidden[rows, cols].astype(F32) + branch
                h = r.middle[rows]
                r.n2[rows] = (h * scale_of(h) * r.gain_m[...]).astype(BF16)
                return carry

            lax.fori_loop(0, tok // 16, middle, 0)
            r.leave(r.middle)
            yield
            tokens = get_n2.steps(at, r.n2, r.n2_all, r.get_n2, activate)
            next(tokens)
            yield
            next(tokens)
            for _ in grads:
                pass
            for one in loads[:2]:
                one.wait()
            for _ in tokens:
                yield

        def cotangents():
            blocks = get_grad.steps(at, r.out_grad, r.grad_all, r.get_grad, grad_of)
            next(blocks)
            yield
            next(blocks)
            yield
            while not projected:
                yield
            loads[2].wait()
            for _ in blocks:
                yield
            save(r.grad_all, r.grad_out)

        projected = []
        out_weights = get_o.steps(at, w_o, r.w_o_all, r.get_o)
        grads = cotangents()
        interleave(FRONT_ORDER, {0: chain(), 1: out_weights, 2: grads})
        for pair in range(n_pairs):
            for d in range(1, n_seq):
                go_o(pair, d, at.s).wait_send()
        save(r.n2_all, r.n2_out)
        for b in range(line):
            for k in range(3):
                stored(b, k).wait()
        for one in saves:
            one.wait()

    return rooms.run(body, "front", 1, n_seq, n_fsdp)


MIDDLE_ORDER = [0, 0, 1, 1, 2, 0, 1, 1, 2, 0, 1, 1, 2, 0, 1, 1, 2, 0, 1, 1, 2, 0, 1, 1, 2, 2, 2, 2, 2, 2]
MIDDLE_ORDER += [2]


def middle(n_seq, n_fsdp, hid, dg, du, n2_all, grad_all, mlp_w, h1, out_grad, gain_m):
    tok, model = h1.shape
    tokens, units = hid.shape
    share, length, line = model // n_seq, n_seq * tok, n_fsdp // 2
    step = min(256, units)
    rooms = Rooms()
    rooms.bring(h1=h1, out_grad=out_grad)
    rooms.take(VMEM, gain_m=gain_m)
    rooms.take(ANY, far=[hid, grad_all, dg, du, n2_all], mlp_w=mlp_w)
    rooms.give(
        ANY,
        grad_down=like((units, model)),
        grads=[like((units, model))] * 2,
        out_part=like((n_fsdp, tok, model)),
    )
    rooms.give(
        VMEM, dh1=like((tok, model), F32), gain=like((8, model), F32), da_cols=like((length, share))
    )
    scatter = ScatterLine(like((n_fsdp, tok, model)), n_fsdp, 2)
    reduce = ReduceSeq((units, model), BF16, n_seq)
    rooms.keep(
        scatter=scatter.scratch,
        reduce=reduce.scratch,
        near=[room(*x.shape) for x in (hid, grad_all, dg, du, n2_all)],
        weights=[room(units, model)] * 3,
        dn2_part=room(n_fsdp, tok, model),
        dn2=room(tok, model, dtype=F32),
        da=room(tok, model),
        stage=room(2, 2 * tok, model),
        load=DMA((8,)),
        stage_s=DMA((2,)),
        swap=[DMA((n_seq,)), DMA((n_seq,))],
    )

    def body(at, r):
        hid, grad_all, dg, du, n2_all = r.near
        gate_w, up_w, down_w = r.weights
        loads = [
            pltpu.make_async_copy(a, b, r.load.at[i])
            for i, (a, b) in enumerate(
                list(zip(r.far, r.near)) + [(r.mlp_w.at[i], w) for i, w in enumerate(r.weights)]
            )
        ]

        def ready(*which):
            for i in which:
                loads[i].wait()

        def to_grad(act, rows_in, i):
            return dot(act[:, i : i + step], rows_in[...].reshape(tokens, model), TN).astype(BF16)

        def chain():
            for i in (0, 1, 2, 3, 5, 6, 4, 7):
                loads[i].start()
            ready(0, 1)
            next(down)
            yield
            ready(2, 3, 5, 6)
            for b in range(line):
                rows = slice(2 * tok * b, 2 * tok * (b + 1))
                part = dot(dg[rows], gate_w[...], NN) + dot(du[rows], up_w[...], NN)
                r.dn2_part[2 * b : 2 * b + 2] = part.astype(BF16).reshape(2, tok, model)
            yield from scatter.steps(at, [r.dn2_part, r.dn2] + r.scatter)
            r.arrive()
            h1, out_grad, gain_m = r.h1, r.out_grad, r.gain_m
            dn2, dh1, da, gain = r.dn2, r.dh1, r.da, r.gain
            gain[...] = jnp.zeros_like(gain)

            def norm(i, carry):
                rows = pl.ds(i * 16, 16)
                h, grad = h1[rows], dn2[rows]
                scale = lax.rsqrt(jnp.mean(h * h, axis=-1, keepdims=True) + NORM_EPS)
                wide = out_grad[rows].astype(F32) + norm_back(grad, h, scale, gain_m[...])
                dh1[rows] = wide
                da[rows] = wide.astype(BF16)
                term = grad * h * scale
                gain[...] += term[:8] + term[8:]
                return carry

            lax.fori_loop(0, tok // 16, norm, 0)
            da_cols = r.da_cols
            swap_s, swap_r = r.swap

            def swap(d):
                peer = at.peer(d)
                cols = pl.ds(pl.multiple_of(peer[0] * share, 128), share)
                rows = pl.ds(pl.multiple_of(at.s * tok, tok), tok)
                return send(da.at[:, cols], da_cols.at[rows], swap_s.at[d], swap_r.at[d], peer)

            for d in reversed(range(1, n_seq)):
                swap(d).start()
            cols = pl.ds(pl.multiple_of(at.s * share, 128), share)
            rows = pl.ds(pl.multiple_of(at.s * tok, tok), tok)
            da_cols[rows] = da[:, cols]
            yield
            for d in range(1, n_seq):
                swap(d).wait()

        def products():
            ready(4, 7)
            jobs = [(r.grads[0], dg, n2_all, i) for i in range(0, units, step)]
            jobs += [(r.grads[1], du, n2_all, i) for i in range(0, units, step)]
            jobs += [(None, None, None, b) for b in range(line)]
            waiting = [None, None]
            for n, (out, act, rows_in, i) in enumerate(jobs):
                if waiting[n % 2] is not None:
                    waiting[n % 2].wait()
                if out is None:
                    rows = slice(2 * tok * i, 2 * tok * (i + 1))
                    r.stage[n % 2] = dot(hid[rows], down_w[...], NN).astype(BF16)
                    src = r.stage.at[n % 2].reshape(2, tok, model)
                    dst = r.out_part.at[pl.ds(2 * i, 2)]
                else:
                    r.stage[n % 2, :step] = to_grad(act, rows_in, i)
                    src, dst = r.stage.at[n % 2, pl.ds(0, step)], out.at[pl.ds(i, step)]
                waiting[n % 2] = pltpu.make_async_copy(src, dst, r.stage_s.at[n % 2])
                waiting[n % 2].start()
                yield
            for one in waiting:
                one.wait()

        def fill(low, rows):
            part = hid[:, low : low + rows]
            rows_in = grad_all[...].reshape(tokens, model)
            r.reduce[0][low : low + rows] = dot(part, rows_in, TN).astype(BF16)

        down = reduce.steps(at, [None, r.grad_down] + r.reduce, fill)
        interleave(MIDDLE_ORDER, {0: chain(), 1: down, 2: products()})

    return rooms.run(body, "middle", 4, n_seq, n_fsdp)


BACK_ONE_ORDER = [2, 0, 3, 0, 1, 2, 2, 3, 2, 2, 1, 0, 2, 2, 0, 2, 3, 0, 1, 0, 0, 2, 2, 3, 0, 0, 2, 1, 0, 0]
BACK_ONE_ORDER += [2, 2, 0, 0, 3, 0, 2]


def back_one(n_seq, n_fsdp, da_cols, w_qkv, w_o, o_all, n1, saved, out_part, h1, grad):
    q, k, v, lse, cos, sin, pos_col, pos_row, doc_col, doc_row = saved
    (length, share), model = q.shape, w_qkv.shape[0]
    tok = length // n_seq
    rooms = Rooms()
    rooms.bring(h1=h1, q=q, k=k, v=v, lse=lse, cos=cos, sin=sin)
    rooms.take(
        VMEM, da_cols=da_cols, pos_col=pos_col, pos_row=pos_row, doc_col=doc_col, doc_row=doc_row
    )
    rooms.take(ANY, w_qkv=w_qkv, w_o=w_o, o_all=o_all, n1=n1, out_part=out_part, g_in=grad)
    rooms.give(ANY, g_out=like(grad.shape), dw_qkv=like((model, 3 * share)))
    rooms.give(
        VMEM,
        dn1_part=like((n_seq, tok, model)),
        dw_o=like((model // n_fsdp, share)),
        block_out=like((tok, model)),
    )
    o_block = like((n_fsdp, model // n_fsdp, share))
    line_o = ScatterLine(o_block, n_fsdp)
    halve = HalveSeq((n_seq, length, share), BF16, n_seq)
    line_out = ScatterLine(out_part, n_fsdp, 2, far=True)
    reduce = ReduceSeq(grad.shape, grad.dtype, n_seq)
    rooms.keep(
        line_o=line_o.scratch,
        line_out=line_out.scratch,
        mlp_out=room(tok, model, dtype=F32),
        reduce=reduce.scratch,
        dw_o_part=room(*o_block.shape),
        w_qkv_here=room(*w_qkv.shape),
        w_o_here=room(*w_o.shape),
        o_here=room(*o_all.shape),
        do_part=room(n_seq, length, share),
        halve=halve.scratch,
        do=room(length, share),
        dqkv=room(length, 3 * share),
        dk=room(length, 128, dtype=F32),
        dv=room(length, 128, dtype=F32),
        dw_stage=room(2, share, 3 * share),
        load=DMA((4,)),
        stage=DMA((2,)),
    )

    def body(at, r):
        begun = []

        def chain():
            loads = [
                pltpu.make_async_copy(a, b, r.load.at[i])
                for i, (a, b) in enumerate(
                    ((r.w_qkv, r.w_qkv_here), (r.w_o, r.w_o_here), (r.o_all, r.o_here), (r.n1, r.o_here))
                )
            ]
            for i in (1, 2, 0):
                loads[i].start()
            loads[1].wait()
            da_cols = r.da_cols
            w_qkv_here, w_o_here, o_here = r.w_qkv_here, r.w_o_here, r.o_here
            do_part = r.do_part
            for d in reversed(range(n_seq)):
                rows = pl.ds(pl.multiple_of(at.peer(d)[0] * share, share), share)
                do_part[d] = dot(da_cols[...], w_o_here[rows], NT).astype(BF16)
            exchange = halve.steps(at, do_part, r.do, r.halve)
            next(exchange)
            yield
            loads[2].wait()
            dw_o = r.dw_o_part
            per = n_fsdp // n_seq
            for j in range(n_seq):
                field = dot(o_here[j], da_cols[...], TN).astype(BF16)
                dw_o[j * per : (j + 1) * per] = field.reshape((per,) + dw_o.shape[1:])
            loads[3].start()
            running[1] = line_o.steps(at, [dw_o, r.dw_o] + r.line_o)
            yield
            r.arrive()
            begun.append(True)
            for _ in exchange:
                yield
            do = r.do
            dqkv = r.dqkv
            masking = [r.pos_col, r.pos_row, r.doc_col, r.doc_row]
            for pair in range(share // 128):
                back_pair(
                    pair, do, r.q, r.k, r.v, r.lse, r.cos, r.sin,
                    dqkv, masking, r.dk, r.dv,
                )
                yield
            loads[3].wait()
            dw_qkv, stage, stage_s = r.dw_qkv, r.dw_stage, r.stage

            def put(j):
                return pltpu.make_async_copy(
                    stage.at[j % 2], dw_qkv.at[pl.ds(j * share, share)], stage_s.at[j % 2]
                )

            for j in range(n_seq):
                if j >= 2:
                    put(j - 2).wait()
                stage[j % 2] = dot(o_here[j], dqkv[...], TN).astype(BF16)
                put(j).start()
                yield
            loads[0].wait()
            dn1_part = r.dn1_part
            for j in range(n_seq):
                rows = slice(j * share, (j + 1) * share)
                field = dot(dqkv[...], w_qkv_here[rows], NT).astype(BF16)
                for i in range(n_seq):
                    dn1_part[jnp.bitwise_xor(at.s, i), :, rows] = field[i * tok : (i + 1) * tok]
                yield
            put(n_seq - 2).wait()
            put(n_seq - 1).wait()

        def rows_out():
            yield from line_out.steps(at, [r.out_part, r.mlp_out] + r.line_out)
            while not begun:
                yield
            h1, mlp_out, block_out = r.h1, r.mlp_out, r.block_out

            def add(i, carry):
                rows = pl.ds(i * 16, 16)
                block_out[rows] = (h1[rows] + mlp_out[rows]).astype(BF16)
                return carry

            lax.fori_loop(0, tok // 16, add, 0)

        running = {
            0: chain(),
            3: rows_out(),
            2: reduce.steps(at, [r.g_in, r.g_out] + r.reduce),
        }
        interleave(BACK_ONE_ORDER, running)

    return rooms.run(body, "back_one", 2, n_seq, n_fsdp)


BACK_TWO_ORDER = [0, 2, 3, 1, 0, 2, 1, 1, 3, 2, 1, 1, 0, 2, 2, 2, 1, 1, 2, 1, 1, 2, 0, 0, 0, 1, 1, 2, 2, 1]
BACK_TWO_ORDER += [1, 0, 1, 1, 3, 0]


def back_two(
    n_seq, n_fsdp, dn1_part, dw_qkv, dw_o, source, dh1, gain_a, gain_m_term, grad
):
    tok, model = source.shape
    rooms = Rooms()
    line = ScatterLine(dw_qkv, n_fsdp, 2, far=True)
    gain_block = like((n_fsdp, 8, model // n_fsdp), F32)
    line_gain = ScatterLine(gain_block, n_fsdp)
    scatter = HalveSeq(dn1_part.shape, BF16, n_seq)
    reduce = ReduceSeq(grad.shape, grad.dtype, n_seq)
    spread, spread_o = SpreadSeq(n_seq), SpreadSeq(n_seq)
    gather = GatherSeq(n_seq)
    rooms.take(
        VMEM, dn1_part=dn1_part, gain_a=gain_a, gain_m_term=gain_m_term,
    )
    rooms.bring(source=source, dh1=dh1)
    rooms.take(ANY, dw_qkv=dw_qkv, dw_o=dw_o, g_in=grad)
    rooms.give(
        ANY,
        g_out=like(grad.shape),
        dw_qkv_all=like((n_seq,) + dw_qkv.shape[1:]),
        dw_o_all=like((n_seq,) + dw_o.shape),
    )
    rooms.give(
        VMEM,
        grad_in=like((tok, model)),
        gains=like(gain_block.shape[1:], F32),
    )
    rooms.keep(
        line=line.scratch,
        line_gain=line_gain.scratch,
        scatter=scatter.scratch,
        reduce=reduce.scratch,
        spread=spread.scratch,
        spread_o=spread_o.scratch,
        gather=gather.scratch,
        dw_own=room(*dw_qkv.shape[1:]),
        dn1=room(tok, model, dtype=F32),
        gain_part=room(*gain_block.shape, dtype=F32),
        gain_own=room(*gain_block.shape[1:], dtype=F32),
        gain_all=room(n_seq, *gain_block.shape[1:], dtype=F32),
        gain_sum=room(8, model, dtype=F32),
    )

    def body(at, r):
        def weights():
            yield from line.steps(at, [r.dw_qkv, r.dw_own] + r.line)
            yield from spread.steps(at, [r.dw_own, r.dw_qkv_all] + r.spread)

        def rows_in():
            yield from scatter.steps(at, r.dn1_part, r.dn1, r.scatter)
            r.arrive()
            source, dh1, dn1 = r.source, r.dh1, r.dn1
            gain_a, grad_in, gain_sum = r.gain_a, r.grad_in, r.gain_sum
            gain_sum[...] = jnp.zeros_like(gain_sum)

            def norm(i, carry):
                rows = pl.ds(i * 16, 16)
                x, grad = source[rows].astype(F32), dn1[rows]
                scale = lax.rsqrt(jnp.mean(x * x, axis=-1, keepdims=True) + NORM_EPS)
                wide = dh1[rows] + norm_back(grad, x, scale, gain_a[...])
                grad_in[rows] = wide.astype(BF16)
                term = grad * x * scale
                gain_sum[...] += term[:8] + term[8:]
                return carry

            lax.fori_loop(0, tok // 16, norm, 0)
            first = jnp.sum(gain_sum[...], axis=0, keepdims=True)
            second = jnp.sum(r.gain_m_term[...], axis=0, keepdims=True)
            row = lax.broadcasted_iota(jnp.int32, gain_sum.shape, 0)
            both = jnp.where(row == 0, first, jnp.where(row == 1, second, 0.0))
            part, width = r.gain_part, model // n_fsdp
            for f in range(n_fsdp):
                part[f] = both[:, f * width : (f + 1) * width]
            yield
            yield from line_gain.steps(at, [part, r.gain_own] + r.line_gain)
            yield from gather.steps(at, [r.gain_own, r.gain_all] + r.gather)
            total = r.gain_all[0]
            for j in range(1, n_seq):
                total = total + r.gain_all[j]
            r.gains[...] = total

        running = {
            0: weights(),
            1: reduce.steps(at, [r.g_in, r.g_out] + r.reduce),
            2: rows_in(),
            3: spread_o.steps(at, [r.dw_o, r.dw_o_all] + r.spread_o),
        }
        interleave(BACK_TWO_ORDER, running)

    return rooms.run(body, "back_two", 3, n_seq, n_fsdp)


def finish_kernel(gate, up, down, qkv, o, rows_out, rows_in, gains, mlp, attn, out, back, gain):
    for c, ref in enumerate((gate, up, down)):
        mlp[c] = ref[...].astype(F32)
    n_seq, rows, share = o.shape
    for s in range(n_seq):
        at = pl.ds(s * share, share)
        for c in range(3):
            attn[:, c, at] = qkv[s, :, c * share : (c + 1) * share].astype(F32)
        attn[:, 3, at] = o[s].astype(F32)
    out[...] = rows_out[...]
    back[...] = rows_in[...]
    gain[...] = gains[...]


def grid_call(kernel, name, grid, args, in_specs, outs, out_specs, scratch=(), aliases=None):
    return pl.pallas_call(
        kernel,
        grid=grid,
        out_shape=outs,
        in_specs=in_specs,
        out_specs=out_specs,
        scratch_shapes=list(scratch),
        input_output_aliases=aliases or {},
        compiler_params=pltpu.CompilerParams(vmem_limit_bytes=62 * 2**20),
        name=name,
    )(*args)


def on_device(
    n_seq, n_fsdp,
    hidden_in, gain_attn, attn_weights, gain_mlp, mlp_weights, out_grad, block_slots, doc_ids,
):
    tok, model = hidden_in.shape[1:]
    share = model // n_seq
    start = lax.axis_index("seq") * share
    w_own = lax.dynamic_slice_in_dim(attn_weights, start, share, 2).reshape(-1, 4 * share)
    mlp_w = mlp_weights.transpose(1, 0, 2)
    a = front(
        n_seq, n_fsdp, w_own, hidden_in[0], jnp.stack([gain_attn, gain_mlp]).astype(F32), out_grad[0],
        mlp_w,
        block_slots.T, doc_ids,
    )
    tables = (a.cos, a.sin, a.pos_col, a.pos_row, a.doc_col, a.doc_row)
    w_qkv, w_o = a.w_qkv_out.reshape(model, -1), a.w_o_out.reshape(model, -1)
    m = middle(
        n_seq, n_fsdp, a.hid, a.dg, a.du, a.n2_out, a.grad_out, mlp_w, a.middle, out_grad[0], a.gain_m
    )
    b = back_one(
        n_seq, n_fsdp, m.da_cols, w_qkv, w_o, a.o_out, a.n1_out,
        (a.q, a.k, a.v, a.lse, *tables), m.out_part, a.middle, m.grads[0],
    )
    c = back_two(
        n_seq, n_fsdp, b.dn1_part, b.dw_qkv.reshape(n_fsdp, -1, 3 * share), b.dw_o,
        hidden_in[0], m.dh1, a.gain_a, m.gain, m.grads[1],
    )
    own_rows, units = b.dw_o.shape[0], c.g_out.shape[0]
    steps = 8
    u, a_rows, t = units // steps, own_rows // steps, tok // steps
    flat = pl.BlockSpec((u, model), lambda i: (i, 0))
    row = pl.BlockSpec((t, model), lambda i: (i, 0))
    whole = pl.BlockSpec(c.gains.shape, lambda i: (0, 0))
    mlp_grad, attn_grad, block_out, grad_in, gains = grid_call(
        finish_kernel,
        "finish",
        (steps,),
        (b.g_out, c.g_out, m.grad_down, c.dw_qkv_all, c.dw_o_all, b.block_out, c.grad_in, c.gains),
        [flat] * 3
        + [pl.BlockSpec((n_seq, a_rows, n * share), lambda i: (0, i, 0)) for n in (3, 1)]
        + [row, row, whole],
        [
            like((3, units, model), F32),
            like((own_rows, 4, model), F32),
            like((tok, model)),
            like((tok, model)),
            like(c.gains.shape, F32),
        ],
        [
            pl.BlockSpec((3, u, model), lambda i: (0, i, 0)),
            pl.BlockSpec((a_rows, 4, model), lambda i: (i, 0, 0)),
            row,
            row,
            whole,
        ],
    )
    mlp_grad = mlp_grad.transpose(1, 0, 2)
    return (block_out[None], grad_in[None], gains[0], attn_grad, gains[1], mlp_grad)


def solution(mesh):
    return jax.shard_map(
        functools.partial(on_device, mesh.shape["seq"], mesh.shape["fsdp"]),
        mesh=mesh,
        in_specs=(
            P("fsdp", "seq", None),
            P("fsdp"),
            P("fsdp", None, None),
            P("fsdp"),
            P("fsdp", None, None),
            P("fsdp", "seq", None),
            P(),
            P("fsdp", None),
        ),
        out_specs=(
            P("fsdp", "seq", None),
            P("fsdp", "seq", None),
            P("fsdp"),
            P("fsdp", None, None),
            P("fsdp"),
            P("fsdp", None, None),
        ),
        check_vma=False,
    )
```
